32 devices in a mesh: dp: 8 (over z, y), fsdp: 4 (over x, core).
Axes of the slice: x: 2, y: 2, z: 4, core: 2. Of those that a mesh axis runs over, the one named last changes fastest.
Arguments:
- tokens: bfloat16 [32768, 1024], P(('dp', 'fsdp')), may hold values from -6 to 6
- cotangent: bfloat16 [32768, 1024], P(('dp', 'fsdp')), may hold values from -6 to 6
- w_qkv: bfloat16 [1024, 3072], P(('dp', 'fsdp')), may hold values from -0.1875 to 0.1875
- w_out: bfloat16 [1024, 1024], P(('dp', 'fsdp')), may hold values from -1.5 to 1.5
- w_fc: bfloat16 [1024, 4096], P(('dp', 'fsdp')), may hold values from -0.1875 to 0.1875
- w_proj: bfloat16 [4096, 1024], P(('dp', 'fsdp')), may hold values from -0.09375 to 0.09375
- bias_qkv: bfloat16 [3072], replicated, may hold values from -1.75 to 1.75
- bias_out: bfloat16 [1024], replicated, may hold values from -1.75 to 1.75
- bias_fc: bfloat16 [4096], replicated, may hold values from -1.75 to 1.75
- bias_proj: bfloat16 [1024], replicated, may hold values from -1.75 to 1.75
- ln_gain: float32 [2, 1024], replicated, may hold values from 0.1 to 1.9
- ln_shift: float32 [2, 1024], replicated, may hold values from -1.75 to 1.75
- prefix_embed: float32 [10, 1024], replicated, may hold values from -6 to 6
- reparam_in: float32 [1024, 512], replicated, may hold values from -0.1875 to 0.1875
- reparam_in_bias: float32 [512], replicated, may hold values from -3 to 3
- reparam_out: float32 [512, 2048], replicated, may hold values from -0.25 to 0.25
- reparam_out_bias: float32 [2048], replicated, may hold values from -3 to 3
- lengths: int32 [32, 4], P(('dp', 'fsdp')), may hold values from 1 to 1024, as said below
- buckets: int32 [32], P(('dp', 'fsdp')), may hold values from 256 to 1024, as said below
Outputs:
- out: bfloat16 [32768, 1024], P(('dp', 'fsdp'))
- grad_tokens: bfloat16 [32768, 1024], P(('dp', 'fsdp'))
- grad_embed: float32 [10, 1024], replicated
- grad_reparam_in: float32 [1024, 512], replicated
- grad_reparam_in_bias: float32 [512], replicated
- grad_reparam_out: float32 [512, 2048], replicated
- grad_reparam_out_bias: float32 [2048], replicated
The draws below stay inside these ranges and needn't reach their ends.
Inputs may be any that keep to these rules, and one draw needn't show every extreme that they name: A slot whose bucket is 1024 holds one sequence of lengths[s, 0] tokens and columns 1 to 3 are unused; a slot whose bucket is one quarter of 1024 holds four sequences, one in each quarter, of lengths[s, 0] to lengths[s, 3] tokens; no length exceeds its slot's bucket. `buckets`: each bucket is 1024 or one quarter of 1024, and both occur.
All inputs are finite; a program needn't handle non-finite values.
Results may differ from the reference program's by a relative error of at most 0.012.
Values may be sent and summed in bfloat16 or wider, within the bound.
A program may use at most 192 MiB of HBM per device.

```python
import math
import jax
import jax.numpy as jnp
from jax import lax

D = 1024
HEADS = 16
HEAD_DIM = 64
FF = 4096
PREFIX = 10
PREFIX_HIDDEN = 512
LEN = 1024
SEQS = 32
TOKENS = 32768


def pick_buckets(key):
    tosses = jax.random.randint(key, (SEQS,), 0, 100)
    full_slot = jax.random.randint(jax.random.fold_in(key, 11), (), 0, SEQS)
    short_slot = (full_slot + 1 + jax.random.randint(jax.random.fold_in(key, 12), (), 0, SEQS - 1)) % SEQS
    slot_ids = jnp.arange(SEQS, dtype=jnp.int32)
    longer = ((tosses < 44) | (slot_ids == full_slot)) & (slot_ids != short_slot)
    return (jnp.where(longer, LEN, LEN // 4).astype(jnp.int32), full_slot)


def draw_buckets(key, part):
    chosen, full_slot = pick_buckets(key)
    return chosen


def draw_lengths(key, part):
    chosen, full_slot = pick_buckets(key)
    key = jax.random.fold_in(key, 3)
    uniform_bits = jax.random.randint(key, (SEQS, 4), 0, 1 << 20)
    column = jnp.arange(4, dtype=jnp.int32)[None, :]
    capacity = jnp.where(column == 0, chosen[:, None], LEN // 4)
    lengths_drawn = 1 + uniform_bits % capacity
    slot_ids = jnp.arange(SEQS, dtype=jnp.int32)[:, None]
    return jnp.where((slot_ids == full_slot) & (column == 0), LEN, lengths_drawn).astype(jnp.int32)


def block_levels(rng, shape, split, low, high):
    factor_of, own = 1.0, jax.random.fold_in(rng, 6)
    for position, blocks in split:
        heights = jnp.exp(jax.random.uniform(jax.random.fold_in(own, position), (blocks,), jnp.float32, low / len(split), high / len(split)))
        factor_of = factor_of * jnp.repeat(heights, shape[position] // blocks).reshape([-1 if axis == position else 1 for axis in range(len(shape))])
    return factor_of


def normal_values(rng, dims, scale, bound, shards=(), held_as=jnp.bfloat16):
    factor_of = block_levels(rng, dims, shards, -0.22, 0.18) if shards else 1.0
    values = jax.random.normal(rng, dims, jnp.float32) * scale * factor_of
    return jnp.minimum(jnp.maximum(values, -bound), bound).astype(held_as)


def setup_inputs(seed: int = 0) -> dict:
    seeds = jax.random.split(jax.random.key(seed), 20)
    return {
        "tokens": normal_values(seeds[0], (TOKENS, D), 1.0, 6.0, ((0, 32),)),
        "cotangent": normal_values(seeds[1], (TOKENS, D), 1.0, 6.0, ((0, 32),)),
        "w_qkv": normal_values(seeds[2], (D, 3 * D), D ** -0.5, 0.1875, ((0, 32),)),
        "w_out": normal_values(seeds[3], (D, D), (D // 64) ** -0.5, 1.5, ((0, 32),)),
        "w_fc": normal_values(seeds[4], (D, FF), D ** -0.5, 0.1875, ((0, 32),)),
        "w_proj": normal_values(seeds[5], (FF, D), FF ** -0.5, 0.09375, ((0, 32),)),
        "bias_qkv": normal_values(seeds[6], (3 * D,), 0.3, 1.75),
        "bias_out": normal_values(seeds[7], (D,), 0.3, 1.75),
        "bias_fc": normal_values(seeds[8], (FF,), 0.3, 1.75),
        "bias_proj": normal_values(seeds[9], (D,), 0.3, 1.75),
        "ln_gain": jnp.clip(1.0 + 0.18 * jax.random.normal(seeds[10], (2, D), jnp.float32), 0.1, 1.9),
        "ln_shift": normal_values(seeds[11], (2, D), 0.3, 1.75, (), jnp.float32),
        "prefix_embed": normal_values(seeds[12], (PREFIX, D), 1.0, 6.0, (), jnp.float32),
        "reparam_in": normal_values(seeds[13], (D, PREFIX_HIDDEN), D ** -0.5, 0.1875, (), jnp.float32),
        "reparam_in_bias": normal_values(seeds[14], (PREFIX_HIDDEN,), 0.5, 3.0, (), jnp.float32),
        "reparam_out": normal_values(seeds[15], (PREFIX_HIDDEN, 2 * D), PREFIX_HIDDEN ** -0.5, 0.25, (), jnp.float32),
        "reparam_out_bias": normal_values(seeds[16], (2 * D,), 0.5, 3.0, (), jnp.float32),
        "lengths": draw_lengths(jax.random.fold_in(seeds[19], 71), 0),
        "buckets": draw_buckets(jax.random.fold_in(seeds[19], 71), 0),
    }


@jax.custom_vjp
def low(v):
    return lax.optimization_barrier(v.astype(jnp.bfloat16)).astype(jnp.float32)

@jax.custom_vjp
def low_back(v):
    return v

def low_keep(v):
    return (low(v), None)

def low_pass(kept, grad):
    return (grad,)

def back_keep(v):
    return (v, None)

def back_low(kept, grad):
    return (low(grad),)
low.defvjp(low_keep, low_pass)
low_back.defvjp(back_keep, back_low)
SCORE_SCALE = 0.125
MASKED = -1e+30
HIGHEST = lax.Precision.HIGHEST

def precise(left, right):
    return jnp.dot(left, right, precision=HIGHEST, preferred_element_type=jnp.float32)

def normalize(field, gain, shift):
    centre = lax.optimization_barrier(jnp.mean(field, axis=-1, keepdims=True))
    centred = field - centre
    spread = lax.optimization_barrier(jnp.mean(centred * centred, axis=-1, keepdims=True))
    return centred * lax.rsqrt(spread + 1e-05) * gain + shift

def visible(seg_lengths, bucket):
    places = jnp.arange(LEN, dtype=jnp.int32)
    segment = places // bucket
    within = places - segment * bucket
    extent = jnp.zeros_like(places)
    for which in range(4):
        extent = extent + jnp.where(segment == which, seg_lengths[which], 0)
    living = within < extent
    return (segment[:, None] == segment[None, :]) & (places[None, :] <= places[:, None]) & living[None, :]

def slot_attention(member, prefix_keys, prefix_values):
    queries, key_rows, values, seg_lengths, bucket = member
    allowed = visible(seg_lengths, bucket)
    pre_scores = jnp.einsum('qhd,khd->hqk', queries, prefix_keys, precision=HIGHEST)
    tok_scores = jnp.einsum('qhd,khd->hqk', queries, key_rows, precision=HIGHEST)
    scores = low_back(jnp.concatenate([pre_scores, tok_scores], 2) * SCORE_SCALE)
    scores = jnp.concatenate([scores[:, :, :PREFIX], jnp.where(allowed[None], scores[:, :, PREFIX:], MASKED)], 2)
    probs = low(jax.nn.softmax(scores, axis=-1))
    every_value = jnp.concatenate([prefix_values, values], 0)
    return jnp.einsum('hqk,khd->qhd', probs, every_value, precision=HIGHEST)

def block(inputs, seg_lengths, slot_buckets, prefix_keys, prefix_values, frozen):
    w_qkv, w_out, w_fc, w_proj, bias_qkv, bias_out, bias_fc, bias_proj, ln_gain, ln_shift = frozen
    slot_count = slot_buckets.shape[0]
    normed = low(normalize(inputs, ln_gain[0], ln_shift[0]))
    joined = precise(normed, w_qkv) + bias_qkv
    queries = low(low_back(joined[:, :D])).reshape(slot_count, LEN, HEADS, HEAD_DIM)
    key_rows = low(low_back(joined[:, D:2 * D])).reshape(slot_count, LEN, HEADS, HEAD_DIM)
    values = low(low_back(joined[:, 2 * D:])).reshape(slot_count, LEN, HEADS, HEAD_DIM)
    attend = jax.checkpoint(slot_attention)
    mixed = lax.map(lambda member: attend(member, prefix_keys, prefix_values), (queries, key_rows, values, seg_lengths, slot_buckets))
    attended = low(low_back(mixed.reshape(slot_count * LEN, D)))
    middle = inputs + low_back(precise(attended, w_out) + bias_out)
    second = low(normalize(middle, ln_gain[1], ln_shift[1]))
    before = low_back(precise(second, w_fc) + bias_fc)
    activated = low(jax.nn.gelu(before, approximate=True))
    return middle + low_back(precise(activated, w_proj) + bias_proj)

def reference(tokens, cotangent, w_qkv, w_out, w_fc, w_proj, bias_qkv, bias_out, bias_fc, bias_proj, ln_gain, ln_shift, prefix_embed, reparam_in, reparam_in_bias, reparam_out, reparam_out_bias, lengths, buckets):
    frozen = tuple((weight.astype(jnp.float32) for weight in (w_qkv, w_out, w_fc, w_proj, bias_qkv, bias_out, bias_fc, bias_proj, ln_gain, ln_shift)))
    group_size = math.gcd(SEQS, max(1, 4096 // LEN))
    grouped_lengths = lengths.reshape(SEQS // group_size, group_size, 4)
    grouped_buckets = buckets.reshape(SEQS // group_size, group_size)
    run_block = jax.checkpoint(block)

    def forward(inputs, embed, first_map, first_bias, second_map, second_bias):
        hidden = jnp.tanh(precise(embed, first_map) + first_bias)
        prefix_rows = low(precise(hidden, second_map) + second_bias)
        prefix_keys = prefix_rows[:, :D].reshape(PREFIX, HEADS, HEAD_DIM)
        prefix_values = prefix_rows[:, D:].reshape(PREFIX, HEADS, HEAD_DIM)
        pieces = inputs.reshape(SEQS // group_size, group_size * LEN, D)
        outputs = lax.map(lambda member: run_block(member[0], member[1], member[2], prefix_keys, prefix_values, frozen), (pieces, grouped_lengths, grouped_buckets))
        return outputs.reshape(TOKENS, D)
    result, pull_back = jax.vjp(forward, tokens.astype(jnp.float32), prefix_embed, reparam_in, reparam_in_bias, reparam_out, reparam_out_bias)
    gradients = pull_back(cotangent.astype(jnp.float32))
    return (result.astype(jnp.bfloat16), gradients[0].astype(jnp.bfloat16), gradients[1], gradients[2], gradients[3], gradients[4], gradients[5])
```

```python
import math
import functools

import jax, jax.numpy as jnp
from jax import lax
from jax.experimental import pallas as pl
from jax.experimental.pallas import tpu as pltpu
from jax.sharding import PartitionSpec as P

f32, bf16 = jnp.float32, jnp.bfloat16
NT=(((1,),(1,)),((),()))
NN=(((1,),(0,)),((),()))
def dot(a,b,d=NN): return lax.dot_general(a,b,d,preferred_element_type=f32)
NEG=-1e30
LEN=1024; BQ=256; NQ=LEN//BQ

def lanes(rows): return lax.broadcasted_iota(jnp.int32,(rows,128),1)

def query_extra(i, rows, neg=None):
    ln=lanes(rows); b=ln%64
    e=jnp.where((b==0)|((b>=4)&(b<8)&(b!=4+i)),1.0,0.0)
    if neg is not None:
        hi=neg.astype(bf16); r=neg-hi.astype(f32); mid=r.astype(bf16); lo=r-mid.astype(f32)
        e=jnp.where(b==1,hi.astype(f32),e); e=jnp.where(b==2,mid.astype(f32),e); e=jnp.where(b==3,lo,e)
    return e.astype(bf16)

def delta_extra(neg):
    b=lanes(neg.shape[0])%64
    hi=neg.astype(bf16); r=neg-hi.astype(f32); mid=r.astype(bf16); lo=r-mid.astype(f32)
    e=jnp.where(b==1,hi.astype(f32),jnp.where(b==2,mid.astype(f32),jnp.where(b==3,lo,0.0)))
    return e.astype(bf16)

def half(a,h):
    return jnp.where((lanes(a.shape[0])<64)==(h==0),a,jnp.zeros_like(a))

def causal():
    return lax.broadcasted_iota(jnp.int32,(BQ,BQ),1)<=lax.broadcasted_iota(jnp.int32,(BQ,BQ),0)

def fwd_pair(q, k, v, pk, pv, kx, pkx, o_ref, lse_ref, kext, vext, pkext, pvext):
    kxv=kx[...]; pkxv=pkx[...]
    ln=lanes(LEN); lp=lanes(128)
    for h in (0,1):
        kext[h,:,:128]=half(k[...],h); kext[h,:,128:]=half(kxv,h)
        vext[h,:,:128]=half(v[...],h); vext[h,:,128:]=jnp.where((ln<64)==(h==0),1.0,0.0).astype(bf16)
        pkext[h*128:(h+1)*128,:128]=half(pk[...],h); pkext[h*128:(h+1)*128,128:]=half(pkxv,h)
        pvext[h*128:(h+1)*128,:128]=half(pv[...],h); pvext[h*128:(h+1)*128,128:]=jnp.where((lp<64)==(h==0),1.0,0.0).astype(bf16)
    for i in range(NQ):
        rows=pl.ds(i*BQ,BQ); n=(i+1)*BQ
        qe=jnp.concatenate([q[rows,:],query_extra(i,BQ)],axis=1)
        spre=dot(qe,pkext[...],NT)
        acc=None; ms=[]; pp=[]
        for h in (0,1):
            s=dot(qe,kext[h,:n,:],NT)
            sd=jnp.where(causal(),s[:,n-BQ:],NEG)
            sp=spre[:,h*128:(h+1)*128]
            m=jnp.maximum(jnp.max(sd,axis=1,keepdims=True),jnp.max(sp,axis=1,keepdims=True))
            if i: m=jnp.maximum(m,jnp.max(s[:,:n-BQ],axis=1,keepdims=True))
            pd=jnp.exp(sd-m).astype(bf16)
            a=dot(pd,vext[h,n-BQ:n,:])
            if i: a=a+dot(jnp.exp(s[:,:n-BQ]-m).astype(bf16),vext[h,:n-BQ,:])
            pp.append(jnp.exp(sp-m).astype(bf16)); ms.append(m)
            acc=a if acc is None else acc+a
        acc=acc+dot(jnp.concatenate(pp,axis=1),pvext[...])
        l=acc[:,128:]
        o_ref[rows,:]=(acc[:,:128]/l).astype(bf16)
        lse_ref[rows,:]=jnp.where(lanes(BQ)<64,ms[0],ms[1])+jnp.log(l)

def bwd_pair(q,k,v,pk,pv,kx,pkx,o,lse,do,dq_ref,dk_ref,dv_ref,dpk_ref,dpv_ref,kext,vext,pkext,pvext,qt,dot_,dkt,dvt,variant=0):
    kxv=kx[...]; pkxv=pkx[...]
    ln=lanes(LEN)%64; lp=lanes(128)%64
    ones=jnp.where((ln>=1)&(ln<4),1.0,0.0).astype(bf16); pones=ones[:128]
    for h in (0,1):
        kext[h,:,:128]=half(k[...],h); kext[h,:,128:]=half(kxv,h)
        vext[h,:,:128]=half(v[...],h); vext[h,:,128:]=half(ones,h)
        pkext[h*128:(h+1)*128,:128]=half(pk[...],h); pkext[h*128:(h+1)*128,128:]=half(pkxv,h)
        pvext[h*128:(h+1)*128,:128]=half(pv[...],h); pvext[h*128:(h+1)*128,128:]=half(pones,h)
    qt[...]=q[...].T; dot_[...]=do[...].T
    gi=lax.broadcasted_iota(jnp.int32,(128,128),0)//64; gj=lax.broadcasted_iota(jnp.int32,(128,128),1)//64
    group=jnp.where(gi==gj,1.0,0.0).astype(bf16)
    dpk=[None,None]; dpv=[None,None]
    for i in reversed(range(NQ)):
        rows=pl.ds(i*BQ,BQ); n=(i+1)*BQ
        dov=do[rows,:]
        prod=dov.astype(f32)*o[rows,:].astype(f32)
        ph=prod.astype(bf16); plo=(prod-ph.astype(f32)).astype(bf16)
        delta=dot(ph,group)+dot(plo,group)
        qe=jnp.concatenate([q[rows,:],query_extra(i,BQ,-lse[rows,:])],axis=1)
        de=jnp.concatenate([dov,delta_extra(-delta)],axis=1)
        pp=jnp.exp(dot(qe,pkext[...],NT))
        dsp=(pp*dot(de,pvext[...],NT)).astype(bf16)
        ppb=pp.astype(bf16)
        dq=dot(dsp,pkext[:,:128])
        for h in (0,1):
            hr=slice(h*64,(h+1)*64)
            qth=qt[hr,i*BQ:(i+1)*BQ]; dth=dot_[hr,i*BQ:(i+1)*BQ]
            a=dot(qth,dsp[:,h*128:(h+1)*128]); b=dot(dth,ppb[:,h*128:(h+1)*128])
            dpk[h]=a if dpk[h] is None else dpk[h]+a
            dpv[h]=b if dpv[h] is None else dpv[h]+b
            s=dot(qe,kext[h,:n,:],NT)
            g=dot(de,vext[h,:n,:],NT)
            p=jnp.exp(s)
            pd=jnp.where(causal(),p[:,n-BQ:],0.0)
            p=pd if i==0 else jnp.concatenate([p[:,:n-BQ],pd],axis=1)
            ds=(p*g).astype(bf16)
            p=p.astype(bf16)
            dq=dq+dot(ds,kext[h,:n,:128])
            if i==NQ-1:
                dkt[hr,:n]=dot(qth,ds); dvt[hr,:n]=dot(dth,p)
            else:
                dkt[hr,:n]+=dot(qth,ds); dvt[hr,:n]+=dot(dth,p)
        dq_ref[rows,:]=(dq*0.125).astype(bf16)
    dk_ref[...]=dkt[...].T.astype(bf16)
    dv_ref[...]=dvt[...].T.astype(bf16)
    dpk_ref[...]=jnp.concatenate(dpk,axis=0)
    dpv_ref[...]=jnp.concatenate(dpv,axis=0)

def ext_scratch():
    return [pltpu.VMEM((2,LEN,256),bf16),pltpu.VMEM((2,LEN,256),bf16),pltpu.VMEM((256,256),bf16),pltpu.VMEM((256,256),bf16)]

def attend_forward(joined, pk, pv, kx, pkx):
    col=lambda o: pl.BlockSpec((LEN,128),lambda p,o=o:(0,p+o))
    pre=pl.BlockSpec((128,128),lambda p:(0,p))
    full=lambda r: pl.BlockSpec((r,128),lambda p:(0,0))
    return pl.pallas_call(fwd_pair,grid=(8,),in_specs=[col(0),col(8),col(16),pre,pre,full(LEN),full(128)],
      out_specs=[col(0),col(0)],out_shape=[jax.ShapeDtypeStruct((LEN,1024),bf16),jax.ShapeDtypeStruct((LEN,1024),f32)],
      scratch_shapes=ext_scratch(),
      compiler_params=pltpu.CompilerParams(vmem_limit_bytes=48<<20))(joined,joined,joined,pk,pv,kx,pkx)

def attend_backward(joined, pk, pv, kx, pkx, o, lse, do):
    col=lambda o: pl.BlockSpec((LEN,128),lambda p,o=o:(0,p+o))
    pre=pl.BlockSpec((128,128),lambda p:(0,p))
    full=lambda r: pl.BlockSpec((r,128),lambda p:(0,0))
    pout=pl.BlockSpec((128,128),lambda p:(p,0))
    return pl.pallas_call(bwd_pair,grid=(8,),in_specs=[col(0),col(8),col(16),pre,pre,full(LEN),full(128),col(0),col(0),col(0)],
      out_specs=[col(0),col(0),col(0),pout,pout],out_shape=[jax.ShapeDtypeStruct((LEN,1024),bf16)]*3+[jax.ShapeDtypeStruct((1024,128),f32)]*2,
      scratch_shapes=ext_scratch()+[pltpu.VMEM((128,LEN),bf16)]*2+[pltpu.VMEM((128,LEN),f32)]*2,
      compiler_params=pltpu.CompilerParams(vmem_limit_bytes=48<<20))(joined,joined,joined,pk,pv,kx,pkx,o,lse,do)

def key_extra(lengths,bucket):
    place=lax.broadcasted_iota(jnp.int32,(LEN,128),0); b=lax.broadcasted_iota(jnp.int32,(LEN,128),1)%64
    seg=place//bucket; within=place-seg*bucket
    ext=jnp.zeros_like(place)
    for w in range(4): ext=ext+jnp.where(seg==w,lengths[w],0)
    e=jnp.where((b==0)&(within>=ext),NEG,0.0)
    e=jnp.where((b>=1)&(b<4),1.0,e)
    e=jnp.where((b>=4)&(b<8)&(bucket<LEN)&(seg==b-4),NEG,e)
    return e.astype(bf16)
def prefix_extra():
    r=lax.broadcasted_iota(jnp.int32,(128,128),0); b=lax.broadcasted_iota(jnp.int32,(128,128),1)%64
    return jnp.where((b==0)&(r>=10),NEG,jnp.where((b>=1)&(b<4),1.0,0.0)).astype(bf16)

D = 1024
PREFIX = 10
HIGHEST = lax.Precision.HIGHEST


def precise(left, right):
    return jnp.dot(left, right, precision=HIGHEST, preferred_element_type=jnp.float32)


def lowdot(left, right):
    return jnp.dot(left, right, preferred_element_type=jnp.float32)


def dot_rows(left, right):
    return lax.dot_general(
        left, right, (((1,), (1,)), ((), ())), preferred_element_type=jnp.float32
    )


def normalize(field, gain, shift):
    centre = jnp.mean(field, axis=-1, keepdims=True)
    centred = field - centre
    spread = jnp.mean(centred * centred, axis=-1, keepdims=True)
    return centred * lax.rsqrt(spread + 1e-05) * gain + shift


def reparam_backward(grad_prefix, prefix_embed, hidden, reparam_in, reparam_out):
    grad_second = precise(hidden.T, grad_prefix)
    grad_second_bias = jnp.sum(grad_prefix, axis=0)
    grad_pre = precise(grad_prefix, reparam_out.T) * (1.0 - hidden * hidden)
    grad_first = precise(prefix_embed.T, grad_pre)
    grad_first_bias = jnp.sum(grad_pre, axis=0)
    grad_embed = precise(grad_pre, reparam_in.T)
    return (grad_embed, grad_first, grad_first_bias, grad_second, grad_second_bias)


MESH = pl.DeviceIdType.MESH


def gather_kernel(dims, wq, wo, wf, wp, gq, go, gf, gp, zs, zr, as_, ar, bs, br, cs, cr, ls):
    Z, Y, X, C = dims
    A = slice(None)
    dp, fs = lax.axis_index("dp"), lax.axis_index("fsdp")
    z, y, x, c = dp // Y, dp % Y, fs // C, fs % C
    zid = lambda dz: (lax.rem(z + dz, Z) * Y + y, fs)
    yid, xid, cid = (z * Y + (1 - y), fs), (dp, (1 - x) * C + c), (dp, x * C + (1 - c))
    bar = pltpu.get_barrier_semaphore()
    for d in [zid(dz) for dz in range(1, Z)] + [yid, xid, cid]:
        pl.semaphore_signal(bar, inc=1, device_id=d, device_id_type=MESH)
    pl.semaphore_wait(bar, Z + 2)
    ins, outs = [wq, wo, wf, wp], [gq, go, gf, gp]
    n = len(CHUNKS)

    def src(k):
        w, j = CHUNKS[k]
        return wp.at[j] if w == 3 else ins[w].at[:, :, pl.ds(j * 1024, 1024)]

    def dst(k, *ix):
        w, j = CHUNKS[k]
        if w == 3:
            return gp.at[(*ix[:4], *(A,) * (4 - len(ix)), j, *ix[4:])]
        return outs[w].at[(*ix, *(A,) * (6 - len(ix)), pl.ds(j * 1024, 1024))]

    def rc(s, d, ss, rs, dev):
        return pltpu.make_async_remote_copy(
            src_ref=s, dst_ref=d, send_sem=ss, recv_sem=rs, device_id=dev, device_id_type=MESH
        )

    def zc(k, dz):
        return rc(src(k), dst(k, z, y, x, c), zs.at[k, dz - 1], zr.at[k, dz - 1], zid(dz))

    def ac(k, h):
        s = dst(k, A, y, x, c, h)
        return rc(s, s, as_.at[k, h], ar.at[k, h], yid if h == 0 else xid)

    def bc(k, h):
        s = dst(k, A, A, x, c, h) if h == 0 else dst(k, A, y, A, c, h)
        return rc(s, s, bs.at[k, h], br.at[k, h], xid if h == 0 else yid)

    def cc(k):
        s = dst(k, A, A, A, c)
        return rc(s, s, cs.at[k], cr.at[k], cid)

    def lc(k):
        return pltpu.make_async_copy(src(k), dst(k, z, y, x, c), ls.at[k])

    def first(k):
        lc(k).start()
        for dz in range(1, Z):
            zc(k, dz).start()

    def second(k):
        lc(k).wait()
        for dz in range(1, Z):
            zc(k, dz).wait_recv()
        for h in (0, 1):
            ac(k, h).start()

    def third(k):
        for h in (0, 1):
            ac(k, h).wait_recv()
        for h in (0, 1):
            bc(k, h).start()

    def fourth(k):
        for h in (0, 1):
            bc(k, h).wait_recv()
        cc(k).start()

    first(0)
    for t in range(n + 3):
        if t + 1 < n:
            first(t + 1)
        if t < n:
            second(t)
        if 0 <= t - 1 < n:
            third(t - 1)
        if 0 <= t - 2 < n:
            fourth(t - 2)
        if 0 <= t - 3 < n:
            cc(t - 3).wait_recv()
    for k in range(n):
        for dz in range(1, Z):
            zc(k, dz).wait_send()
        for h in (0, 1):
            ac(k, h).wait_send()
            bc(k, h).wait_send()
        cc(k).wait_send()


CHUNKS = [(0, 0), (0, 1), (0, 2), (1, 0)] + [(w, j) for j in range(4) for w in (2, 3)]


def gather_weights(dims, wq, wo, wf, wp):
    if dims is None:
        return tuple(lax.all_gather(t, ("dp", "fsdp"), axis=0, tiled=True) for t in (wq, wo, wf, wp))
    n, Z = len(CHUNKS), dims[0]
    S = pltpu.SemaphoreType.DMA
    anys = pl.BlockSpec(memory_space=pl.ANY)
    o = pl.pallas_call(
        functools.partial(gather_kernel, dims),
        out_shape=[jax.ShapeDtypeStruct((*dims, 2, 16, w.shape[1]), bf16) for w in (wq, wo, wf)]
        + [jax.ShapeDtypeStruct((*dims, 4, 2, 16, wp.shape[1]), bf16)],
        in_specs=[anys] * 4,
        out_specs=[anys] * 4,
        scratch_shapes=[S((n, Z - 1)), S((n, Z - 1))] + [S((n, 2))] * 4 + [S((n,))] * 3,
        compiler_params=pltpu.CompilerParams(collective_id=0, has_side_effects=True),
    )(*(w.reshape(2, 16, w.shape[1]) for w in (wq, wo, wf)), wp.reshape(4, 2, 16, wp.shape[1]))
    return tuple(t.reshape(math.prod(t.shape[:-1]), t.shape[-1]) for t in o)


def prefix_back(blocks):
    return blocks.reshape(8, 2, 64, 128)[..., :PREFIX].transpose(3, 0, 1, 2).reshape(PREFIX, D)


def on_device(
    dims, tokens, cotangent, w_qkv, w_out, w_fc, w_proj, bias_qkv, bias_out, bias_fc, bias_proj,
    ln_gain, ln_shift, prefix_embed, reparam_in, reparam_in_bias, reparam_out, reparam_out_bias,
    lengths, buckets,
):
    full_qkv, full_out, full_fc, full_proj = gather_weights(dims, w_qkv, w_out, w_fc, w_proj)
    hidden = jnp.tanh(precise(prefix_embed, reparam_in) + reparam_in_bias)
    prefix_rows = (precise(hidden, reparam_out) + reparam_out_bias).astype(bf16)
    padded = jnp.pad(prefix_rows, ((0, 128 - PREFIX), (0, 0)))
    pk, pv = padded[:, :D], padded[:, D:]
    kx, pkx = key_extra(lengths[0], buckets[0]), prefix_extra()
    inputs = tokens.astype(jnp.float32)
    normed = normalize(inputs, ln_gain[0], ln_shift[0]).astype(bf16)
    joined = (lowdot(normed, full_qkv) + bias_qkv.astype(jnp.float32)).astype(bf16)
    scale = jnp.where(jnp.arange(3 * D) < D, 0.125, 1.0).astype(bf16)
    joined = joined * scale
    attended, lse = attend_forward(joined, pk, pv, kx, pkx)
    middle = inputs + (lowdot(attended, full_out) + bias_out.astype(jnp.float32))
    second = normalize(middle, ln_gain[1], ln_shift[1]).astype(bf16)
    before = lowdot(second, full_fc) + bias_fc.astype(jnp.float32)
    activated = jax.nn.gelu(before, approximate=True).astype(bf16)
    result = middle + (lowdot(activated, full_proj) + bias_proj.astype(jnp.float32))
    grad_hidden = dot_rows(cotangent, full_proj)
    gelu_pull = jax.vjp(lambda field: jax.nn.gelu(field, approximate=True), before)[1]
    grad_before = gelu_pull(grad_hidden)[0].astype(bf16)
    grad_second = dot_rows(grad_before, full_fc)
    norm_two = jax.vjp(lambda field: normalize(field, ln_gain[1], ln_shift[1]), middle)[1]
    grad_middle = cotangent.astype(jnp.float32) + norm_two(grad_second)[0]
    grad_attended = dot_rows(grad_middle.astype(bf16), full_out).astype(bf16)
    dq, dk, dv, dpk, dpv = attend_backward(joined, pk, pv, kx, pkx, attended, lse, grad_attended)
    grad_prefix = jnp.concatenate([prefix_back(dpk), prefix_back(dpv)], 1)
    grad_prefix = lax.psum(grad_prefix, ("dp", "fsdp"))
    grad_normed = dot_rows(jnp.concatenate([dq, dk, dv], 1), full_qkv)
    norm_one = jax.vjp(lambda field: normalize(field, ln_gain[0], ln_shift[0]), inputs)[1]
    grad_tokens = (grad_middle + norm_one(grad_normed)[0]).astype(bf16)
    return (
        result.astype(bf16),
        grad_tokens,
        *reparam_backward(grad_prefix, prefix_embed, hidden, reparam_in, reparam_out),
    )


def chip_dims(mesh):
    if dict(mesh.shape) == {"dp": 8, "fsdp": 4}:
        return (4, 2, 2, 2)
    return None


def solution(mesh):
    split, lone = P(("dp", "fsdp"), None), P()
    return jax.shard_map(
        functools.partial(on_device, chip_dims(mesh)),
        mesh=mesh,
        in_specs=(split,) * 6 + (lone,) * 11 + (split, P(("dp", "fsdp"))),
        out_specs=(split, split) + (lone,) * 5,
        check_vma=False,
    )
```

```python
import functools
import math

import jax, jax.numpy as jnp
from jax import lax
from jax.experimental import pallas as pl
from jax.experimental.pallas import tpu as pltpu
from jax.sharding import PartitionSpec as P

f32, bf16 = jnp.float32, jnp.bfloat16
NT=(((1,),(1,)),((),()))
NN=(((1,),(0,)),((),()))
def dot(a,b,d=NN): return lax.dot_general(a,b,d,preferred_element_type=f32)
NEG=-1e30
LEN=1024; BQ=256; NQ=LEN//BQ

def lanes(rows): return lax.broadcasted_iota(jnp.int32,(rows,128),1)

def query_extra(i, rows, neg=None):
    ln=lanes(rows); b=ln%64
    e=jnp.where((b==0)|((b>=4)&(b<8)&(b!=4+i)),1.0,0.0)
    if neg is not None:
        hi=neg.astype(bf16); r=neg-hi.astype(f32); mid=r.astype(bf16); lo=r-mid.astype(f32)
        e=jnp.where(b==1,hi.astype(f32),e); e=jnp.where(b==2,mid.astype(f32),e); e=jnp.where(b==3,lo,e)
    return e.astype(bf16)

def delta_extra(neg):
    b=lanes(neg.shape[0])%64
    hi=neg.astype(bf16); r=neg-hi.astype(f32); mid=r.astype(bf16); lo=r-mid.astype(f32)
    e=jnp.where(b==1,hi.astype(f32),jnp.where(b==2,mid.astype(f32),jnp.where(b==3,lo,0.0)))
    return e.astype(bf16)

def half(a,h):
    return jnp.where((lanes(a.shape[0])<64)==(h==0),a,jnp.zeros_like(a))

def causal():
    return lax.broadcasted_iota(jnp.int32,(BQ,BQ),1)<=lax.broadcasted_iota(jnp.int32,(BQ,BQ),0)

def fwd_pair(q, k, v, pk, pv, kx, pkx, o_ref, lse_ref, kext, vext, pkext, pvext):
    kxv=kx[...]; pkxv=pkx[...]
    ln=lanes(LEN); lp=lanes(128)
    for h in (0,1):
        kext[h,:,:128]=half(k[...],h); kext[h,:,128:]=half(kxv,h)
        vext[h,:,:128]=half(v[...],h); vext[h,:,128:]=jnp.where((ln<64)==(h==0),1.0,0.0).astype(bf16)
        pkext[h*128:(h+1)*128,:128]=half(pk[...],h); pkext[h*128:(h+1)*128,128:]=half(pkxv,h)
        pvext[h*128:(h+1)*128,:128]=half(pv[...],h); pvext[h*128:(h+1)*128,128:]=jnp.where((lp<64)==(h==0),1.0,0.0).astype(bf16)
    for i in range(NQ):
        rows=pl.ds(i*BQ,BQ); n=(i+1)*BQ
        qe=jnp.concatenate([q[rows,:],query_extra(i,BQ)],axis=1)
        spre=dot(qe,pkext[...],NT)
        acc=None; ms=[]; pp=[]
        for h in (0,1):
            s=dot(qe,kext[h,:n,:],NT)
            sd=jnp.where(causal(),s[:,n-BQ:],NEG)
            sp=spre[:,h*128:(h+1)*128]
            m=jnp.maximum(jnp.max(sd,axis=1,keepdims=True),jnp.max(sp,axis=1,keepdims=True))
            if i: m=jnp.maximum(m,jnp.max(s[:,:n-BQ],axis=1,keepdims=True))
            pd=jnp.exp(sd-m).astype(bf16)
            a=dot(pd,vext[h,n-BQ:n,:])
            if i: a=a+dot(jnp.exp(s[:,:n-BQ]-m).astype(bf16),vext[h,:n-BQ,:])
            pp.append(jnp.exp(sp-m).astype(bf16)); ms.append(m)
            acc=a if acc is None else acc+a
        acc=acc+dot(jnp.concatenate(pp,axis=1),pvext[...])
        l=acc[:,128:]
        o_ref[rows,:]=(acc[:,:128]/l).astype(bf16)
        lse_ref[rows,:]=jnp.where(lanes(BQ)<64,ms[0],ms[1])+jnp.log(l)

def bwd_pair(q,k,v,pk,pv,kx,pkx,o,lse,do,dq_ref,dk_ref,dv_ref,dpk_ref,dpv_ref,kext,vext,pkext,pvext,qt,dot_,dkt,dvt,variant=0):
    kxv=kx[...]; pkxv=pkx[...]
    ln=lanes(LEN)%64; lp=lanes(128)%64
    ones=jnp.where((ln>=1)&(ln<4),1.0,0.0).astype(bf16); pones=ones[:128]
    for h in (0,1):
        kext[h,:,:128]=half(k[...],h); kext[h,:,128:]=half(kxv,h)
        vext[h,:,:128]=half(v[...],h); vext[h,:,128:]=half(ones,h)
        pkext[h*128:(h+1)*128,:128]=half(pk[...],h); pkext[h*128:(h+1)*128,128:]=half(pkxv,h)
        pvext[h*128:(h+1)*128,:128]=half(pv[...],h); pvext[h*128:(h+1)*128,128:]=half(pones,h)
    qt[...]=q[...].T; dot_[...]=do[...].T
    gi=lax.broadcasted_iota(jnp.int32,(128,128),0)//64; gj=lax.broadcasted_iota(jnp.int32,(128,128),1)//64
    group=jnp.where(gi==gj,1.0,0.0).astype(bf16)
    dpk=[None,None]; dpv=[None,None]
    for i in reversed(range(NQ)):
        rows=pl.ds(i*BQ,BQ); n=(i+1)*BQ
        dov=do[rows,:]
        prod=dov.astype(f32)*o[rows,:].astype(f32)
        ph=prod.astype(bf16); plo=(prod-ph.astype(f32)).astype(bf16)
        delta=dot(ph,group)+dot(plo,group)
        qe=jnp.concatenate([q[rows,:],query_extra(i,BQ,-lse[rows,:])],axis=1)
        de=jnp.concatenate([dov,delta_extra(-delta)],axis=1)
        pp=jnp.exp(dot(qe,pkext[...],NT))
        dsp=(pp*dot(de,pvext[...],NT)).astype(bf16)
        ppb=pp.astype(bf16)
        dq=dot(dsp,pkext[:,:128])
        for h in (0,1):
            hr=slice(h*64,(h+1)*64)
            qth=qt[hr,i*BQ:(i+1)*BQ]; dth=dot_[hr,i*BQ:(i+1)*BQ]
            a=dot(qth,dsp[:,h*128:(h+1)*128]); b=dot(dth,ppb[:,h*128:(h+1)*128])
            dpk[h]=a if dpk[h] is None else dpk[h]+a
            dpv[h]=b if dpv[h] is None else dpv[h]+b
            s=dot(qe,kext[h,:n,:],NT)
            g=dot(de,vext[h,:n,:],NT)
            p=jnp.exp(s)
            pd=jnp.where(causal(),p[:,n-BQ:],0.0)
            p=pd if i==0 else jnp.concatenate([p[:,:n-BQ],pd],axis=1)
            ds=(p*g).astype(bf16)
            p=p.astype(bf16)
            dq=dq+dot(ds,kext[h,:n,:128])
            if i==NQ-1:
                dkt[hr,:n]=dot(qth,ds); dvt[hr,:n]=dot(dth,p)
            else:
                dkt[hr,:n]+=dot(qth,ds); dvt[hr,:n]+=dot(dth,p)
        dq_ref[rows,:]=(dq*0.125).astype(bf16)
    dk_ref[...]=dkt[...].T.astype(bf16)
    dv_ref[...]=dvt[...].T.astype(bf16)
    dpk_ref[...]=jnp.concatenate(dpk,axis=0)
    dpv_ref[...]=jnp.concatenate(dpv,axis=0)

def ext_scratch():
    return [pltpu.VMEM((2,LEN,256),bf16),pltpu.VMEM((2,LEN,256),bf16),pltpu.VMEM((256,256),bf16),pltpu.VMEM((256,256),bf16)]

def attend_forward(joined, pk, pv, kx, pkx):
    col=lambda o: pl.BlockSpec((LEN,128),lambda p,o=o:(0,p+o))
    pre=pl.BlockSpec((128,128),lambda p:(0,p))
    full=lambda r: pl.BlockSpec((r,128),lambda p:(0,0))
    return pl.pallas_call(fwd_pair,grid=(8,),in_specs=[col(0),col(8),col(16),pre,pre,full(LEN),full(128)],
      out_specs=[col(0),col(0)],out_shape=[jax.ShapeDtypeStruct((LEN,1024),bf16),jax.ShapeDtypeStruct((LEN,1024),f32)],
      scratch_shapes=ext_scratch(),
      compiler_params=pltpu.CompilerParams(vmem_limit_bytes=48<<20))(joined,joined,joined,pk,pv,kx,pkx)

def attend_backward(joined, pk, pv, kx, pkx, o, lse, do):
    col=lambda o: pl.BlockSpec((LEN,128),lambda p,o=o:(0,p+o))
    pre=pl.BlockSpec((128,128),lambda p:(0,p))
    full=lambda r: pl.BlockSpec((r,128),lambda p:(0,0))
    pout=pl.BlockSpec((128,128),lambda p:(p,0))
    return pl.pallas_call(bwd_pair,grid=(8,),in_specs=[col(0),col(8),col(16),pre,pre,full(LEN),full(128),col(0),col(0),col(0)],
      out_specs=[col(0),col(0),col(0),pout,pout],out_shape=[jax.ShapeDtypeStruct((LEN,1024),bf16)]*3+[jax.ShapeDtypeStruct((1024,128),f32)]*2,
      scratch_shapes=ext_scratch()+[pltpu.VMEM((128,LEN),bf16)]*2+[pltpu.VMEM((128,LEN),f32)]*2,
      compiler_params=pltpu.CompilerParams(vmem_limit_bytes=48<<20))(joined,joined,joined,pk,pv,kx,pkx,o,lse,do)

def key_extra(lengths,bucket):
    place=lax.broadcasted_iota(jnp.int32,(LEN,128),0); b=lax.broadcasted_iota(jnp.int32,(LEN,128),1)%64
    seg=place//bucket; within=place-seg*bucket
    ext=jnp.zeros_like(place)
    for w in range(4): ext=ext+jnp.where(seg==w,lengths[w],0)
    e=jnp.where((b==0)&(within>=ext),NEG,0.0)
    e=jnp.where((b>=1)&(b<4),1.0,e)
    e=jnp.where((b>=4)&(b<8)&(bucket<LEN)&(seg==b-4),NEG,e)
    return e.astype(bf16)
def prefix_extra():
    r=lax.broadcasted_iota(jnp.int32,(128,128),0); b=lax.broadcasted_iota(jnp.int32,(128,128),1)%64
    return jnp.where((b==0)&(r>=10),NEG,jnp.where((b>=1)&(b<4),1.0,0.0)).astype(bf16)

D = 1024
PREFIX = 10
HIGHEST = lax.Precision.HIGHEST


def precise(left, right):
    return jnp.dot(left, right, precision=HIGHEST, preferred_element_type=jnp.float32)


def lowdot(left, right):
    return jnp.dot(left, right, preferred_element_type=jnp.float32)


def dot_rows(left, right):
    return lax.dot_general(
        left, right, (((1,), (1,)), ((), ())), preferred_element_type=jnp.float32
    )


def normalize(field, gain, shift):
    centre = jnp.mean(field, axis=-1, keepdims=True)
    centred = field - centre
    spread = jnp.mean(centred * centred, axis=-1, keepdims=True)
    return centred * lax.rsqrt(spread + 1e-05) * gain + shift


def reparam_backward(grad_prefix, prefix_embed, hidden, reparam_in, reparam_out):
    grad_second = precise(hidden.T, grad_prefix)
    grad_second_bias = jnp.sum(grad_prefix, axis=0)
    grad_pre = precise(grad_prefix, reparam_out.T) * (1.0 - hidden * hidden)
    grad_first = precise(prefix_embed.T, grad_pre)
    grad_first_bias = jnp.sum(grad_pre, axis=0)
    grad_embed = precise(grad_pre, reparam_in.T)
    return (grad_embed, grad_first, grad_first_bias, grad_second, grad_second_bias)


MESH = pl.DeviceIdType.MESH
A = slice(None)
ROOT = math.sqrt(2.0 / math.pi)
N_A, N_P = 8, 4
N = N_A + N_P


def rows_loop(body, count=4):
    lax.fori_loop(0, count, lambda r, _: (body(r), 0)[1], 0)


def block(index, size=256):
    return pl.ds(pl.multiple_of(index * size, size), size)


def center(field):
    mean = jnp.mean(field, axis=-1, keepdims=True)
    centred = field - mean
    return centred, lax.rsqrt(jnp.mean(centred * centred, axis=-1, keepdims=True) + 1e-05)


def key_extra_into(kx, lengths, buckets):
    full = buckets[0] == LEN
    for r in range(4):
        place = lax.broadcasted_iota(jnp.int32, (256, 128), 0)
        b = lanes(256) % 64
        within = jnp.where(full, place + r * 256, place)
        extent = jnp.where(full, lengths[0, 0], lengths[0, r])
        e = jnp.where((b == 0) & (within >= extent), NEG, 0.0)
        e = jnp.where((b >= 1) & (b < 4), 1.0, e)
        e = jnp.where((b == 4 + r) & jnp.logical_not(full), NEG, e)
        kx[r * 256:(r + 1) * 256, :] = e.astype(bf16)


def front_kernel(
    dims, x_hbm, cot_hbm, wq, wo, wf, wp, b_qkv, b_out, b_fc, b_proj, gain, shift, embed, r_in, r_in_b,
    r_out, r_out_b, lengths, buckets,
    ga, gp, joined, o_hbm, lse_hbm, gm_hbm, gatt_hbm, out_hbm, hid_out, pre_out,
    sh, xb, nb, ob, gs, middle, acc, big, W, WP, kx, pkx, pk, pv, kext, vext, pkext, pvext, emb,
    zs, zr, zps, zpr, as_, ar, bs, br, cs, cr, ls, loc,
):
    Z, Y, X, C = dims
    dp, fs = lax.axis_index("dp"), lax.axis_index("fsdp")
    z, y, x, c = dp // Y, dp % Y, fs // C, fs % C
    zid = lambda dz: (lax.rem(z + dz, Z) * Y + y, fs)
    yid, xid, cid = (z * Y + (1 - y), fs), (dp, (1 - x) * C + c), (dp, x * C + (1 - c))

    def rc(s, d, ss, rs, dev):
        return pltpu.make_async_remote_copy(
            src_ref=s, dst_ref=d, send_sem=ss, recv_sem=rs, device_id=dev, device_id_type=MESH
        )

    def place(k, *ix):
        return ga.at[(k, *ix)] if k < N_A else gp.at[(k - N_A, *ix[1:])]

    def own(k):
        return (sh.at[k] if k < N_A else wp), place(k, z, y, x, c)

    def zc(k, dz):
        s, d = own(k)
        if k < N_A:
            return rc(s, d, zs.at[k, dz - 1], zr.at[k, dz - 1], zid(dz))
        return rc(s, d, zps.at[dz - 1], zpr.at[k - N_A], zid(dz))

    def ac(k, h):
        s = place(k, A, y, x, c, h)
        return rc(s, s, as_.at[k, h], ar.at[k, h], yid if h == 0 else xid)

    def bc(k, h):
        s = place(k, A, A, x, c, h) if h == 0 else place(k, A, y, A, c, h)
        return rc(s, s, bs.at[k, h], br.at[k, h], xid if h == 0 else yid)

    def cc(k):
        s = place(k, A, A, A, c)
        return rc(s, s, cs.at[k], cr.at[k], cid)

    def lc(k):
        return pltpu.make_async_copy(*own(k), ls.at[k])

    def stage_z(k):
        def go():
            lc(k).start()
            for dz in (2, 1, 3):
                zc(k, dz).start()
        if k < N_A:
            go()
        else:
            pl.when(z == k - N_A)(go)

    def stage_a(k):
        if k < N_A:
            lc(k).wait()
            for dz in (1, 2, 3):
                zc(k, dz).wait_recv()
        else:
            pl.when(z == k - N_A)(lambda: lc(k).wait())
            pl.when(z != k - N_A)(lambda: zc(k, 1).wait_recv())
        for h in (0, 1):
            ac(k, h).start()

    def stage_b(k):
        for h in (0, 1):
            ac(k, h).wait_recv()
        for h in (0, 1):
            bc(k, h).start()

    def stage_c(k):
        for h in (0, 1):
            bc(k, h).wait_recv()
        cc(k).start()

    def pump(t):
        if t + 1 < N:
            stage_z(t + 1)
        if 0 <= t - 2 < N:
            stage_c(t - 2)
        if 0 <= t - 1 < N:
            stage_b(t - 1)
        if t < N:
            stage_a(t)
        if 0 <= t - 3 < N:
            cc(t - 3).wait_recv()

    def local(s, d, i):
        return pltpu.make_async_copy(s, d, loc.at[i])

    def load(k):
        if k < N_A:
            return local(ga.at[k], W.at[k % 3], 20 + k)
        return local(gp.at[k - N_A], WP.at[k % 2], 20 + k)

    shards = [local(wq.at[:, :, pl.ds(j * 1024, 1024)], sh.at[j], j) for j in range(3)]
    shards += [local(wo, sh.at[3], 3)]
    shards += [local(wf.at[:, :, pl.ds(j * 1024, 1024)], sh.at[4 + j], 4 + j) for j in range(4)]
    for d in shards:
        d.start()
    rin = local(r_in, acc.at[:, pl.ds(0, 512)], 8)
    rout = [local(r_out.at[:, pl.ds(j * 1024, 1024)], gs.at[pl.ds(j * 512, 512), :], 9 + j) for j in (0, 1)]
    xload = local(x_hbm, xb, 11)
    xload.start()
    bar = pltpu.get_barrier_semaphore()
    for d in [zid(dz) for dz in range(1, Z)] + [yid, xid, cid]:
        pl.semaphore_signal(bar, inc=1, device_id=d, device_id_type=MESH)
    pl.semaphore_wait(bar, Z + 2)
    for d in shards:
        d.wait()
    stage_z(0)
    for d in [rin] + rout:
        d.start()
    xload.wait()

    def norm_one(r):
        rows = block(r)
        centred, inv = center(xb[rows, :].astype(f32))
        nb[rows, :] = (centred * inv * gain[0:1, :] + shift[0:1, :]).astype(bf16)
    rows_loop(norm_one)
    pump(0)
    emb[...] = jnp.zeros_like(emb)
    emb[0:10, :] = embed[...]
    rin.wait()
    hid = jnp.tanh(
        jnp.dot(emb[...], acc[:, 0:512], precision=HIGHEST, preferred_element_type=f32) + r_in_b[...]
    )
    hid_out[...] = hid
    pump(1)
    live = lax.broadcasted_iota(jnp.int32, (16, 1024), 0) < 10
    for j, dest in ((0, pk), (1, pv)):
        rout[j].wait()
        t = jnp.dot(hid, gs[j * 512:(j + 1) * 512, :], precision=HIGHEST, preferred_element_type=f32)
        t = jnp.where(live, t + r_out_b[:, j * 1024:(j + 1) * 1024], 0.0)
        dest[...] = jnp.zeros_like(dest)
        dest[0:16, :] = t.astype(bf16)
        pre_out[:, j * 1024:(j + 1) * 1024] = dest[...]
    key_extra_into(kx, lengths, buckets)
    pkx[...] = prefix_extra()
    pump(2)
    pump(3)
    load(0).start()
    saves = []
    for k in range(3):
        load(k).wait()
        dest = big.at[5 + k]

        def project(cb, k=k, dest=dest):
            cols = block(cb)
            t = jnp.dot(nb[...], W[k, ..., cols].reshape(1024, 256), preferred_element_type=f32)
            t = t + b_qkv[:, pl.ds(pl.multiple_of(k * 1024 + cb * 256, 256), 256)].astype(f32)
            t = t.astype(bf16)
            dest[:, cols] = t * jnp.asarray(0.125, bf16) if k == 0 else t
        rows_loop(project)
        saves.append(local(dest, joined.at[:, pl.ds(k * 1024, 1024)], 12 + k))
        saves[-1].start()
        pump(4 + k)
        load(k + 1).start()

    def attend(p):
        cols = block(p, 128)
        fwd_pair(
            *(big.at[5 + k, :, cols] for k in range(3)), pk.at[:, cols], pv.at[:, cols], kx, pkx,
            ob.at[:, cols], gs.at[:, cols], kext, vext, pkext, pvext,
        )
        for at, t in ((1, 7), (4, 8), (7, 9)):
            pl.when(p == at)(functools.partial(pump, t))
    rows_loop(attend, 8)
    keep = [local(ob, o_hbm, 15), local(gs, lse_hbm, 16)]
    for d in keep:
        d.start()
    load(3).wait()

    def project_out(cb):
        cols = block(cb)
        t = jnp.dot(ob[...], W[0, ..., cols].reshape(1024, 256), preferred_element_type=f32)
        middle[:, cols] = xb[:, cols].astype(f32) + (t + b_out[:, cols].astype(f32))
    load(4).start()
    rows_loop(project_out)
    cotload = local(cot_hbm, xb, 17)
    cotload.start()
    load(5).start()
    pump(10)

    def norm_two(r):
        rows = block(r)
        m = middle[rows, :]
        centred, inv = center(m)
        nb[rows, :] = (centred * inv * gain[1:2, :] + shift[1:2, :]).astype(bf16)
        acc[rows, :] = m + b_proj[...].astype(f32)
    rows_loop(norm_two)
    for d in saves + keep:
        d.wait()
    for f in range(4):
        k = 4 + f
        load(k).wait()
        if f + 2 < 4:
            load(k + 2).start()

        def hidden_part(cb, k=k, f=f):
            cols = block(cb)
            u = jnp.dot(nb[...], W[k % 3, ..., cols].reshape(1024, 256), preferred_element_type=f32)
            u = u + b_fc[:, pl.ds(pl.multiple_of(f * 1024 + cb * 256, 256), 256)].astype(f32)
            sq = u * u
            t = jnp.tanh(u * (ROOT + (ROOT * 0.044715) * sq))
            plus = 0.5 + 0.5 * t
            big[f, :, cols] = (u * plus).astype(bf16)
            slope = plus + (0.5 * u) * (1.0 - t * t) * (ROOT + (3 * ROOT * 0.044715) * sq)
            big[4 + f, :, cols] = slope.astype(bf16)
        rows_loop(hidden_part)
        if f == 1:
            pump(11)
            load(8).start()
    load(4).start()
    cotload.wait()
    gs[...] = jnp.zeros_like(gs)
    for j in range(4):
        k = 8 + j
        load(k).wait()
        slot = k % 2

        def out_part(cb, j=j, slot=slot):
            cols = block(cb)
            t = jnp.dot(big[j], WP[slot, ..., cols].reshape(1024, 256), preferred_element_type=f32)
            acc[:, cols] += t
            g = dot(xb[...], WP[slot, cb // 2, cb % 2].reshape(256, 1024), NT)
            big[4 + j, :, cols] = (g * big[4 + j, :, cols].astype(f32)).astype(bf16)
        rows_loop(out_part)
        if j < 3:
            pump(12 + j)
            load(k + 1).start()
        load(4 + j).wait()
        load(4 + j + 1 if j < 3 else 3).start()

        def second_part(cb, j=j):
            cols = block(cb)
            gs[:, cols] += dot(big[4 + j], W[(4 + j) % 3, cb].reshape(256, 1024), NT)
        rows_loop(second_part)

    def norm_two_back(r):
        rows = block(r)
        centred, inv = center(middle[rows, :])
        n = centred * inv
        g = gs[rows, :] * gain[1:2, :]
        t = g - jnp.mean(g, axis=-1, keepdims=True) - n * jnp.mean(g * n, axis=-1, keepdims=True)
        t = xb[rows, :].astype(f32) + inv * t
        gs[rows, :] = t
        nb[rows, :] = t.astype(bf16)
        ob[rows, :] = acc[rows, :].astype(bf16)
    rows_loop(norm_two_back)
    last = [local(gs, gm_hbm, 18), local(ob, out_hbm, 19)]
    for d in last:
        d.start()
    load(3).wait()

    def out_back(cb):
        big[0, :, block(cb)] = dot(nb[...], W[0, cb].reshape(256, 1024), NT).astype(bf16)
    rows_loop(out_back)
    last.append(local(big.at[0], gatt_hbm, 32))
    last[-1].start()
    for k in range(N):
        if k < N_A:
            for dz in (1, 2, 3):
                zc(k, dz).wait_send()
        for h in (0, 1):
            ac(k, h).wait_send()
            bc(k, h).wait_send()
        cc(k).wait_send()
    for dz in (1, 2, 3):
        zc(N_A, dz).wait_send()
    for d in last:
        d.wait()


def front(dims, x, cot, wq, wo, wf, wp, b_qkv, b_out, b_fc, b_proj, gain, shift, embed, r_in, r_in_b, r_out, r_out_b, lengths, buckets):
    Z, Y, X, C = dims
    S = pltpu.SemaphoreType.DMA
    V = pltpu.VMEM
    anys, vm, sm = (pl.BlockSpec(memory_space=s) for s in (pl.ANY, pltpu.VMEM, pltpu.SMEM))
    sds = jax.ShapeDtypeStruct
    T = x.shape[0]
    row = lambda t: t.reshape(1, -1)
    return pl.pallas_call(
        functools.partial(front_kernel, dims),
        out_shape=[
            sds((N_A, Z, Y, X, C, 2, 16, 1024), bf16), sds((N_P, Y, X, C, 2, 64, 1024), bf16),
            sds((T, 3072), bf16), sds((T, 1024), bf16), sds((T, 1024), f32), sds((T, 1024), f32),
            sds((T, 1024), bf16), sds((T, 1024), bf16), sds((16, 512), f32), sds((128, 2048), bf16),
        ],
        in_specs=[anys] * 6 + [vm] * 7 + [anys, vm, anys, vm, sm, sm],
        out_specs=[anys] * 8 + [vm] * 2,
        scratch_shapes=[
            V((N_A, 2, 16, 1024), bf16), V((T, 1024), bf16), V((T, 1024), bf16), V((T, 1024), bf16),
            V((T, 1024), f32), V((T, 1024), f32), V((T, 1024), f32), V((8, T, 1024), bf16),
            V((3, Z, Y, X, C, 2, 16, 1024), bf16), V((2, Y, X, C, 2, 64, 1024), bf16),
            V((T, 128), bf16), V((128, 128), bf16), V((128, 1024), bf16), V((128, 1024), bf16),
            *ext_scratch(), V((16, 1024), f32),
            S((N_A, 3)), S((N_A, 3)), S((3,)), S((N_P,)), S((N, 2)), S((N, 2)), S((N, 2)), S((N, 2)),
            S((N,)), S((N,)), S((N,)), S((33,)),
        ],
        compiler_params=pltpu.CompilerParams(
            collective_id=0, has_side_effects=True, vmem_limit_bytes=60 << 20
        ),
    )(
        x, cot, *(w.reshape(2, 16, w.shape[1]) for w in (wq, wo, wf)), wp.reshape(2, 64, 1024),
        row(b_qkv), row(b_out), row(b_fc), row(b_proj), gain, shift, embed, r_in, row(r_in_b), r_out,
        row(r_out_b), lengths, buckets,
    )


def prefix_back(blocks):
    return blocks.reshape(8, 2, 64, 128)[..., :PREFIX].transpose(3, 0, 1, 2).reshape(PREFIX, D)


def plain_front(
    tokens, cotangent, w_qkv, w_out, w_fc, w_proj, bias_qkv, bias_out, bias_fc, bias_proj,
    ln_gain, ln_shift, prefix_embed, reparam_in, reparam_in_bias, reparam_out, reparam_out_bias,
    kx, pkx,
):
    full_qkv, full_out, full_fc, full_proj = (
        lax.all_gather(t, ("dp", "fsdp"), axis=0, tiled=True) for t in (w_qkv, w_out, w_fc, w_proj)
    )
    hidden = jnp.tanh(precise(prefix_embed, reparam_in) + reparam_in_bias)
    prefix_rows = (precise(hidden, reparam_out) + reparam_out_bias).astype(bf16)
    padded = jnp.pad(prefix_rows, ((0, 128 - PREFIX), (0, 0)))
    inputs = tokens.astype(jnp.float32)
    normed = normalize(inputs, ln_gain[0], ln_shift[0]).astype(bf16)
    joined = (lowdot(normed, full_qkv) + bias_qkv.astype(jnp.float32)).astype(bf16)
    scale = jnp.where(jnp.arange(3 * D) < D, 0.125, 1.0).astype(bf16)
    joined = joined * scale
    attended, lse = attend_forward(joined, padded[:, :D], padded[:, D:], kx, pkx)
    middle = inputs + (lowdot(attended, full_out) + bias_out.astype(jnp.float32))
    second = normalize(middle, ln_gain[1], ln_shift[1]).astype(bf16)
    before = lowdot(second, full_fc) + bias_fc.astype(jnp.float32)
    activated = jax.nn.gelu(before, approximate=True).astype(bf16)
    result = middle + (lowdot(activated, full_proj) + bias_proj.astype(jnp.float32))
    grad_hidden = dot_rows(cotangent, full_proj)
    gelu_pull = jax.vjp(lambda field: jax.nn.gelu(field, approximate=True), before)[1]
    grad_before = gelu_pull(grad_hidden)[0].astype(bf16)
    grad_second = dot_rows(grad_before, full_fc)
    norm_two = jax.vjp(lambda field: normalize(field, ln_gain[1], ln_shift[1]), middle)[1]
    grad_middle = cotangent.astype(jnp.float32) + norm_two(grad_second)[0]
    grad_attended = dot_rows(grad_middle.astype(bf16), full_out).astype(bf16)
    weights = [full_qkv[:, i * D : (i + 1) * D] for i in range(3)]
    return weights, joined, attended, lse, grad_middle, grad_attended, result.astype(bf16), hidden, padded


def on_device(dims, *args):
    (
        tokens, cotangent, w_qkv, w_out, w_fc, w_proj, bias_qkv, bias_out, bias_fc, bias_proj,
        ln_gain, ln_shift, prefix_embed, reparam_in, reparam_in_bias, reparam_out, reparam_out_bias,
        lengths, buckets,
    ) = args
    kx, pkx = key_extra(lengths[0], buckets[0]), prefix_extra()
    if dims is None:
        weights, joined, attended, lse, grad_middle, grad_attended, result, hidden, padded = plain_front(
            *args[:-2], kx, pkx
        )
    else:
        (
            gathered, _, joined, attended, lse, grad_middle, grad_attended, result, hidden, padded,
        ) = front(dims, *args)
        weights = [gathered[i].reshape(D, D) for i in range(3)]
        hidden = hidden[:PREFIX]
    pk, pv = padded[:, :D], padded[:, D:]
    dq, dk, dv, dpk, dpv = attend_backward(joined, pk, pv, kx, pkx, attended, lse, grad_attended)
    grad_prefix = jnp.concatenate([prefix_back(dpk), prefix_back(dpv)], 1)
    grad_prefix = lax.psum(grad_prefix, ("dp", "fsdp"))
    grad_normed = sum(dot_rows(g, w) for g, w in zip((dq, dk, dv), weights))
    inputs = tokens.astype(jnp.float32)
    norm_one = jax.vjp(lambda field: normalize(field, ln_gain[0], ln_shift[0]), inputs)[1]
    grad_tokens = (grad_middle + norm_one(grad_normed)[0]).astype(bf16)
    return (
        result,
        grad_tokens,
        *reparam_backward(grad_prefix, prefix_embed, hidden, reparam_in, reparam_out),
    )


def chip_dims(mesh):
    if dict(mesh.shape) == {"dp": 8, "fsdp": 4}:
        return (4, 2, 2, 2)
    return None


def solution(mesh):
    split, lone = P(("dp", "fsdp"), None), P()
    return jax.shard_map(
        functools.partial(on_device, chip_dims(mesh)),
        mesh=mesh,
        in_specs=(split,) * 6 + (lone,) * 11 + (split, P(("dp", "fsdp"))),
        out_specs=(split, split) + (lone,) * 5,
        check_vma=False,
    )
```

```python
import functools, math
import jax, jax.numpy as jnp
from jax import lax
from jax.experimental import pallas as pl
from jax.experimental.pallas import tpu as pltpu
from jax.sharding import PartitionSpec as P

f32, bf16 = jnp.float32, jnp.bfloat16
MESH = pl.DeviceIdType.MESH
A = slice(None)
D = 1024
LEN = 1024
PREFIX = 10
BQ = 256
NQ = LEN // BQ
NEG = -1e30
ROOT = math.sqrt(2.0 / math.pi)
HIGHEST = lax.Precision.HIGHEST
NT = (((1,), (1,)), ((), ()))
NN = (((1,), (0,)), ((), ()))
QUERY, KEY, VALUE, OUT = range(4)
FC = (4, 6, 8, 10)
PROJ = (5, 7, 9, 11)
N = 12


def dot(a, b, dims=NN):
    return lax.dot_general(a, b, dims, preferred_element_type=f32)


def precise(a, b, dims=NN):
    return lax.dot_general(a, b, dims, precision=HIGHEST, preferred_element_type=f32)


def lanes(rows):
    return lax.broadcasted_iota(jnp.int32, (rows, 128), 1)


def split_three(value):
    high = value.astype(bf16)
    rest = value - high.astype(f32)
    mid = rest.astype(bf16)
    return high.astype(f32), mid.astype(f32), rest - mid.astype(f32)


def extra(base, value):
    b = lanes(value.shape[0]) % 64
    high, mid, low = split_three(value)
    return jnp.where(b == 1, high, jnp.where(b == 2, mid, jnp.where(b == 3, low, base))).astype(bf16)


def query_flags(i, rows):
    b = lanes(rows) % 64
    return jnp.where((b == 0) | ((b >= 4) & (b < 8) & (b != 4 + i)), 1.0, 0.0)


def half(a, h):
    return jnp.where((lanes(a.shape[0]) < 64) == (h == 0), a, jnp.zeros_like(a))


def causal():
    shape = (BQ, BQ)
    return lax.broadcasted_iota(jnp.int32, shape, 1) <= lax.broadcasted_iota(jnp.int32, shape, 0)


def forward_pair(q, k, v, pk, pv, kx, pkx, o_ref, qx_ref, kext, vext, pkext, pvext):
    ln, lp = lanes(LEN), lanes(128)
    for h in (0, 1):
        rows = slice(h * 128, (h + 1) * 128)
        kext[h, :, :128] = half(k[...], h)
        kext[h, :, 128:] = half(kx[...], h)
        vext[h, :, :128] = half(v[...], h)
        vext[h, :, 128:] = jnp.where((ln < 64) == (h == 0), 1.0, 0.0).astype(bf16)
        pkext[rows, :128] = half(pk[...], h)
        pkext[rows, 128:] = half(pkx[...], h)
        pvext[rows, :128] = half(pv[...], h)
        pvext[rows, 128:] = jnp.where((lp < 64) == (h == 0), 1.0, 0.0).astype(bf16)
    for i in range(NQ):
        rows, n = pl.ds(i * BQ, BQ), (i + 1) * BQ
        flags = query_flags(i, BQ)
        qe = jnp.concatenate([q[rows, :], flags.astype(bf16)], axis=1)
        before = dot(qe, pkext[...], NT)
        acc, tops, parts = None, [], []
        for h in (0, 1):
            s = dot(qe, kext[h, :n, :], NT)
            near = jnp.where(causal(), s[:, n - BQ :], NEG)
            first = before[:, h * 128 : (h + 1) * 128]
            m = jnp.maximum(
                jnp.max(near, axis=1, keepdims=True), jnp.max(first, axis=1, keepdims=True)
            )
            if i:
                m = jnp.maximum(m, jnp.max(s[:, : n - BQ], axis=1, keepdims=True))
            a = dot(jnp.exp(near - m).astype(bf16), vext[h, n - BQ : n, :])
            if i:
                a = a + dot(jnp.exp(s[:, : n - BQ] - m).astype(bf16), vext[h, : n - BQ, :])
            parts.append(jnp.exp(first - m).astype(bf16))
            tops.append(m)
            acc = a if acc is None else acc + a
        acc = acc + dot(jnp.concatenate(parts, axis=1), pvext[...])
        total = acc[:, 128:]
        o_ref[rows, :] = (acc[:, :128] / total).astype(bf16)
        lse = jnp.where(lanes(BQ) < 64, tops[0], tops[1]) + jnp.log(total)
        qx_ref[rows, :] = extra(flags, -lse)


def backward_pair(
    q, k, v, kx, qx, do, dx, dsp, pkd, dq_ref, dk_ref, dv_ref, kext, vext, qt, dot_t, dkt, dvt
):
    b = lanes(LEN) % 64
    ones = jnp.where((b >= 1) & (b < 4), 1.0, 0.0).astype(bf16)
    for h in (0, 1):
        kext[h, :, :128] = half(k[...], h)
        kext[h, :, 128:] = half(kx[...], h)
        vext[h, :, :128] = half(v[...], h)
        vext[h, :, 128:] = half(ones, h)
    qt[...] = q[...].T
    dot_t[...] = do[...].T
    for i in reversed(range(NQ)):
        rows, n = pl.ds(i * BQ, BQ), (i + 1) * BQ
        qe = jnp.concatenate([q[rows, :], qx[rows, :]], axis=1)
        de = jnp.concatenate([do[rows, :], dx[rows, :]], axis=1)
        dq = dot(dsp[rows, :], pkd[...])
        for h in (0, 1):
            hr = slice(h * 64, (h + 1) * 64)
            qth, dth = qt[hr, i * BQ : (i + 1) * BQ], dot_t[hr, i * BQ : (i + 1) * BQ]
            s = dot(qe, kext[h, :n, :], NT)
            g = dot(de, vext[h, :n, :], NT)
            p = jnp.exp(s)
            near = jnp.where(causal(), p[:, n - BQ :], 0.0)
            p = near if i == 0 else jnp.concatenate([p[:, : n - BQ], near], axis=1)
            ds = (p * g).astype(bf16)
            p = p.astype(bf16)
            dq = dq + dot(ds, kext[h, :n, :128])
            if i == NQ - 1:
                dkt[hr, :n] = dot(qth, ds)
                dvt[hr, :n] = dot(dth, p)
            else:
                dkt[hr, :n] += dot(qth, ds)
                dvt[hr, :n] += dot(dth, p)
        dq_ref[rows, :] = (dq * 0.125).astype(bf16)
    dk_ref[...] = dkt[...].T.astype(bf16)
    dv_ref[...] = dvt[...].T.astype(bf16)


def block(index, size=256):
    return pl.ds(pl.multiple_of(index * size, size), size)


def loop(body, count=4):
    lax.fori_loop(0, count, lambda r, _: (body(r), 0)[1], 0)


def unrolled(body, count=4):
    for r in range(count):
        body(r)


def center(field):
    mean = jnp.mean(field, axis=-1, keepdims=True)
    centred = field - mean
    return centred, lax.rsqrt(jnp.mean(centred * centred, axis=-1, keepdims=True) + 1e-05)


def norm_back(grad, normed, inv):
    down = grad - jnp.mean(grad, axis=-1, keepdims=True)
    return inv * (down - normed * jnp.mean(grad * normed, axis=-1, keepdims=True))


def key_columns(kx, lengths, buckets):
    full = buckets[0] == LEN
    b = lanes(256) % 64
    for r in range(4):
        place = lax.broadcasted_iota(jnp.int32, (256, 128), 0)
        within = jnp.where(full, place + r * 256, place)
        extent = jnp.where(full, lengths[0, 0], lengths[0, r])
        e = jnp.where((b == 0) & (within >= extent), NEG, 0.0)
        e = jnp.where((b >= 1) & (b < 4), 1.0, e)
        e = jnp.where((b == 4 + r) & jnp.logical_not(full), NEG, e)
        kx[r * 256 : (r + 1) * 256, :] = e.astype(bf16)


def prefix_columns():
    r, b = lax.broadcasted_iota(jnp.int32, (128, 128), 0), lanes(128) % 64
    return jnp.where((b == 0) & (r >= PREFIX), NEG, jnp.where((b >= 1) & (b < 4), 1.0, 0.0)).astype(bf16)


def head_rows(shape, per_head):
    r = lax.broadcasted_iota(jnp.int32, shape, 0) // 16
    return r == lax.broadcasted_iota(jnp.int32, shape, 1) // per_head


def layer_kernel(
    dims, x_hbm, cot_hbm, wq, wo, wf, wp, b_qkv, b_out, b_fc, b_proj, gain, shift, embed, r_in, r_in_b,
    r_out, r_out_b, lengths, buckets,
    ga, gp, out_hbm, gtok_hbm, hid_out, pre_out, grad_prefix_out, emb,
    sh, xb, nb, ob, qkv, qx, dob, gs, middle, acc, big, W, WP, kx, pkx, pk, pv, kext, vext, pkext, pvext,
    qt, dot_t, dkt, dvt, dsp, pkd, total, came,
    zs, zr, zps, zpr, as_, ar, bs, br, cs, cr, ls, loc, ts, tr,
):
    Z, Y, X, C = dims
    dp, fs = lax.axis_index("dp"), lax.axis_index("fsdp")
    z, y, x, c = dp // Y, dp % Y, fs // C, fs % C
    zid = lambda dz: (lax.rem(z + dz, Z) * Y + y, fs)
    yid, xid, cid = (z * Y + (1 - y), fs), (dp, (1 - x) * C + c), (dp, x * C + (1 - c))

    def remote(s, d, ss, rs, dev):
        return pltpu.make_async_remote_copy(
            src_ref=s, dst_ref=d, send_sem=ss, recv_sem=rs, device_id=dev, device_id_type=MESH
        )

    def place(k, *ix):
        if k in PROJ:
            return gp.at[(PROJ.index(k), *ix[1:])]
        return ga.at[(k if k < 4 else 4 + FC.index(k), *ix)]

    def own(k):
        if k in PROJ:
            return wp, place(k, z, y, x, c)
        return sh.at[k if k < 4 else 4 + FC.index(k)], place(k, z, y, x, c)

    def z_copy(k, dz):
        s, d = own(k)
        if k in PROJ:
            return remote(s, d, zps.at[dz - 1], zpr.at[PROJ.index(k)], zid(dz))
        return remote(s, d, zs.at[k, dz - 1], zr.at[k, dz - 1], zid(dz))

    def a_copy(k, h):
        s = place(k, A, y, x, c, h)
        return remote(s, s, as_.at[k, h], ar.at[k, h], yid if h == 0 else xid)

    def b_copy(k, h):
        s = place(k, A, A, x, c, h) if h == 0 else place(k, A, y, A, c, h)
        return remote(s, s, bs.at[k, h], br.at[k, h], xid if h == 0 else yid)

    def c_copy(k):
        s = place(k, A, A, A, c)
        return remote(s, s, cs.at[k], cr.at[k], cid)

    def own_copy(k):
        return pltpu.make_async_copy(*own(k), ls.at[k])

    def stage_z(k):
        def go():
            own_copy(k).start()
            for dz in (2, 1, 3):
                z_copy(k, dz).start()

        if k in PROJ:
            pl.when(z == PROJ.index(k))(go)
        else:
            go()

    def stage_a(k):
        if k in PROJ:
            j = PROJ.index(k)
            pl.when(z == j)(lambda: own_copy(k).wait())
            pl.when(z != j)(lambda: z_copy(k, 1).wait_recv())
        else:
            own_copy(k).wait()
            for dz in (1, 2, 3):
                z_copy(k, dz).wait_recv()
        for h in (0, 1):
            a_copy(k, h).start()

    def stage_b(k):
        for h in (0, 1):
            a_copy(k, h).wait_recv()
        for h in (0, 1):
            b_copy(k, h).start()

    def stage_c(k):
        for h in (0, 1):
            b_copy(k, h).wait_recv()
        c_copy(k).start()

    def pump(t):
        if t + 1 < N:
            stage_z(t + 1)
        if 0 <= t - 2 < N:
            stage_c(t - 2)
        if 0 <= t - 1 < N:
            stage_b(t - 1)
        if t < N:
            stage_a(t)
        if 0 <= t - 3 < N:
            c_copy(t - 3).wait_recv()

    def local(s, d, i):
        return pltpu.make_async_copy(s, d, loc.at[i])

    slots = {QUERY: 0, KEY: 1, VALUE: 2, OUT: 0, FC[0]: 1, FC[1]: 2, FC[2]: 0, FC[3]: 1}

    def load(k, slot=None):
        if k in PROJ:
            return local(gp.at[PROJ.index(k)], WP.at[PROJ.index(k) % 2], 20 + k)
        return local(ga.at[k if k < 4 else 4 + FC.index(k)], W.at[slots[k] if slot is None else slot], 20 + k)

    shards = [local(wq.at[:, :, pl.ds(j * D, D)], sh.at[j], j) for j in range(3)]
    shards += [local(wo, sh.at[3], 3)]
    shards += [local(wf.at[:, :, pl.ds(j * D, D)], sh.at[4 + j], 4 + j) for j in range(4)]
    for d in shards:
        d.start()
    rin = local(r_in, middle.at[:, pl.ds(0, 512)], 8)
    rout = [local(r_out.at[:, pl.ds(j * D, D)], acc.at[pl.ds(j * 512, 512), :], 9 + j) for j in (0, 1)]
    xload = local(x_hbm, xb, 11)
    xload.start()
    barrier = pltpu.get_barrier_semaphore()
    for d in [zid(dz) for dz in range(1, Z)] + [yid, xid, cid]:
        pl.semaphore_signal(barrier, inc=1, device_id=d, device_id_type=MESH)
    pl.semaphore_wait(barrier, Z + 2)
    for d in shards:
        d.wait()
    stage_z(0)
    for d in [rin] + rout:
        d.start()
    xload.wait()

    def norm_one(r):
        rows = block(r)
        centred, inv = center(xb[rows, :].astype(f32))
        nb[rows, :] = (centred * inv * gain[0:1, :] + shift[0:1, :]).astype(bf16)

    loop(norm_one)
    pump(0)
    emb[...] = jnp.zeros_like(emb)
    emb[0:PREFIX, :] = embed[...]
    rin.wait()
    hid = jnp.tanh(precise(emb[...], middle[:, 0:512]) + r_in_b[...])
    hid_out[...] = hid
    pump(1)
    live = lax.broadcasted_iota(jnp.int32, (16, D), 0) < PREFIX
    for j, dest in ((0, pk), (1, pv)):
        rout[j].wait()
        t = precise(hid, acc[j * 512 : (j + 1) * 512, :])
        t = jnp.where(live, t + r_out_b[:, j * D : (j + 1) * D], 0.0)
        dest[...] = jnp.zeros_like(dest)
        dest[0:16, :] = t.astype(bf16)
    key_columns(kx, lengths, buckets)
    pkx[...] = prefix_columns()
    pump(2)
    pump(3)
    load(QUERY).start()
    for k in range(3):
        load(k).wait()
        for cb in range(4):
            cols = slice(cb * 256, (cb + 1) * 256)
            t = dot(nb[...], W[k, ..., cols].reshape(D, 256))
            t = t + b_qkv[:, k * D + cb * 256 : k * D + (cb + 1) * 256].astype(f32)
            t = t.astype(bf16)
            qkv[k, :, cols] = t * jnp.asarray(0.125, bf16) if k == 0 else t
        pump(4 + k)
        load(k + 1).start()

    def attend(p):
        cols = block(p, 128)
        forward_pair(
            *(qkv.at[k, :, cols] for k in range(3)), pk.at[:, cols], pv.at[:, cols], kx, pkx,
            ob.at[:, cols], qx.at[:, cols], kext, vext, pkext, pvext,
        )
        for at, t in ((1, 7), (4, 8), (6, 9)):
            pl.when(p == at)(functools.partial(pump, t))

    loop(attend, 8)
    load(OUT).wait()
    load(FC[0]).start()
    load(PROJ[0]).start()
    load(FC[1]).start()
    for cb in range(4):
        cols = slice(cb * 256, (cb + 1) * 256)
        t = dot(ob[...], W[0, ..., cols].reshape(D, 256))
        middle[:, cols] = xb[:, cols].astype(f32) + (t + b_out[:, cols].astype(f32))
    cotload = local(cot_hbm, xb, 12)
    cotload.start()

    def norm_two(r):
        rows = block(r)
        m = middle[rows, :]
        centred, inv = center(m)
        nb[rows, :] = (centred * inv * gain[1:2, :] + shift[1:2, :]).astype(bf16)
        acc[rows, :] = m + b_proj[...].astype(f32)
        gs[rows, :] = jnp.zeros_like(m)

    loop(norm_two)
    for f in range(4):
        k, r = FC[f], f % 2
        load(k).wait()
        for cb in range(4):
            cols = slice(cb * 256, (cb + 1) * 256)
            u = dot(nb[...], W[slots[k], ..., cols].reshape(D, 256))
            u = u + b_fc[:, f * D + cb * 256 : f * D + (cb + 1) * 256].astype(f32)
            sq = u * u
            t = jnp.tanh(u * (ROOT + (ROOT * 0.044715) * sq))
            plus = 0.5 + 0.5 * t
            big[r, :, cols] = (u * plus).astype(bf16)
            slope = plus + (0.5 * u) * (1.0 - t * t) * (ROOT + (3 * ROOT * 0.044715) * sq)
            big[2 + r, :, cols] = slope.astype(bf16)
        if f == 0:
            pump(10)
            cotload.wait()
        elif f < 3:
            pump(11 + f)
        if f == 3:
            pump(14)
            load(PROJ[3]).start()
        load(PROJ[f]).wait()
        if f == 2:
            load(FC[3]).start()
        for cb in range(4):
            cols = slice(cb * 256, (cb + 1) * 256)
            acc[:, cols] += dot(big[r], WP[r, ..., cols].reshape(D, 256))
            g = dot(xb[...], WP[r, cb // 2, cb % 2].reshape(256, D), NT)
            big[2 + r, :, cols] = (g * big[2 + r, :, cols].astype(f32)).astype(bf16)
        if f == 0:
            pump(11)
            load(FC[2]).start()
        if f < 2:
            load(PROJ[f + 1]).start()
        for cb in range(4):
            cols = slice(cb * 256, (cb + 1) * 256)
            gs[:, cols] += dot(big[2 + r], W[slots[k], cb].reshape(256, D), NT)
        if f == 2:
            load(OUT, 2).start()
            load(QUERY, 0).start()
    load(KEY, 1).start()

    def norm_two_back(r):
        rows = block(r)
        centred, inv = center(middle[rows, :])
        t = norm_back(gs[rows, :] * gain[1:2, :], centred * inv, inv)
        t = xb[rows, :].astype(f32) + t
        gs[rows, :] = t
        nb[rows, :] = t.astype(bf16)
        big[0, rows, :] = acc[rows, :].astype(bf16)

    loop(norm_two_back)
    out_save = local(big.at[0], out_hbm, 13)
    out_save.start()
    xload = local(x_hbm, xb, 11)
    xload.start()
    for d in rout:
        d.start()
    load(OUT, 2).wait()
    for cb in range(4):
        dob[:, cb * 256 : (cb + 1) * 256] = dot(nb[...], W[2, cb].reshape(256, D), NT).astype(bf16)
    load(VALUE, 2).start()

    gi = lax.broadcasted_iota(jnp.int32, (128, 128), 0) // 64
    group = jnp.where(gi == lanes(128) // 64, 1.0, 0.0).astype(bf16)

    def delta(p):
        cols = block(p, 128)
        prod = dob[:, cols].astype(f32) * ob[:, cols].astype(f32)
        high = prod.astype(bf16)
        low = (prod - high.astype(f32)).astype(bf16)
        big[3, :, cols] = extra(0.0, -(dot(high, group) + dot(low, group)))

    loop(delta, 8)
    same = head_rows((256, D), 64)
    spread = [jnp.concatenate([t[0:16, :]] * 16, axis=0) for t in (pk, pv)]
    spread = [jnp.where(same, t, jnp.zeros_like(t)) for t in spread]
    pkd[...] = spread[0]
    lane = lax.broadcasted_iota(jnp.int32, (256, D), 1) % 64
    unit = jnp.where(same & (lane >= 1) & (lane < 4), 1.0, 0.0)
    dead = lax.broadcasted_iota(jnp.int32, (256, D), 0) % 16 >= PREFIX
    mask = jnp.where(same & (lane == 0) & dead, NEG, unit).astype(bf16)
    unit = unit.astype(bf16)
    prob = jnp.exp(dot(qkv[0], spread[0], NT) + dot(qx[...], mask, NT))
    grad = dot(dob[...], spread[1], NT) + dot(big[3], unit, NT)
    dsp[...] = (prob * grad).astype(bf16)
    for j, (left, right) in enumerate(((dsp[...], qkv[0]), (prob.astype(bf16), dob[...]))):
        t = jnp.where(same, dot(left.T, right), 0.0)
        total[0, :, j * D : (j + 1) * D] = jnp.sum(t.reshape(16, 16, D), axis=0)

    partners = [cid, xid, yid, ((z + 1 - 2 * (z % 2)) * Y + y, fs), zid(2)]

    def exchange(s):
        return remote(total.at[s], came.at[s], ts.at[s], tr.at[s], partners[s])

    def step(s):
        if s > 0:
            exchange(s - 1).wait_recv()
            total[s] = total[s - 1] + came[s - 1]
        if s < 5:
            exchange(s).start()

    out_save.wait()

    def attend_back(p):
        for s in range(6):
            pl.when(p == s)(functools.partial(step, s))
        cols = block(p, 128)
        backward_pair(
            *(qkv.at[k, :, cols] for k in range(3)), kx, qx.at[:, cols], dob.at[:, cols],
            big.at[3, :, cols], dsp, pkd.at[:, cols], *(big.at[k, :, cols] for k in range(3)),
            kext, vext, qt, dot_t, dkt, dvt,
        )

    loop(attend_back, 8)
    for d in rout:
        d.wait()
    grad_prefix_out[...] = total[5]
    hid = hid_out[...]
    t = sum(precise(total[5, :, j * D : (j + 1) * D], acc[j * 512 : (j + 1) * 512, :], NT) for j in (0, 1))
    pre_out[...] = t * (1.0 - hid * hid)
    for k in range(3):
        load(k, k).wait()
    for cb in range(4):
        cols = slice(cb * 256, (cb + 1) * 256)
        acc[:, cols] = sum(dot(big[k], W[k, cb].reshape(256, D), NT) for k in range(3))
    xload.wait()

    def norm_one_back(r):
        rows = block(r)
        centred, inv = center(xb[rows, :].astype(f32))
        t = norm_back(acc[rows, :] * gain[0:1, :], centred * inv, inv)
        nb[rows, :] = (gs[rows, :] + t).astype(bf16)

    loop(norm_one_back)
    gtok_save = local(nb, gtok_hbm, 14)
    gtok_save.start()
    for k in range(N):
        if k not in PROJ:
            for dz in (1, 2, 3):
                z_copy(k, dz).wait_send()
        for h in (0, 1):
            a_copy(k, h).wait_send()
            b_copy(k, h).wait_send()
        c_copy(k).wait_send()
    for dz in (1, 2, 3):
        z_copy(PROJ[0], dz).wait_send()
    for s in range(5):
        exchange(s).wait_send()
    gtok_save.wait()


def layer(
    dims, x, cot, wq, wo, wf, wp, b_qkv, b_out, b_fc, b_proj, gain, shift, embed, r_in, r_in_b, r_out,
    r_out_b, lengths, buckets,
):
    Z, Y, X, C = dims
    S, V, sds = pltpu.SemaphoreType.DMA, pltpu.VMEM, jax.ShapeDtypeStruct
    anys, vm, sm = (pl.BlockSpec(memory_space=s) for s in (pl.ANY, pltpu.VMEM, pltpu.SMEM))
    row = lambda t: t.reshape(1, -1)
    wide, wide32 = V((LEN, D), bf16), V((LEN, D), f32)
    return pl.pallas_call(
        functools.partial(layer_kernel, dims),
        out_shape=[
            sds((8, Z, Y, X, C, 2, 16, D), bf16), sds((4, Y, X, C, 2, 64, D), bf16),
            sds((LEN, D), bf16), sds((LEN, D), bf16),
            sds((16, 512), f32), sds((16, 512), f32), sds((16, 2 * D), f32), sds((16, D), f32),
        ],
        in_specs=[anys] * 6 + [vm] * 7 + [anys, vm, anys, vm, sm, sm],
        out_specs=[anys] * 4 + [vm] * 4,
        scratch_shapes=[
            V((8, 2, 16, D), bf16), wide, wide, wide, V((3, LEN, D), bf16), wide, wide,
            wide32, wide32, wide32, V((4, LEN, D), bf16),
            V((3, Z, Y, X, C, 2, 16, D), bf16), V((2, Y, X, C, 2, 64, D), bf16),
            V((LEN, 128), bf16), V((128, 128), bf16), V((128, D), bf16), V((128, D), bf16),
            V((2, LEN, 256), bf16), V((2, LEN, 256), bf16), V((256, 256), bf16), V((256, 256), bf16),
            V((128, LEN), bf16), V((128, LEN), bf16), V((128, LEN), f32), V((128, LEN), f32),
            V((LEN, 256), bf16), V((256, D), bf16), V((6, 16, 2 * D), f32), V((5, 16, 2 * D), f32),
            S((N, 3)), S((N, 3)), S((3,)), S((4,)), S((N, 2)), S((N, 2)), S((N, 2)), S((N, 2)),
            S((N,)), S((N,)), S((N,)), S((32,)), S((5,)), S((5,)),
        ],
        compiler_params=pltpu.CompilerParams(
            collective_id=0, has_side_effects=True, vmem_limit_bytes=62 << 20
        ),
    )(
        x, cot, *(w.reshape(2, 16, w.shape[1]) for w in (wq, wo, wf)), wp.reshape(2, 64, D),
        row(b_qkv), row(b_out), row(b_fc), row(b_proj), gain, shift, embed, r_in, row(r_in_b), r_out,
        row(r_out_b), lengths, buckets,
    )


def finish_kernel(
    out_in, gtok_in, hid, pre, grad_prefix, emb, r_in, out, gtok, g_embed, g_in, g_in_b, g_out, g_out_b, sems
):
    copies = [
        pltpu.make_async_copy(out_in, out, sems.at[0]), pltpu.make_async_copy(gtok_in, gtok, sems.at[1])
    ]
    for d in copies:
        d.start()
    g_out[...] = precise(hid[...].T, grad_prefix[...])
    g_out_b[...] = jnp.sum(grad_prefix[...], axis=0, keepdims=True)
    g_in[...] = precise(emb[...].T, pre[...])
    g_in_b[...] = jnp.sum(pre[...], axis=0, keepdims=True)
    g_embed[...] = precise(pre[...], r_in[...], NT)[0:PREFIX]
    for d in copies:
        d.wait()


def finish(out, gtok, hid, pre, grad_prefix, emb, r_in):
    anys, vm = (pl.BlockSpec(memory_space=s) for s in (pl.ANY, pltpu.VMEM))
    sds = jax.ShapeDtypeStruct
    o = pl.pallas_call(
        finish_kernel,
        out_shape=[
            sds(out.shape, bf16), sds(gtok.shape, bf16), sds((PREFIX, D), f32), sds((D, 512), f32),
            sds((1, 512), f32), sds((512, 2 * D), f32), sds((1, 2 * D), f32),
        ],
        in_specs=[anys, anys] + [vm] * 5,
        out_specs=[anys, anys] + [vm] * 5,
        scratch_shapes=[pltpu.SemaphoreType.DMA((2,))],
        compiler_params=pltpu.CompilerParams(vmem_limit_bytes=40 << 20),
    )(out, gtok, hid, pre, grad_prefix, emb, r_in)
    return (*o[:4], o[4].reshape(-1), o[5], o[6].reshape(-1))


def normalize(field, gain, shift):
    centred, inv = center(field)
    return centred * inv * gain + shift


def plain_heads(matrix):
    return matrix.reshape(matrix.shape[0], 16, 64).transpose(1, 0, 2)


def plain_visible(seg_lengths, bucket):
    places = jnp.arange(LEN, dtype=jnp.int32)
    segment = places // bucket
    within = places - segment * bucket
    extent = sum(jnp.where(segment == which, seg_lengths[which], 0) for which in range(4))
    same = segment[:, None] == segment[None, :]
    return same & (places[None, :] <= places[:, None]) & (within < extent)[None, :]


def plain_attend(q, k, v, allowed):
    mix = lambda spec, a, b: jnp.einsum(spec, a.astype(bf16), b.astype(bf16), preferred_element_type=f32)
    scores = jnp.where(allowed, mix("qd,kd->qk", q, k) * 0.125, NEG)
    return mix("qk,kd->qd", jax.nn.softmax(scores, axis=-1), v)


def plain_layer(
    tokens, cotangent, w_qkv, w_out, w_fc, w_proj, bias_qkv, bias_out, bias_fc, bias_proj,
    ln_gain, ln_shift, prefix_embed, reparam_in, reparam_in_bias, reparam_out, reparam_out_bias,
    lengths, buckets,
):
    full_qkv, full_out, full_fc, full_proj = (
        lax.all_gather(t, ("dp", "fsdp"), axis=0, tiled=True) for t in (w_qkv, w_out, w_fc, w_proj)
    )
    hidden = jnp.tanh(precise(prefix_embed, reparam_in) + reparam_in_bias)
    prefix_rows = (precise(hidden, reparam_out) + reparam_out_bias).astype(bf16)
    pk, pv = plain_heads(prefix_rows[:, :D]), plain_heads(prefix_rows[:, D:])
    inputs = tokens.astype(f32)
    norm_one = lambda field: normalize(field, ln_gain[0], ln_shift[0])
    norm_two = lambda field: normalize(field, ln_gain[1], ln_shift[1])
    normed, pull_one = jax.vjp(norm_one, inputs)
    joined = (dot(normed.astype(bf16), full_qkv) + bias_qkv.astype(f32)).astype(bf16)
    q, k, v = (plain_heads(joined[:, i * D : (i + 1) * D]) for i in range(3))
    allowed = jnp.concatenate([jnp.ones((LEN, PREFIX), bool), plain_visible(lengths[0], buckets[0])], 1)

    def one_head(parts):
        q, k, v, pk, pv, grad = parts
        run = lambda q, k, v: plain_attend(q, k, v, allowed)
        mixed, pull = jax.vjp(run, q.astype(f32), *(jnp.concatenate(t).astype(f32) for t in ((pk, k), (pv, v))))
        return mixed, pull(grad.astype(f32))

    heads = (q, k, v, pk, pv)
    mixed = lax.map(lambda parts: one_head((*parts, parts[0]))[0], heads)
    back = lambda t: t.transpose(1, 0, 2).reshape(-1, D)
    attended = back(mixed).astype(bf16)
    middle = inputs + (dot(attended, full_out) + bias_out.astype(f32))
    second, pull_two = jax.vjp(norm_two, middle)
    before = dot(second.astype(bf16), full_fc) + bias_fc.astype(f32)
    activated, pull_gelu = jax.vjp(lambda field: jax.nn.gelu(field, approximate=True), before)
    result = middle + (dot(activated.astype(bf16), full_proj) + bias_proj.astype(f32))
    grad_before = pull_gelu(dot(cotangent, full_proj, NT))[0].astype(bf16)
    grad_middle = cotangent.astype(f32) + pull_two(dot(grad_before, full_fc, NT))[0]
    grad_attended = dot(grad_middle.astype(bf16), full_out, NT).astype(bf16)
    dq, dk, dv = lax.map(lambda parts: one_head(parts)[1], (*heads, plain_heads(grad_attended)))
    grads = [back(t).astype(bf16) for t in (dq, dk[:, PREFIX:], dv[:, PREFIX:])]
    grad_prefix = jnp.concatenate([back(t[:, :PREFIX]) for t in (dk, dv)], 1)
    grad_prefix = lax.psum(grad_prefix, ("dp", "fsdp"))
    grad_normed = dot(jnp.concatenate(grads, 1), full_qkv, NT)
    grad_tokens = (grad_middle + pull_one(grad_normed)[0]).astype(bf16)
    grad_pre = precise(grad_prefix, reparam_out, NT) * (1.0 - hidden * hidden)
    return (
        result.astype(bf16), grad_tokens, precise(grad_pre, reparam_in, NT), precise(prefix_embed.T, grad_pre),
        jnp.sum(grad_pre, axis=0), precise(hidden.T, grad_prefix), jnp.sum(grad_prefix, axis=0),
    )


def on_device(dims, *args):
    if dims is None:
        return plain_layer(*args)
    _, _, out, gtok, hid, pre, grad_prefix, emb = layer(dims, *args)
    return finish(out, gtok, hid, pre, grad_prefix, emb, args[13])


def chip_dims(mesh):
    if dict(mesh.shape) == {"dp": 8, "fsdp": 4}:
        return (4, 2, 2, 2)
    return None


def solution(mesh):
    split, lone = P(("dp", "fsdp"), None), P()
    return jax.shard_map(
        functools.partial(on_device, chip_dims(mesh)),
        mesh=mesh,
        in_specs=(split,) * 6 + (lone,) * 11 + (split, P(("dp", "fsdp"))),
        out_specs=(split, split) + (lone,) * 5,
        check_vma=False,
    )
```

```python
import functools, math
import jax, jax.numpy as jnp
from jax import lax
from jax.experimental import pallas as pl
from jax.experimental.pallas import tpu as pltpu
from jax.sharding import PartitionSpec as P

f32, bf16 = jnp.float32, jnp.bfloat16
MESH = pl.DeviceIdType.MESH
A = slice(None)
D = 1024
LEN = 1024
PREFIX = 10
BQ = 256
NQ = LEN // BQ
NEG = -1e30
ROOT = math.sqrt(2.0 / math.pi)
HIGHEST = lax.Precision.HIGHEST
NT = (((1,), (1,)), ((), ()))
NN = (((1,), (0,)), ((), ()))
OUT = 4
FC = (5, 7, 9, 12)
PROJ = (6, 8, 10, 11)
SIDE = 12
N = 12
AHEAD = ((2,), (3, 4), (5, 6), (7, 8), (9, 10), (11,), (SIDE,))
HID, PRE, GPRE, EMB, GEMB = slice(0, 512), slice(512, D), slice(D, 3 * D), slice(3 * D, 4 * D), slice(4 * D, 5 * D)


def dot(a, b, dims=NN):
    return lax.dot_general(a, b, dims, preferred_element_type=f32)


def precise(a, b, dims=NN):
    return lax.dot_general(a, b, dims, precision=HIGHEST, preferred_element_type=f32)


def close(a, b):
    high, ahigh = b.astype(bf16), a.astype(bf16)
    low, alow = (b - high.astype(f32)).astype(bf16), (a - ahigh.astype(f32)).astype(bf16)
    t = dot(jnp.concatenate([ahigh, alow], axis=0), high, NT)
    return t[: a.shape[0]] + t[a.shape[0] :] + dot(ahigh, low, NT)


def lanes(rows):
    return lax.broadcasted_iota(jnp.int32, (rows, 128), 1)


def split_three(value):
    high = value.astype(bf16)
    rest = value - high.astype(f32)
    mid = rest.astype(bf16)
    return high.astype(f32), mid.astype(f32), rest - mid.astype(f32)


def extra(base, value):
    b = lanes(value.shape[0]) % 64
    high, mid, low = split_three(value)
    return jnp.where(b == 1, high, jnp.where(b == 2, mid, jnp.where(b == 3, low, base))).astype(bf16)


def query_flags(i, rows):
    b = lanes(rows) % 64
    return jnp.where((b == 0) | ((b >= 4) & (b < 8) & (b != 4 + i)), 1.0, 0.0)


def half(a, h):
    return jnp.where((lanes(a.shape[0]) < 64) == (h == 0), a, jnp.zeros_like(a))


def causal():
    shape = (BQ, BQ)
    return lax.broadcasted_iota(jnp.int32, shape, 1) <= lax.broadcasted_iota(jnp.int32, shape, 0)


def forward_pair(q, k, v, pk, pv, kx, pkx, o_ref, qx_ref, kext, vext, pkext, pvext):
    ln, lp = lanes(LEN), lanes(128)
    for h in (0, 1):
        rows = slice(h * 128, (h + 1) * 128)
        kext[h, :, :128] = half(k[...], h)
        kext[h, :, 128:] = half(kx[...], h)
        vext[h, :, :128] = half(v[...], h)
        vext[h, :, 128:] = jnp.where((ln < 64) == (h == 0), 1.0, 0.0).astype(bf16)
        pkext[rows, :128] = half(pk[...], h)
        pkext[rows, 128:] = half(pkx[...], h)
        pvext[rows, :128] = half(pv[...], h)
        pvext[rows, 128:] = jnp.where((lp < 64) == (h == 0), 1.0, 0.0).astype(bf16)
    for i in range(NQ):
        rows, n = pl.ds(i * BQ, BQ), (i + 1) * BQ
        flags = query_flags(i, BQ)
        qe = jnp.concatenate([q[rows, :], flags.astype(bf16)], axis=1)
        before = dot(qe, pkext[...], NT)
        acc, tops, parts = None, [], []
        for h in (0, 1):
            s = dot(qe, kext[h, :n, :], NT)
            near = jnp.where(causal(), s[:, n - BQ :], NEG)
            first = before[:, h * 128 : (h + 1) * 128]
            m = jnp.maximum(
                jnp.max(near, axis=1, keepdims=True), jnp.max(first, axis=1, keepdims=True)
            )
            if i:
                m = jnp.maximum(m, jnp.max(s[:, : n - BQ], axis=1, keepdims=True))
            a = dot(jnp.exp(near - m).astype(bf16), vext[h, n - BQ : n, :])
            if i:
                a = a + dot(jnp.exp(s[:, : n - BQ] - m).astype(bf16), vext[h, : n - BQ, :])
            parts.append(jnp.exp(first - m).astype(bf16))
            tops.append(m)
            acc = a if acc is None else acc + a
        acc = acc + dot(jnp.concatenate(parts, axis=1), pvext[...])
        total = acc[:, 128:]
        o_ref[rows, :] = (acc[:, :128] / total).astype(bf16)
        lse = jnp.where(lanes(BQ) < 64, tops[0], tops[1]) + jnp.log(total)
        qx_ref[rows, :] = extra(flags, -lse)


def backward_pair(
    q, k, v, kx, qx, do, dx, dsp, pkd, dq_ref, dk_ref, dv_ref, kext, vext, qt, dot_t, dkt, dvt
):
    b = lanes(LEN) % 64
    ones = jnp.where((b >= 1) & (b < 4), 1.0, 0.0).astype(bf16)
    for h in (0, 1):
        kext[h, :, :128] = half(k[...], h)
        kext[h, :, 128:] = half(kx[...], h)
        vext[h, :, :128] = half(v[...], h)
        vext[h, :, 128:] = half(ones, h)
    qt[...] = q[...].T
    dot_t[...] = do[...].T
    for i in reversed(range(NQ)):
        rows, n = pl.ds(i * BQ, BQ), (i + 1) * BQ
        qe = jnp.concatenate([q[rows, :], qx[rows, :]], axis=1)
        de = jnp.concatenate([do[rows, :], dx[rows, :]], axis=1)
        dq = dot(dsp[rows, :], pkd[...])
        for h in (0, 1):
            hr = slice(h * 64, (h + 1) * 64)
            qth, dth = qt[hr, i * BQ : (i + 1) * BQ], dot_t[hr, i * BQ : (i + 1) * BQ]
            s = dot(qe, kext[h, :n, :], NT)
            g = dot(de, vext[h, :n, :], NT)
            p = jnp.exp(s)
            near = jnp.where(causal(), p[:, n - BQ :], 0.0)
            p = near if i == 0 else jnp.concatenate([p[:, : n - BQ], near], axis=1)
            ds = (p * g).astype(bf16)
            p = p.astype(bf16)
            dq = dq + dot(ds, kext[h, :n, :128])
            if i == NQ - 1:
                dkt[hr, :n] = dot(qth, ds)
                dvt[hr, :n] = dot(dth, p)
            else:
                dkt[hr, :n] += dot(qth, ds)
                dvt[hr, :n] += dot(dth, p)
        dq_ref[rows, :] = (dq * 0.125).astype(bf16)
    dk_ref[...] = dkt[...].T.astype(bf16)
    dv_ref[...] = dvt[...].T.astype(bf16)


def block(index, size=256):
    return pl.ds(pl.multiple_of(index * size, size), size)


def loop(body, count=4):
    lax.fori_loop(0, count, lambda r, _: (body(r), 0)[1], 0)


def unrolled(body, count=4):
    for r in range(count):
        body(r)


def center(field):
    mean = jnp.mean(field, axis=-1, keepdims=True)
    centred = field - mean
    return centred, lax.rsqrt(jnp.mean(centred * centred, axis=-1, keepdims=True) + 1e-05)


def norm_back(grad, normed, inv):
    down = grad - jnp.mean(grad, axis=-1, keepdims=True)
    return inv * (down - normed * jnp.mean(grad * normed, axis=-1, keepdims=True))


def key_columns(kx, lengths, buckets):
    full = buckets[0] == LEN
    b = lanes(256) % 64
    for r in range(4):
        place = lax.broadcasted_iota(jnp.int32, (256, 128), 0)
        within = jnp.where(full, place + r * 256, place)
        extent = jnp.where(full, lengths[0, 0], lengths[0, r])
        e = jnp.where((b == 0) & (within >= extent), NEG, 0.0)
        e = jnp.where((b >= 1) & (b < 4), 1.0, e)
        e = jnp.where((b == 4 + r) & jnp.logical_not(full), NEG, e)
        kx[r * 256 : (r + 1) * 256, :] = e.astype(bf16)


def prefix_columns():
    r, b = lax.broadcasted_iota(jnp.int32, (128, 128), 0), lanes(128) % 64
    return jnp.where((b == 0) & (r >= PREFIX), NEG, jnp.where((b >= 1) & (b < 4), 1.0, 0.0)).astype(bf16)


def head_rows(shape, per_head):
    r = lax.broadcasted_iota(jnp.int32, shape, 0) // 16
    return r == lax.broadcasted_iota(jnp.int32, shape, 1) // per_head


def layer_kernel(
    dims, x_hbm, cot_hbm, wq, wo, wf, wp, b_qkv, b_out, b_fc, b_proj, gain, shift, embed, r_in, r_in_b,
    r_out, r_out_b, lengths, buckets,
    ga, gp, out_hbm, gtok_hbm, small,
    shq, sh, shp, bias, xb, nb, ob, qkv, qx, dob, gs, middle, acc, big, WQ, W, WP, kx, pkx, pk, pv, kext, vext, pkext, pvext,
    qt, dot_t, dkt, dvt, dsp, pkd, total, came,
    zs, zr, zps, zpr, as_, ar, bs, br, cs, cr, ls, loc, ts, tr,
):
    Z, Y, X, C = dims
    dp, fs = lax.axis_index("dp"), lax.axis_index("fsdp")
    z, y, x, c = dp // Y, dp % Y, fs // C, fs % C
    zid = lambda dz: (lax.rem(z + dz, Z) * Y + y, fs)
    yid, xid, cid = (z * Y + (1 - y), fs), (dp, (1 - x) * C + c), (dp, x * C + (1 - c))

    def remote(s, d, ss, rs, dev):
        return pltpu.make_async_remote_copy(
            src_ref=s, dst_ref=d, send_sem=ss, recv_sem=rs, device_id=dev, device_id_type=MESH
        )

    def place(k, *ix):
        if k < OUT:
            return WQ.at[(k, *ix)]
        if k in PROJ:
            return gp.at[(PROJ.index(k), *ix[1:])]
        return ga.at[(0 if k == OUT else 1 + FC.index(k), *ix)]

    def own(k):
        if k < OUT:
            return shq.at[k], place(k, z, y, x, c)
        if k in PROJ:
            return shp, place(k, z, y, x, c)
        return sh.at[0 if k == OUT else 1 + FC.index(k)], place(k, z, y, x, c)

    def z_copy(k, dz):
        if k in PROJ:
            return remote(*own(k), zps.at[dz - 1], zpr.at[PROJ.index(k)], zid(dz))
        s, d = own(k)
        if k == SIDE:
            s = d = place(k, z, A, A, c)
        return remote(s, d, zs.at[k, dz - 1], zr.at[k, dz - 1], zid(dz))

    def a_copy(k, h):
        first = (h == 0) != (k == SIDE)
        s = place(k, z if k == SIDE else A, y, x, c, h)
        return remote(s, s, as_.at[k, h], ar.at[k, h], yid if first else xid)

    def b_copy(k, h):
        first = (h == 0) != (k == SIDE)
        ix = (A, x) if first else (y, A)
        s = place(k, z if k == SIDE else A, *ix, c, h)
        return remote(s, s, bs.at[k, h], br.at[k, h], xid if first else yid)

    def c_copy(k):
        s = place(k, A, A, A, c)
        return remote(s, s, cs.at[k], cr.at[k], cid)

    def own_copy(k):
        return pltpu.make_async_copy(*own(k), ls.at[k])

    def stage_z(k):
        def go():
            if k != SIDE:
                own_copy(k).start()
            for dz in (2, 1, 3):
                z_copy(k, dz).start()

        if k == SIDE:
            for h in (0, 1):
                b_copy(k, h).wait_recv()
        if k in PROJ:
            pl.when(z == PROJ.index(k))(go)
        else:
            go()

    def stage_a(k):
        if k in PROJ:
            j = PROJ.index(k)
            pl.when(z == j)(lambda: own_copy(k).wait())
            pl.when(z != j)(lambda: z_copy(k, 1).wait_recv())
        else:
            own_copy(k).wait()
            for dz in (1, 2, 3) if k != SIDE else ():
                z_copy(k, dz).wait_recv()
        for h in (0, 1):
            a_copy(k, h).start()

    def stage_b(k):
        for h in (0, 1):
            a_copy(k, h).wait_recv()
        for h in (0, 1):
            b_copy(k, h).start()

    def stage_c(k):
        if k == SIDE:
            for dz in (1, 2, 3):
                z_copy(k, dz).wait_recv()
        else:
            for h in (0, 1):
                b_copy(k, h).wait_recv()
        c_copy(k).start()

    def pump(t):
        for k in AHEAD[t] if t < len(AHEAD) else ():
            stage_z(k)
        for k in (t,) if t < 2 else (2, 3) if t == 2 else (t + 1,):
            if k < N:
                stage_a(k)
        if 0 <= t - 1 < N:
            stage_b(t - 1)
        if 0 <= t - 2 < N:
            stage_c(t - 2)
        if 0 <= t - 3 < N:
            c_copy(t - 3).wait_recv()

    def local(s, d, i):
        return pltpu.make_async_copy(s, d, loc.at[i])

    slots = {OUT: 0, FC[0]: 1, FC[1]: 0, FC[2]: 1, FC[3]: 0}

    def load(k, slot=None):
        if k in PROJ:
            return local(gp.at[PROJ.index(k)], WP.at[PROJ.index(k) % 2], 20 + k)
        return local(ga.at[0 if k == OUT else 1 + FC.index(k)], W.at[slots[k] if slot is None else slot], 20 + k)

    shards = [
        local(wq.at[:, :, pl.ds(j * D + g * 256, 256)], shq.at[g, :, :, pl.ds(j * 256, 256)], 33 + 3 * g + j)
        for g in range(4) for j in range(3)
    ]
    shards += [local(wf.at[:, :, pl.ds(3 * D, D)], sh.at[4], 4), local(wo, sh.at[0], 0)]
    shards += [local(wf.at[:, :, pl.ds(j * D, D)], sh.at[1 + j], 1 + j) for j in range(3)]
    shards += [local(wp, shp, 15)]
    for d in shards:
        d.start()
    rin = local(r_in, middle.at[:, pl.ds(0, 512)], 8)
    rout = [local(r_out.at[:, pl.ds(j * D, D)], acc.at[pl.ds(j * 512, 512), :], 9 + j) for j in (0, 1)]
    xload = local(x_hbm, xb, 11)
    xload.start()
    barrier = pltpu.get_barrier_semaphore()
    for d in [zid(dz) for dz in range(1, Z)] + [yid, xid, cid]:
        pl.semaphore_signal(barrier, inc=1, device_id=d, device_id_type=MESH)
    pl.semaphore_wait(barrier, Z + 2)
    for d in shards:
        d.wait()
    own_copy(SIDE).start()
    stage_z(0)
    stage_a(SIDE)
    stage_z(1)
    for d in [rin] + rout:
        d.start()
    xload.wait()

    def norm_one(r):
        rows = block(r)
        centred, inv = center(xb[rows, :].astype(f32))
        nb[rows, :] = (centred * inv * gain[0:1, :] + shift[0:1, :]).astype(bf16)

    loop(norm_one)
    pump(0)
    stage_b(SIDE)
    for j in range(3):
        bias[j : j + 1, :] = b_qkv[pl.ds(j * D, D)].reshape(1, D).astype(f32)
    small[...] = jnp.zeros_like(small)
    small[0:PREFIX, EMB] = embed[...]
    rin.wait()
    hid = jnp.tanh(precise(small[:, EMB], middle[:, 0:512]) + r_in_b[...].reshape(1, 512))
    small[:, HID] = hid
    pump(1)
    live = lax.broadcasted_iota(jnp.int32, (16, D), 0) < PREFIX
    for j, dest in ((0, pk), (1, pv)):
        rout[j].wait()
        t = precise(hid, acc[j * 512 : (j + 1) * 512, :])
        t = jnp.where(live, t + r_out_b[pl.ds(j * D, D)].reshape(1, D), 0.0)
        dest[...] = jnp.zeros_like(dest)
        dest[0:16, :] = t.astype(bf16)
    key_columns(kx, lengths, buckets)
    pkx[...] = prefix_columns()
    pump(2)
    pump(3)

    def project(g):
        cols = block(g)
        for j in range(3):
            t = dot(nb[...], WQ[g, ..., j * 256 : (j + 1) * 256].reshape(D, 256))
            t = (t + bias[j : j + 1, cols]).astype(bf16)
            qkv[j, :, cols] = t * jnp.asarray(0.125, bf16) if j == 0 else t

    def attend(p):
        cols = block(p, 128)
        pl.when(p % 2 == 0)(lambda: project(p // 2))
        forward_pair(
            *(qkv.at[k, :, cols] for k in range(3)), pk.at[:, cols], pv.at[:, cols], kx, pkx,
            ob.at[:, cols], qx.at[:, cols], kext, vext, pkext, pvext,
        )
        for at, t in ((0, 4), (2, 5), (4, 6), (6, 7)):
            pl.when(p == at)(functools.partial(pump, t))

    loop(attend, 8)
    load(OUT).start()
    load(OUT).wait()
    for cb in range(4):
        cols = slice(cb * 256, (cb + 1) * 256)
        t = dot(ob[...], W[0, ..., cols].reshape(D, 256))
        middle[:, cols] = xb[:, cols].astype(f32) + (t + b_out[pl.ds(cb * 256, 256)].reshape(1, 256).astype(f32))
    cotload = local(cot_hbm, xb, 12)
    cotload.start()
    pump(8)
    load(FC[0]).start()

    def norm_two(r):
        rows = block(r)
        m = middle[rows, :]
        centred, inv = center(m)
        nb[rows, :] = (centred * inv * gain[1:2, :] + shift[1:2, :]).astype(bf16)
        acc[rows, :] = m + b_proj[...].reshape(1, D).astype(f32)
        gs[rows, :] = jnp.zeros_like(m)

    loop(norm_two)
    def hidden_part(f):
        k, r = FC[f], f % 2
        load(k).wait()
        for cb in range(4):
            cols = slice(cb * 256, (cb + 1) * 256)
            u = dot(nb[...], W[slots[k], ..., cols].reshape(D, 256))
            u = u + b_fc[pl.ds(f * D + cb * 256, 256)].reshape(1, 256).astype(f32)
            sq = u * u
            t = jnp.tanh(u * (ROOT + (ROOT * 0.044715) * sq))
            plus = 0.5 + 0.5 * t
            big[r, :, cols] = (u * plus).astype(bf16)
            slope = plus + (0.5 * u) * (1.0 - t * t) * (ROOT + (3 * ROOT * 0.044715) * sq)
            big[2 + r, :, cols] = slope.astype(bf16)

    def out_part(f):
        r = f % 2
        load(PROJ[f]).wait()
        for cb in range(4):
            cols = slice(cb * 256, (cb + 1) * 256)
            acc[:, cols] += dot(big[r], WP[r, ..., cols].reshape(D, 256))
            g = dot(xb[...], WP[r, cb // 2, cb % 2].reshape(256, D), NT)
            big[2 + r, :, cols] = (g * big[2 + r, :, cols].astype(f32)).astype(bf16)

    def second_part(f):
        for cb in range(4):
            cols = slice(cb * 256, (cb + 1) * 256)
            gs[:, cols] += dot(big[2 + f % 2], W[slots[FC[f]], cb].reshape(256, D), NT)

    hidden_part(0)
    pump(9)
    load(PROJ[0]).start()
    cotload.wait()
    out_part(0)
    pump(10)
    load(FC[1]).start()
    second_part(0)
    hidden_part(1)
    pump(11)
    load(PROJ[1]).start()
    out_part(1)
    pump(12)
    load(FC[2]).start()
    second_part(1)
    hidden_part(2)
    stage_c(SIDE)
    pump(13)
    load(PROJ[2]).start()
    out_part(2)
    c_copy(SIDE).wait_recv()
    load(FC[3]).start()
    second_part(2)
    load(OUT, 1).start()
    hidden_part(3)
    pump(14)
    load(PROJ[3]).start()
    out_part(3)
    second_part(3)

    def norm_two_back(r):
        rows = block(r)
        centred, inv = center(middle[rows, :])
        t = norm_back(gs[rows, :] * gain[1:2, :], centred * inv, inv)
        t = xb[rows, :].astype(f32) + t
        gs[rows, :] = t
        nb[rows, :] = t.astype(bf16)
        WP[0, r // 2, r % 2] = acc[rows, :].astype(bf16).reshape(C, 2, 64, D)

    loop(norm_two_back)
    out_save = local(WP.at[0], out_hbm, 13)
    out_save.start()
    xload = local(x_hbm, xb, 11)
    xload.start()
    for d in [rin] + rout:
        d.start()
    load(OUT, 1).wait()
    for cb in range(4):
        dob[:, cb * 256 : (cb + 1) * 256] = dot(nb[...], W[1, cb].reshape(256, D), NT).astype(bf16)

    gi = lax.broadcasted_iota(jnp.int32, (128, 128), 0) // 64
    group = jnp.where(gi == lanes(128) // 64, 1.0, 0.0).astype(bf16)

    def delta(p):
        cols = block(p, 128)
        prod = dob[:, cols].astype(f32) * ob[:, cols].astype(f32)
        high = prod.astype(bf16)
        low = (prod - high.astype(f32)).astype(bf16)
        big[p // 2, :, pl.ds(pl.multiple_of(768 + (p % 2) * 128, 128), 128)] = extra(
            0.0, -(dot(high, group) + dot(low, group))
        )

    loop(delta, 8)
    same = head_rows((256, D), 64)
    spread = [jnp.concatenate([t[0:16, :]] * 16, axis=0) for t in (pk, pv)]
    spread = [jnp.where(same, t, jnp.zeros_like(t)) for t in spread]
    pkd[...] = spread[0]
    lane = lax.broadcasted_iota(jnp.int32, (256, D), 1) % 64
    unit = jnp.where(same & (lane >= 1) & (lane < 4), 1.0, 0.0)
    dead = lax.broadcasted_iota(jnp.int32, (256, D), 0) % 16 >= PREFIX
    mask = jnp.where(same & (lane == 0) & dead, NEG, unit).astype(bf16)
    unit = unit.astype(bf16)
    prob = jnp.exp(dot(qkv[0], spread[0], NT) + dot(qx[...], mask, NT))
    deltas = jnp.concatenate([big[g, :, 768:] for g in range(4)], axis=1)
    grad = dot(dob[...], spread[1], NT) + dot(deltas, unit, NT)
    dsp[...] = (prob * grad).astype(bf16)
    for j, (left, right) in enumerate(((dsp[...], qkv[0]), (prob.astype(bf16), dob[...]))):
        t = jnp.where(same, dot(left.T, right), 0.0)
        total[0, :, j * D : (j + 1) * D] = jnp.sum(t.reshape(16, 16, D), axis=0)

    partners = [cid, xid, yid, ((z + 1 - 2 * (z % 2)) * Y + y, fs), zid(2)]

    def exchange(s):
        return remote(total.at[s], came.at[s], ts.at[s], tr.at[s], partners[s])

    def step(s):
        if s > 0:
            exchange(s - 1).wait_recv()
            total[s] = total[s - 1] + came[s - 1]
        if s < 5:
            exchange(s).start()

    out_save.wait()

    def attend_back(p):
        for s in range(6):
            pl.when(p == s)(functools.partial(step, s))
        cols = block(p, 128)
        part = lambda j: big.at[p // 2, :, pl.ds(pl.multiple_of(j * 256 + (p % 2) * 128, 128), 128)]
        backward_pair(
            *(qkv.at[k, :, cols] for k in range(3)), kx, qx.at[:, cols], dob.at[:, cols],
            part(3), dsp, pkd.at[:, cols], part(0), part(1), part(2),
            kext, vext, qt, dot_t, dkt, dvt,
        )

    loop(attend_back, 8)
    for d in rout:
        d.wait()
    rin.wait()
    small[:, GPRE] = total[5]
    hid = small[:, HID]
    t = sum(close(total[5, :, j * D : (j + 1) * D], acc[j * 512 : (j + 1) * 512, :]) for j in (0, 1))
    t = t * (1.0 - hid * hid)
    small[:, PRE] = t
    small[:, GEMB] = close(t, middle[:, 0:512])
    for cb in range(4):
        cols = slice(cb * 256, (cb + 1) * 256)
        acc[:, cols] = sum(dot(big[g, :, :768], WQ[g, cb].reshape(256, 768), NT) for g in range(4))
    xload.wait()

    def norm_one_back(r):
        rows = block(r)
        centred, inv = center(xb[rows, :].astype(f32))
        t = norm_back(acc[rows, :] * gain[0:1, :], centred * inv, inv)
        nb[rows, :] = (gs[rows, :] + t).astype(bf16)

    loop(norm_one_back)
    gtok_save = local(nb, gtok_hbm, 14)
    gtok_save.start()
    for k in range(N + 1):
        if k not in PROJ:
            for dz in (1, 2, 3):
                z_copy(k, dz).wait_send()
        for h in (0, 1):
            a_copy(k, h).wait_send()
            b_copy(k, h).wait_send()
        c_copy(k).wait_send()
    for dz in (1, 2, 3):
        z_copy(PROJ[0], dz).wait_send()
    for s in range(5):
        exchange(s).wait_send()
    gtok_save.wait()


def layer(
    dims, x, cot, wq, wo, wf, wp, b_qkv, b_out, b_fc, b_proj, gain, shift, embed, r_in, r_in_b, r_out,
    r_out_b, lengths, buckets,
):
    Z, Y, X, C = dims
    S, V, sds = pltpu.SemaphoreType.DMA, pltpu.VMEM, jax.ShapeDtypeStruct
    anys, vm, sm = (pl.BlockSpec(memory_space=s) for s in (pl.ANY, pltpu.VMEM, pltpu.SMEM))
    wide, wide32 = V((LEN, D), bf16), V((LEN, D), f32)
    return pl.pallas_call(
        functools.partial(layer_kernel, dims),
        out_shape=[
            sds((5, Z, Y, X, C, 2, 16, D), bf16), sds((4, Y, X, C, 2, 64, D), bf16),
            sds((Y, X, C, 2, 64, D), bf16), sds((LEN, D), bf16),
            sds((16, 5 * D), f32),
        ],
        in_specs=[anys] * 6 + [vm] * 7 + [anys, vm, anys, vm, sm, sm],
        out_specs=[anys] * 4 + [vm],
        scratch_shapes=[
            V((4, 2, 16, 768), bf16), V((5, 2, 16, D), bf16), V((2, 64, D), bf16), V((8, D), f32), wide, wide, wide, V((3, LEN, D), bf16), wide, wide,
            wide32, wide32, wide32, V((4, LEN, D), bf16),
            V((4, Z, Y, X, C, 2, 16, 768), bf16), V((2, Z, Y, X, C, 2, 16, D), bf16), V((2, Y, X, C, 2, 64, D), bf16),
            V((LEN, 128), bf16), V((128, 128), bf16), V((128, D), bf16), V((128, D), bf16),
            V((2, LEN, 256), bf16), V((2, LEN, 256), bf16), V((256, 256), bf16), V((256, 256), bf16),
            V((128, LEN), bf16), V((128, LEN), bf16), V((128, LEN), f32), V((128, LEN), f32),
            V((LEN, 256), bf16), V((256, D), bf16), V((6, 16, 2 * D), f32), V((5, 16, 2 * D), f32),
            S((N + 1, 3)), S((N + 1, 3)), S((3,)), S((4,)), *[S((N + 1, 2))] * 4, *[S((N + 1,))] * 3, S((45,)),
            S((5,)), S((5,)),
        ],
        compiler_params=pltpu.CompilerParams(
            collective_id=0, has_side_effects=True, vmem_limit_bytes=62 << 20
        ),
    )(
        x, cot, *(w.reshape(2, 16, w.shape[1]) for w in (wq, wo, wf)), wp.reshape(2, 64, D),
        b_qkv, b_out, b_fc, b_proj, gain, shift, embed, r_in, r_in_b, r_out, r_out_b, lengths, buckets,
    )


def three(value):
    return [t.astype(bf16) for t in split_three(value)]


def outer(left, right):
    a, b, c = three(left)
    p, q, r = three(right)
    pairs = ((a, p), (a, q), (b, p), (a, r), (c, p), (b, q))
    left, right = (jnp.concatenate(t, axis=0) for t in zip(*pairs))
    return lambda rows: lax.dot_general(
        left[:, rows], right, (((0,), (0,)), ((), ())), preferred_element_type=f32
    )


def finish_kernel(out_in, gtok_in, small, out, gtok, g_embed, g_in, g_in_b, g_out, g_out_b, big, mid, first, second, sems):
    copies = []

    def copy(s, d):
        copies.append(pltpu.make_async_copy(s, d, sems.at[len(copies)]))
        copies[-1].start()

    copy(out_in, first)
    copy(gtok_in, second)
    make = outer(small[:, HID], small[:, GPRE])
    for r in range(4):
        rows = slice(r * 128, (r + 1) * 128)
        big[rows, :] = make(rows)
        copy(big.at[rows, :], g_out.at[rows, :])
    for t, d in enumerate(((first, out), (second, gtok))):
        copies[t].wait()
        copy(*d)
    make = outer(small[:, EMB], small[:, PRE])
    for r in range(2):
        rows = slice(r * 512, (r + 1) * 512)
        mid[rows, :] = make(rows)
        copy(mid.at[rows, :], g_in.at[rows, :])
    g_out_b[...] = jnp.sum(small[:, GPRE], axis=0)
    g_in_b[...] = jnp.sum(small[:, PRE], axis=0)
    g_embed[...] = small[0:PREFIX, GEMB]
    for d in copies[2:]:
        d.wait()


def finish(out, gtok, small):
    anys, vm = (pl.BlockSpec(memory_space=s) for s in (pl.ANY, pltpu.VMEM))
    sds = jax.ShapeDtypeStruct
    return pl.pallas_call(
        finish_kernel,
        out_shape=[
            sds(out.shape, bf16), sds(gtok.shape, bf16), sds((PREFIX, D), f32), sds((D, 512), f32),
            sds((512,), f32), sds((512, 2 * D), f32), sds((2 * D,), f32),
        ],
        in_specs=[anys, anys, vm],
        out_specs=[anys, anys, vm, anys, vm, anys, vm],
        scratch_shapes=[
            pltpu.VMEM((512, 2 * D), f32), pltpu.VMEM((D, 512), f32),
            pltpu.VMEM(out.shape, bf16), pltpu.VMEM(gtok.shape, bf16), pltpu.SemaphoreType.DMA((10,))
        ],
        compiler_params=pltpu.CompilerParams(vmem_limit_bytes=62 << 20),
    )(out, gtok, small)


def normalize(field, gain, shift):
    centred, inv = center(field)
    return centred * inv * gain + shift


def plain_heads(matrix):
    return matrix.reshape(matrix.shape[0], 16, 64).transpose(1, 0, 2)


def plain_visible(seg_lengths, bucket):
    places = jnp.arange(LEN, dtype=jnp.int32)
    segment = places // bucket
    within = places - segment * bucket
    extent = sum(jnp.where(segment == which, seg_lengths[which], 0) for which in range(4))
    same = segment[:, None] == segment[None, :]
    return same & (places[None, :] <= places[:, None]) & (within < extent)[None, :]


def plain_attend(q, k, v, allowed):
    mix = lambda spec, a, b: jnp.einsum(spec, a.astype(bf16), b.astype(bf16), preferred_element_type=f32)
    scores = jnp.where(allowed, mix("qd,kd->qk", q, k) * 0.125, NEG)
    return mix("qk,kd->qd", jax.nn.softmax(scores, axis=-1), v)


def plain_layer(
    tokens, cotangent, w_qkv, w_out, w_fc, w_proj, bias_qkv, bias_out, bias_fc, bias_proj,
    ln_gain, ln_shift, prefix_embed, reparam_in, reparam_in_bias, reparam_out, reparam_out_bias,
    lengths, buckets,
):
    full_qkv, full_out, full_fc, full_proj = (
        lax.all_gather(t, ("dp", "fsdp"), axis=0, tiled=True) for t in (w_qkv, w_out, w_fc, w_proj)
    )
    hidden = jnp.tanh(precise(prefix_embed, reparam_in) + reparam_in_bias)
    prefix_rows = (precise(hidden, reparam_out) + reparam_out_bias).astype(bf16)
    pk, pv = plain_heads(prefix_rows[:, :D]), plain_heads(prefix_rows[:, D:])
    inputs = tokens.astype(f32)
    norm_one = lambda field: normalize(field, ln_gain[0], ln_shift[0])
    norm_two = lambda field: normalize(field, ln_gain[1], ln_shift[1])
    normed, pull_one = jax.vjp(norm_one, inputs)
    joined = (dot(normed.astype(bf16), full_qkv) + bias_qkv.astype(f32)).astype(bf16)
    q, k, v = (plain_heads(joined[:, i * D : (i + 1) * D]) for i in range(3))
    allowed = jnp.concatenate([jnp.ones((LEN, PREFIX), bool), plain_visible(lengths[0], buckets[0])], 1)

    def one_head(parts):
        q, k, v, pk, pv, grad = parts
        run = lambda q, k, v: plain_attend(q, k, v, allowed)
        mixed, pull = jax.vjp(run, q.astype(f32), *(jnp.concatenate(t).astype(f32) for t in ((pk, k), (pv, v))))
        return mixed, pull(grad.astype(f32))

    heads = (q, k, v, pk, pv)
    mixed = lax.map(lambda parts: one_head((*parts, parts[0]))[0], heads)
    back = lambda t: t.transpose(1, 0, 2).reshape(-1, D)
    attended = back(mixed).astype(bf16)
    middle = inputs + (dot(attended, full_out) + bias_out.astype(f32))
    second, pull_two = jax.vjp(norm_two, middle)
    before = dot(second.astype(bf16), full_fc) + bias_fc.astype(f32)
    activated, pull_gelu = jax.vjp(lambda field: jax.nn.gelu(field, approximate=True), before)
    result = middle + (dot(activated.astype(bf16), full_proj) + bias_proj.astype(f32))
    grad_before = pull_gelu(dot(cotangent, full_proj, NT))[0].astype(bf16)
    grad_middle = cotangent.astype(f32) + pull_two(dot(grad_before, full_fc, NT))[0]
    grad_attended = dot(grad_middle.astype(bf16), full_out, NT).astype(bf16)
    dq, dk, dv = lax.map(lambda parts: one_head(parts)[1], (*heads, plain_heads(grad_attended)))
    grads = [back(t).astype(bf16) for t in (dq, dk[:, PREFIX:], dv[:, PREFIX:])]
    grad_prefix = jnp.concatenate([back(t[:, :PREFIX]) for t in (dk, dv)], 1)
    grad_prefix = lax.psum(grad_prefix, ("dp", "fsdp"))
    grad_normed = dot(jnp.concatenate(grads, 1), full_qkv, NT)
    grad_tokens = (grad_middle + pull_one(grad_normed)[0]).astype(bf16)
    grad_pre = precise(grad_prefix, reparam_out, NT) * (1.0 - hidden * hidden)
    return (
        result.astype(bf16), grad_tokens, precise(grad_pre, reparam_in, NT), precise(prefix_embed.T, grad_pre),
        jnp.sum(grad_pre, axis=0), precise(hidden.T, grad_prefix), jnp.sum(grad_prefix, axis=0),
    )


def on_device(dims, *args):
    if dims is None:
        return plain_layer(*args)
    _, _, out, gtok, small = layer(dims, *args)
    return tuple(finish(out.reshape(gtok.shape), gtok, small))


def chip_dims(mesh):
    if dict(mesh.shape) == {"dp": 8, "fsdp": 4}:
        return (4, 2, 2, 2)
    return None


def solution(mesh):
    split, lone = P(("dp", "fsdp"), None), P()
    return jax.shard_map(
        functools.partial(on_device, chip_dims(mesh)),
        mesh=mesh,
        in_specs=(split,) * 6 + (lone,) * 11 + (split, P(("dp", "fsdp"))),
        out_specs=(split, split) + (lone,) * 5,
        check_vma=False,
    )
```

```python
import functools, math
import jax, jax.numpy as jnp
from jax import lax
from jax.experimental import pallas as pl
from jax.experimental.pallas import tpu as pltpu
from jax.sharding import PartitionSpec as P

f32, bf16 = jnp.float32, jnp.bfloat16
MESH = pl.DeviceIdType.MESH
A = slice(None)
D = 1024
LEN = 1024
PREFIX = 10
BQ = 256
NQ = LEN // BQ
NEG = -1e30
ROOT = math.sqrt(2.0 / math.pi)
HIGHEST = lax.Precision.HIGHEST
NT = (((1,), (1,)), ((), ()))
NN = (((1,), (0,)), ((), ()))
OUT = 4
FC = (5, 7, 9, 12)
PROJ = (6, 8, 10, 11)
SIDE = 12
N = 12
AHEAD = ((2,), (3, 4), (5, 6), (7, 8), (9, 10), (11,), (SIDE,))
HID, PRE, GPRE, EMB, GEMB = slice(0, 512), slice(512, D), slice(D, 3 * D), slice(3 * D, 4 * D), slice(4 * D, 5 * D)


def dot(a, b, dims=NN):
    return lax.dot_general(a, b, dims, preferred_element_type=f32)


def precise(a, b, dims=NN):
    return lax.dot_general(a, b, dims, precision=HIGHEST, preferred_element_type=f32)


def close(a, b):
    high = a.astype(bf16)
    low = (a - high.astype(f32)).astype(bf16)
    t = dot(jnp.concatenate([high, low], axis=0), b.astype(bf16), NT)
    return t[: a.shape[0]] + t[a.shape[0] :]


def lanes(rows):
    return lax.broadcasted_iota(jnp.int32, (rows, 128), 1)


def split_three(value):
    high = value.astype(bf16)
    rest = value - high.astype(f32)
    mid = rest.astype(bf16)
    return high.astype(f32), mid.astype(f32), rest - mid.astype(f32)


def extra(base, value):
    b = lanes(value.shape[0]) % 64
    high, mid, low = split_three(value)
    return jnp.where(b == 1, high, jnp.where(b == 2, mid, jnp.where(b == 3, low, base))).astype(bf16)


def query_flags(i, rows):
    b = lanes(rows) % 64
    return jnp.where((b == 0) | ((b >= 4) & (b < 8) & (b != 4 + i)), 1.0, 0.0)


def half(a, h):
    return jnp.where((lanes(a.shape[0]) < 64) == (h == 0), a, jnp.zeros_like(a))


def causal():
    shape = (BQ, BQ)
    return lax.broadcasted_iota(jnp.int32, shape, 1) <= lax.broadcasted_iota(jnp.int32, shape, 0)


def forward_pair(q, k, v, pk, pv, kx, pkx, o_ref, qx_ref, kext, vext, pkext, pvext, keep):
    ln, lp = lanes(LEN), lanes(128)
    for h in (0, 1):
        rows = slice(h * 128, (h + 1) * 128)
        kext[h, :, :128] = half(k[...], h)
        kext[h, :, 128:] = half(kx[...], h)
        vext[h, :, :128] = half(v[...], h)
        vext[h, :, 128:] = jnp.where((ln < 64) == (h == 0), 1.0, 0.0).astype(bf16)
        pkext[rows, :128] = half(pk[...], h)
        pkext[rows, 128:] = half(pkx[...], h)
        pvext[rows, :128] = half(pv[...], h)
        pvext[rows, 128:] = jnp.where((lp < 64) == (h == 0), 1.0, 0.0).astype(bf16)
    for i in range(NQ):
        rows, n = pl.ds(i * BQ, BQ), (i + 1) * BQ
        flags = query_flags(i, BQ)
        qe = jnp.concatenate([q[rows, :], flags.astype(bf16)], axis=1)
        before = dot(qe, pkext[...], NT)
        acc, tops, parts = None, [], []
        for h in (0, 1):
            s = dot(qe, kext[h, :n, :], NT)
            near = jnp.where(causal(), s[:, n - BQ :], NEG)
            first = before[:, h * 128 : (h + 1) * 128]
            m = jnp.maximum(
                jnp.max(near, axis=1, keepdims=True), jnp.max(first, axis=1, keepdims=True)
            )
            if i:
                m = jnp.maximum(m, jnp.max(s[:, : n - BQ], axis=1, keepdims=True))
            near = jnp.exp(near - m).astype(bf16)
            keep(h, i, slice(n - BQ, n), near)
            a = dot(near, vext[h, n - BQ : n, :])
            if i:
                far = jnp.exp(s[:, : n - BQ] - m).astype(bf16)
                keep(h, i, slice(0, n - BQ), far)
                a = a + dot(far, vext[h, : n - BQ, :])
            parts.append(jnp.exp(first - m).astype(bf16))
            tops.append(m)
            acc = a if acc is None else acc + a
        acc = acc + dot(jnp.concatenate(parts, axis=1), pvext[...])
        inverse = 1.0 / acc[:, 128:]
        o_ref[rows, :] = (acc[:, :128] * inverse).astype(bf16)
        b, high = lanes(BQ) % 64, inverse.astype(bf16).astype(f32)
        flags = jnp.where(b == 8, high, jnp.where(b == 9, inverse - high, flags))
        qx_ref[rows, :] = extra(flags, -jnp.where(lanes(BQ) < 64, tops[0], tops[1]))


def backward_pair(q, k, v, do, dx, dsp, pkd, dq_ref, dk_ref, dv_ref, kext, vext, qt, dot_t, dkt, dvt, kept):
    b = lanes(LEN) % 64
    ones = jnp.where((b >= 1) & (b < 4), 1.0, 0.0).astype(bf16)
    for h in (0, 1):
        kext[h, :, :128] = half(k[...], h)
        vext[h, :, :128] = half(v[...], h)
        vext[h, :, 128:] = half(ones, h)
    qt[...] = q[...].T
    dot_t[...] = do[...].T

    def grad_probs(i, h):
        rows = pl.ds(i * BQ, BQ)
        return dot(jnp.concatenate([do[rows, :], dx[rows, :]], axis=1), vext[h, : (i + 1) * BQ, :], NT)

    steps = [(i, h) for i in reversed(range(NQ)) for h in (0, 1)]
    ahead = grad_probs(*steps[0])
    for (i, h), after in zip(steps, steps[1:] + [None]):
        rows, n = pl.ds(i * BQ, BQ), (i + 1) * BQ
        g = ahead
        if after is not None:
            ahead = grad_probs(*after)
        if h == 0:
            dq = dot(dsp[rows, :], pkd[...])
        hr = slice(h * 64, (h + 1) * 64)
        qth, dth = qt[hr, i * BQ : (i + 1) * BQ], dot_t[hr, i * BQ : (i + 1) * BQ]
        p = kept(h, i, n)
        ds = (p.astype(f32) * g).astype(bf16)
        dq = dq + dot(ds, kext[h, :n, :128])
        if i == NQ - 1:
            dkt[hr, :n] = dot(qth, ds)
            dvt[hr, :n] = dot(dth, p)
        else:
            dkt[hr, :n] += dot(qth, ds)
            dvt[hr, :n] += dot(dth, p)
        if h == 1:
            dq_ref[rows, :] = (dq * 0.125).astype(bf16)
    dk_ref[...] = dkt[...].T.astype(bf16)
    dv_ref[...] = dvt[...].T.astype(bf16)


def block(index, size=256):
    return pl.ds(pl.multiple_of(index * size, size), size)


def loop(body, count=4):
    lax.fori_loop(0, count, lambda r, _: (body(r), 0)[1], 0)


def unrolled(body, count=4):
    for r in range(count):
        body(r)


def center(field):
    mean = jnp.mean(field, axis=-1, keepdims=True)
    centred = field - mean
    return centred, lax.rsqrt(jnp.mean(centred * centred, axis=-1, keepdims=True) + 1e-05)


def norm_back(grad, normed, inv):
    down = grad - jnp.mean(grad, axis=-1, keepdims=True)
    return inv * (down - normed * jnp.mean(grad * normed, axis=-1, keepdims=True))


def key_columns(kx, lengths, buckets):
    full = buckets[0] == LEN
    b = lanes(256) % 64
    for r in range(4):
        place = lax.broadcasted_iota(jnp.int32, (256, 128), 0)
        within = jnp.where(full, place + r * 256, place)
        extent = jnp.where(full, lengths[0, 0], lengths[0, r])
        e = jnp.where((b == 0) & (within >= extent), NEG, 0.0)
        e = jnp.where((b >= 1) & (b < 4), 1.0, e)
        e = jnp.where((b == 4 + r) & jnp.logical_not(full), NEG, e)
        kx[r * 256 : (r + 1) * 256, :] = e.astype(bf16)


def prefix_columns():
    r, b = lax.broadcasted_iota(jnp.int32, (128, 128), 0), lanes(128) % 64
    return jnp.where((b == 0) & (r >= PREFIX), NEG, jnp.where((b >= 1) & (b < 4), 1.0, 0.0)).astype(bf16)


def head_rows(shape, per_head):
    r = lax.broadcasted_iota(jnp.int32, shape, 0) // 16
    return r == lax.broadcasted_iota(jnp.int32, shape, 1) // per_head


def layer_kernel(
    dims, x_hbm, cot_hbm, wq, wo, wf, wp, b_qkv, b_out, b_fc, b_proj, gain, shift, embed, r_in, r_in_b,
    r_out, r_out_b, lengths, buckets,
    ga, gp, stash, out_hbm, gtok_hbm, small,
    shq, sh, shp, bias, xb, nb, ob, qkv, qx, dob, gs, middle, acc, big, WQ, W, kx, pkx, pk, pv, kext, vext, pkext, pvext,
    qt, dot_t, dkt, dvt, dsp, pkd, total, came,
    zs, zr, zps, zpr, as_, ar, bs, br, cs, cr, ls, loc, ts, tr, keeps,
):
    Z, Y, X, C = dims
    dp, fs = lax.axis_index("dp"), lax.axis_index("fsdp")
    z, y, x, c = dp // Y, dp % Y, fs // C, fs % C
    zid = lambda dz: (lax.rem(z + dz, Z) * Y + y, fs)
    yid, xid, cid = (z * Y + (1 - y), fs), (dp, (1 - x) * C + c), (dp, x * C + (1 - c))

    def remote(s, d, ss, rs, dev):
        return pltpu.make_async_remote_copy(
            src_ref=s, dst_ref=d, send_sem=ss, recv_sem=rs, device_id=dev, device_id_type=MESH
        )

    def place(k, *ix):
        if k < OUT:
            return WQ.at[(k, *ix)]
        if k in PROJ:
            return gp.at[(PROJ.index(k), ix[1] * X + ix[2], *ix[3:])]
        return ga.at[(0 if k == OUT else 1 + FC.index(k), *ix)]

    def own(k):
        if k < OUT:
            return shq.at[k], place(k, z, y, x, c)
        if k in PROJ:
            return shp, place(k, z, y, x, c)
        return sh.at[0 if k == OUT else 1 + FC.index(k)], place(k, z, y, x, c)

    def z_copy(k, dz):
        if k in PROJ:
            return remote(*own(k), zps.at[dz - 1], zpr.at[PROJ.index(k)], zid(dz))
        s, d = own(k)
        if k == SIDE:
            s = d = place(k, z, A, A, c)
        return remote(s, d, zs.at[k, dz - 1], zr.at[k, dz - 1], zid(dz))

    def a_copy(k, h):
        first = (h == 0) != (k == SIDE)
        s = place(k, z if k == SIDE else A, y, x, c, h)
        return remote(s, s, as_.at[k, h], ar.at[k, h], yid if first else xid)

    def b_copy(k, h):
        first = (h != 1) != (k == SIDE)
        if k in PROJ:
            plane = gp.at[PROJ.index(k)]
            s = plane.at[pl.ds(y * X, X), c, 1] if h == 1 else plane.at[(h // 2) * X + x, c, 0]
        else:
            ix = (A, x) if first else (y, A)
            s = place(k, z if k == SIDE else A, *ix, c, h)
        return remote(s, s, bs.at[k, h], br.at[k, h], xid if first else yid)

    def halves(k):
        return (0, 1, 2) if k in PROJ else (0, 1)

    def c_copy(k):
        s = gp.at[PROJ.index(k), :, c] if k in PROJ else place(k, A, A, A, c)
        return remote(s, s, cs.at[k], cr.at[k], cid)

    def own_copy(k):
        return pltpu.make_async_copy(*own(k), ls.at[k])

    def stage_z(k):
        def go():
            if k != SIDE:
                own_copy(k).start()
            for dz in (2, 1, 3):
                z_copy(k, dz).start()

        if k == SIDE:
            for h in (0, 1):
                b_copy(k, h).wait_recv()
        if k in PROJ:
            pl.when(z == PROJ.index(k))(go)
        else:
            go()

    def stage_a(k):
        if k in PROJ:
            j = PROJ.index(k)
            pl.when(z == j)(lambda: own_copy(k).wait())
            pl.when(z != j)(lambda: z_copy(k, 1).wait_recv())
        else:
            own_copy(k).wait()
            for dz in (1, 2, 3) if k != SIDE else ():
                z_copy(k, dz).wait_recv()
        for h in (0, 1):
            a_copy(k, h).start()

    def stage_b(k):
        for h in (0, 1):
            a_copy(k, h).wait_recv()
        for h in halves(k):
            b_copy(k, h).start()

    def stage_c(k):
        if k == SIDE:
            for dz in (1, 2, 3):
                z_copy(k, dz).wait_recv()
        else:
            for h in halves(k):
                b_copy(k, h).wait_recv()
        c_copy(k).start()

    def pump(t):
        for k in AHEAD[t] if t < len(AHEAD) else ():
            stage_z(k)
        for k in (t,) if t < 2 else (2, 3) if t == 2 else (t + 1,):
            if k < N:
                stage_a(k)
        if 0 <= t - 1 < N:
            stage_b(t - 1)
        if 0 <= t - 2 < N:
            stage_c(t - 2)
        if 0 <= t - 3 < N:
            c_copy(t - 3).wait_recv()

    def local(s, d, i):
        return pltpu.make_async_copy(s, d, loc.at[i])

    slots = {OUT: 0, FC[0]: 1, FC[1]: 0, FC[2]: 1, FC[3]: 0, PROJ[0]: 2, PROJ[1]: 3, PROJ[2]: 2, PROJ[3]: 3}

    def load(k, slot=None):
        s = gp.at[PROJ.index(k)] if k in PROJ else ga.at[0 if k == OUT else 1 + FC.index(k)]
        return local(s, W.at[slots[k] if slot is None else slot], 20 + k)

    def probs(p, out):
        def piece(h, i):
            n = slice(0, (i + 1) * BQ)
            here = W.at[2 * (p % 2) + h, i, :, :, :, :, :, n]
            there = stash.at[2 * p + h, i, :, :, :, :, :, n]
            sem = keeps.at[p % 2, h, i]
            return pltpu.make_async_copy(here, there, sem) if out else pltpu.make_async_copy(there, here, sem)

        return [piece(h, i) for h in (0, 1) for i in range(NQ)]

    def start_all(copies):
        for d in copies:
            d.start()

    def wait_all(copies):
        for d in copies:
            d.wait()

    shards = [
        local(wq.at[:, :, pl.ds(j * D + g * 256, 256)], shq.at[g, :, :, pl.ds(j * 256, 256)], 33 + 3 * g + j)
        for g in range(4) for j in range(3)
    ]
    shards += [local(wf.at[:, :, pl.ds(3 * D, D)], sh.at[4], 4), local(wo, sh.at[0], 0)]
    shards += [local(wf.at[:, :, pl.ds(j * D, D)], sh.at[1 + j], 1 + j) for j in range(3)]
    shards += [local(wp, shp, 15)]
    for d in shards:
        d.start()
    rin = local(r_in, middle.at[:, pl.ds(0, 512)], 8)
    rout = [local(r_out.at[:, pl.ds(j * D, D)], acc.at[pl.ds(j * 512, 512), :], 9 + j) for j in (0, 1)]
    xload = local(x_hbm, xb, 11)
    xload.start()
    barrier = pltpu.get_barrier_semaphore()
    for d in [zid(dz) for dz in range(1, Z)] + [yid, xid, cid]:
        pl.semaphore_signal(barrier, inc=1, device_id=d, device_id_type=MESH)
    pl.semaphore_wait(barrier, Z + 2)
    for d in shards:
        d.wait()
    own_copy(SIDE).start()
    stage_z(0)
    stage_a(SIDE)
    stage_z(1)
    for d in [rin] + rout:
        d.start()
    xload.wait()

    def norm_one(r):
        rows = block(r)
        centred, inv = center(xb[rows, :].astype(f32))
        nb[rows, :] = (centred * inv * gain[0:1, :] + shift[0:1, :]).astype(bf16)

    loop(norm_one)
    pump(0)
    stage_b(SIDE)
    for j in range(3):
        bias[j : j + 1, :] = b_qkv[pl.ds(j * D, D)].reshape(1, D).astype(f32)
    small[...] = jnp.zeros_like(small)
    small[0:PREFIX, EMB] = embed[...]
    rin.wait()
    hid = jnp.tanh(precise(small[:, EMB], middle[:, 0:512]) + r_in_b[...].reshape(1, 512))
    small[:, HID] = hid
    pump(1)
    live = lax.broadcasted_iota(jnp.int32, (16, D), 0) < PREFIX
    for j, dest in ((0, pk), (1, pv)):
        rout[j].wait()
        t = precise(hid, acc[j * 512 : (j + 1) * 512, :])
        t = jnp.where(live, t + r_out_b[pl.ds(j * D, D)].reshape(1, D), 0.0)
        dest[...] = jnp.zeros_like(dest)
        dest[0:16, :] = t.astype(bf16)
    key_columns(kx, lengths, buckets)
    pkx[...] = prefix_columns()
    pump(2)
    pump(3)

    def project(g):
        cols = block(g)
        for j in range(3):
            t = dot(nb[...], WQ[g, ..., j * 256 : (j + 1) * 256].reshape(D, 256))
            t = (t + bias[j : j + 1, cols]).astype(bf16)
            qkv[j, :, cols] = t * jnp.asarray(0.125, bf16) if j == 0 else t

    def attend(p):
        cols = block(p, 128)
        pl.when(p % 2 == 0)(lambda: project(p // 2))
        pl.when(p >= 2)(lambda: wait_all(probs(p - 2, True)))

        def keep(h, i, cols, value):
            W[2 * (p % 2) + h, i, :, :, :, :, :, cols] = value.reshape(Y, X, C, 2, 16, value.shape[1])

        forward_pair(
            *(qkv.at[k, :, cols] for k in range(3)), pk.at[:, cols], pv.at[:, cols], kx, pkx,
            ob.at[:, cols], qx.at[:, cols], kext, vext, pkext, pvext, keep,
        )
        start_all(probs(p, True))
        for at, t in ((0, 4), (2, 5), (4, 6), (6, 7)):
            pl.when(p == at)(functools.partial(pump, t))

    loop(attend, 8)
    wait_all(probs(6, True))
    load(OUT).start()
    wait_all(probs(7, True))
    load(OUT).wait()
    for cb in range(4):
        cols = slice(cb * 256, (cb + 1) * 256)
        t = dot(ob[...], W[0, ..., cols].reshape(D, 256))
        middle[:, cols] = xb[:, cols].astype(f32) + (t + b_out[pl.ds(cb * 256, 256)].reshape(1, 256).astype(f32))
    cotload = local(cot_hbm, xb, 12)
    cotload.start()
    pump(8)
    load(FC[0]).start()

    def norm_two(r):
        rows = block(r)
        m = middle[rows, :]
        centred, inv = center(m)
        nb[rows, :] = (centred * inv * gain[1:2, :] + shift[1:2, :]).astype(bf16)
        acc[rows, :] = m + b_proj[...].reshape(1, D).astype(f32)
        gs[rows, :] = jnp.zeros_like(m)

    loop(norm_two)
    def hidden_part(f):
        k, r = FC[f], f % 2
        load(k).wait()
        for cb in range(4):
            cols = slice(cb * 256, (cb + 1) * 256)
            u = dot(nb[...], W[slots[k], ..., cols].reshape(D, 256))
            u = u + b_fc[pl.ds(f * D + cb * 256, 256)].reshape(1, 256).astype(f32)
            sq = u * u
            t = jnp.tanh(u * (ROOT + (ROOT * 0.044715) * sq))
            plus = 0.5 + 0.5 * t
            big[r, :, cols] = (u * plus).astype(bf16)
            slope = plus + (0.5 * u) * (1.0 - t * t) * (ROOT + (3 * ROOT * 0.044715) * sq)
            big[2 + r, :, cols] = slope.astype(bf16)

    def out_part(f):
        r = f % 2
        load(PROJ[f]).wait()
        for cb in range(4):
            cols = slice(cb * 256, (cb + 1) * 256)
            acc[:, cols] += dot(big[r], W[2 + r, ..., cols].reshape(D, 256))
            g = dot(xb[...], W[2 + r, cb].reshape(256, D), NT)
            big[2 + r, :, cols] = (g * big[2 + r, :, cols].astype(f32)).astype(bf16)

    def second_part(f):
        for cb in range(4):
            cols = slice(cb * 256, (cb + 1) * 256)
            gs[:, cols] += dot(big[2 + f % 2], W[slots[FC[f]], cb].reshape(256, D), NT)

    hidden_part(0)
    pump(9)
    load(PROJ[0]).start()
    cotload.wait()
    out_part(0)
    pump(10)
    load(FC[1]).start()
    second_part(0)
    hidden_part(1)
    pump(11)
    load(PROJ[1]).start()
    out_part(1)
    pump(12)
    load(FC[2]).start()
    second_part(1)
    stage_c(SIDE)
    hidden_part(2)
    c_copy(SIDE).wait_recv()
    load(FC[3]).start()
    pump(13)
    load(PROJ[2]).start()
    hidden_part(3)
    out_part(2)
    pump(14)
    load(PROJ[3]).start()
    second_part(2)
    load(OUT, 1).start()
    out_part(3)
    second_part(3)

    def norm_two_back(r):
        rows = block(r)
        centred, inv = center(middle[rows, :])
        t = norm_back(gs[rows, :] * gain[1:2, :], centred * inv, inv)
        t = xb[rows, :].astype(f32) + t
        gs[rows, :] = t
        nb[rows, :] = t.astype(bf16)
        W[2, r] = acc[rows, :].astype(bf16).reshape(Y, X, C, 2, 16, D)

    loop(norm_two_back)
    out_save = local(W.at[2], out_hbm, 13)
    out_save.start()
    xload = local(x_hbm, xb, 11)
    xload.start()
    for d in [rin] + rout:
        d.start()
    load(OUT, 1).wait()
    for cb in range(4):
        dob[:, cb * 256 : (cb + 1) * 256] = dot(nb[...], W[1, cb].reshape(256, D), NT).astype(bf16)

    start_all(probs(0, False))
    gi = lax.broadcasted_iota(jnp.int32, (128, 128), 0) // 64
    group = jnp.where(gi == lanes(128) // 64, 1.0, 0.0).astype(bf16)
    row = lax.broadcasted_iota(jnp.int32, (128, 128), 0) % 64
    pick = jnp.where((row == 8) | (row == 9), group, jnp.zeros_like(group))
    group = jnp.concatenate([group, group], axis=0)

    def delta(p):
        cols = block(p, 128)
        inverse = dot(qx[:, cols], pick)
        scaled = (dob[:, cols].astype(f32) * inverse).astype(bf16)
        dob[:, cols] = scaled
        prod = scaled.astype(f32) * ob[:, cols].astype(f32)
        high = prod.astype(bf16)
        low = (prod - high.astype(f32)).astype(bf16)
        sums = -dot(jnp.concatenate([high, low], axis=1), group)
        high = sums.astype(bf16)
        low = (sums - high.astype(f32)).astype(bf16)
        b = lanes(LEN) % 64
        off = pl.multiple_of(768 + (p % 2) * 128, 128)
        big[p // 2, :, pl.ds(off, 128)] = jnp.where(b == 1, high, jnp.where(b == 2, low, jnp.zeros_like(low)))

    loop(delta, 8)
    same = head_rows((256, D), 64)
    spread = [jnp.concatenate([t[0:16, :]] * 16, axis=0) for t in (pk, pv)]
    spread = [jnp.where(same, t, jnp.zeros_like(t)) for t in spread]
    pkd[...] = spread[0]
    lane = lax.broadcasted_iota(jnp.int32, (256, D), 1) % 64
    unit = jnp.where(same & (lane >= 1) & (lane < 4), 1.0, 0.0)
    dead = lax.broadcasted_iota(jnp.int32, (256, D), 0) % 16 >= PREFIX
    mask = jnp.where(same & (lane == 0) & dead, NEG, unit).astype(bf16)
    unit = unit.astype(bf16)
    prob = jnp.exp(dot(qkv[0], spread[0], NT) + dot(qx[...], mask, NT))
    deltas = jnp.concatenate([big[g, :, 768:] for g in range(4)], axis=1)
    grad = dot(dob[...], spread[1], NT) + dot(deltas, unit, NT)
    dsp[...] = (prob * grad).astype(bf16)
    for j, (left, right) in enumerate(((dsp[...], qkv[0]), (prob.astype(bf16), dob[...]))):
        t = jnp.where(same, dot(left.T, right), 0.0)
        total[0, :, j * D : (j + 1) * D] = jnp.sum(t.reshape(16, 16, D), axis=0)

    partners = [cid, xid, yid, ((z + 1 - 2 * (z % 2)) * Y + y, fs), zid(2)]

    def exchange(s):
        return remote(total.at[s], came.at[s], ts.at[s], tr.at[s], partners[s])

    def step(s):
        if s > 0:
            exchange(s - 1).wait_recv()
            total[s] = total[s - 1] + came[s - 1]
        if s < 5:
            exchange(s).start()

    out_save.wait()
    start_all(probs(1, False))

    def attend_back(p):
        for s in range(6):
            pl.when(p == s)(functools.partial(step, s))
        cols = block(p, 128)
        part = lambda j: big.at[p // 2, :, pl.ds(pl.multiple_of(j * 256 + (p % 2) * 128, 128), 128)]
        wait_all(probs(p, False))
        kept = lambda h, i, n: W[2 * (p % 2) + h, i, :, :, :, :, :, :n].reshape(BQ, n)
        backward_pair(
            *(qkv.at[k, :, cols] for k in range(3)), dob.at[:, cols], part(3), dsp, pkd.at[:, cols],
            part(0), part(1), part(2), kext, vext, qt, dot_t, dkt, dvt, kept,
        )
        pl.when(p < 6)(lambda: start_all(probs(p + 2, False)))

    loop(attend_back, 8)
    for d in rout:
        d.wait()
    rin.wait()
    small[:, GPRE] = total[5]
    hid = small[:, HID]
    t = sum(close(total[5, :, j * D : (j + 1) * D], acc[j * 512 : (j + 1) * 512, :]) for j in (0, 1))
    t = t * (1.0 - hid * hid)
    small[:, PRE] = t
    small[:, GEMB] = close(t, middle[:, 0:512])
    for cb in range(4):
        cols = slice(cb * 256, (cb + 1) * 256)
        acc[:, cols] = sum(dot(big[g, :, :768], WQ[g, cb].reshape(256, 768), NT) for g in range(4))
    xload.wait()

    def norm_one_back(r):
        rows = block(r)
        centred, inv = center(xb[rows, :].astype(f32))
        t = norm_back(acc[rows, :] * gain[0:1, :], centred * inv, inv)
        nb[rows, :] = (gs[rows, :] + t).astype(bf16)

    loop(norm_one_back)
    gtok_save = local(nb, gtok_hbm, 14)
    gtok_save.start()
    for k in range(N + 1):
        if k not in PROJ:
            for dz in (1, 2, 3):
                z_copy(k, dz).wait_send()
        for h in (0, 1):
            a_copy(k, h).wait_send()
        for h in halves(k):
            b_copy(k, h).wait_send()
        c_copy(k).wait_send()
    for dz in (1, 2, 3):
        z_copy(PROJ[0], dz).wait_send()
    for s in range(5):
        exchange(s).wait_send()
    gtok_save.wait()


def layer(
    dims, x, cot, wq, wo, wf, wp, b_qkv, b_out, b_fc, b_proj, gain, shift, embed, r_in, r_in_b, r_out,
    r_out_b, lengths, buckets,
):
    Z, Y, X, C = dims
    S, V, sds = pltpu.SemaphoreType.DMA, pltpu.VMEM, jax.ShapeDtypeStruct
    anys, vm, sm = (pl.BlockSpec(memory_space=s) for s in (pl.ANY, pltpu.VMEM, pltpu.SMEM))
    wide, wide32 = V((LEN, D), bf16), V((LEN, D), f32)
    return pl.pallas_call(
        functools.partial(layer_kernel, dims),
        out_shape=[
            sds((5, Z, Y, X, C, 2, 16, D), bf16), sds((4, Z, Y, X, C, 2, 16, D), bf16),
            sds((16, Z, Y, X, C, 2, 16, LEN), bf16), sds((Z, Y, X, C, 2, 16, D), bf16), sds((LEN, D), bf16),
            sds((16, 5 * D), f32),
        ],
        in_specs=[anys] * 6 + [vm] * 7 + [anys, vm, anys, vm, sm, sm],
        out_specs=[anys] * 5 + [vm],
        scratch_shapes=[
            V((4, 2, 16, 768), bf16), V((5, 2, 16, D), bf16), V((2, 2, 2, 16, D), bf16), V((8, D), f32), wide, wide, wide, V((3, LEN, D), bf16), wide, wide,
            wide32, wide32, wide32, V((4, LEN, D), bf16),
            V((4, Z, Y, X, C, 2, 16, 768), bf16), V((4, Z, Y, X, C, 2, 16, D), bf16),
            V((LEN, 128), bf16), V((128, 128), bf16), V((128, D), bf16), V((128, D), bf16),
            V((2, LEN, 256), bf16), V((2, LEN, 256), bf16), V((256, 256), bf16), V((256, 256), bf16),
            V((128, LEN), bf16), V((128, LEN), bf16), V((128, LEN), f32), V((128, LEN), f32),
            V((LEN, 256), bf16), V((256, D), bf16), V((6, 16, 2 * D), f32), V((5, 16, 2 * D), f32),
            S((N + 1, 3)), S((N + 1, 3)), S((3,)), S((4,)), *[S((N + 1, 2))] * 2, *[S((N + 1, 3))] * 2, *[S((N + 1,))] * 3, S((45,)),
            S((5,)), S((5,)), S((2, 2, NQ)),
        ],
        compiler_params=pltpu.CompilerParams(
            collective_id=0, has_side_effects=True, vmem_limit_bytes=62 << 20
        ),
    )(
        x, cot, *(w.reshape(2, 16, w.shape[1]) for w in (wq, wo, wf)), wp.reshape(2, 2, 2, 16, D),
        b_qkv, b_out, b_fc, b_proj, gain, shift, embed, r_in, r_in_b, r_out, r_out_b, lengths, buckets,
    )


def outer(left, right):
    a, b, c = (t.astype(bf16) for t in split_three(left))
    p, q, r = (t.astype(bf16) for t in split_three(right))
    left = jnp.concatenate([a, a, b, a, c, b], axis=0)
    right = jnp.concatenate([p, q, p, r, p, q], axis=0)
    return dot(left.T, right)


def finish_kernel(out_in, gtok_in, small, out, gtok, g_embed, g_in, g_in_b, g_out, g_out_b):
    g_out[...] = outer(small[:, HID], small[:, GPRE])
    g_in[...] = outer(small[:, EMB], small[:, PRE])
    out[...] = out_in[...]
    gtok[...] = gtok_in[...]
    g_out_b[...] = jnp.sum(small[:, GPRE], axis=0)
    g_in_b[...] = jnp.sum(small[:, PRE], axis=0)
    g_embed[...] = small[0:PREFIX, GEMB]


def finish(out, gtok, small):
    vm, sds = pl.BlockSpec(memory_space=pltpu.VMEM), jax.ShapeDtypeStruct
    return pl.pallas_call(
        finish_kernel,
        out_shape=[
            sds(out.shape, bf16), sds(gtok.shape, bf16), sds((PREFIX, D), f32), sds((D, 512), f32),
            sds((512,), f32), sds((512, 2 * D), f32), sds((2 * D,), f32),
        ],
        in_specs=[vm] * 3,
        out_specs=[vm] * 7,
        compiler_params=pltpu.CompilerParams(vmem_limit_bytes=62 << 20),
    )(out, gtok, small)


def normalize(field, gain, shift):
    centred, inv = center(field)
    return centred * inv * gain + shift


def plain_heads(matrix):
    return matrix.reshape(matrix.shape[0], 16, 64).transpose(1, 0, 2)


def plain_visible(seg_lengths, bucket):
    places = jnp.arange(LEN, dtype=jnp.int32)
    segment = places // bucket
    within = places - segment * bucket
    extent = sum(jnp.where(segment == which, seg_lengths[which], 0) for which in range(4))
    same = segment[:, None] == segment[None, :]
    return same & (places[None, :] <= places[:, None]) & (within < extent)[None, :]


def plain_attend(q, k, v, allowed):
    mix = lambda spec, a, b: jnp.einsum(spec, a.astype(bf16), b.astype(bf16), preferred_element_type=f32)
    scores = jnp.where(allowed, mix("qd,kd->qk", q, k) * 0.125, NEG)
    return mix("qk,kd->qd", jax.nn.softmax(scores, axis=-1), v)


def plain_layer(
    tokens, cotangent, w_qkv, w_out, w_fc, w_proj, bias_qkv, bias_out, bias_fc, bias_proj,
    ln_gain, ln_shift, prefix_embed, reparam_in, reparam_in_bias, reparam_out, reparam_out_bias,
    lengths, buckets,
):
    full_qkv, full_out, full_fc, full_proj = (
        lax.all_gather(t, ("dp", "fsdp"), axis=0, tiled=True) for t in (w_qkv, w_out, w_fc, w_proj)
    )
    hidden = jnp.tanh(precise(prefix_embed, reparam_in) + reparam_in_bias)
    prefix_rows = (precise(hidden, reparam_out) + reparam_out_bias).astype(bf16)
    pk, pv = plain_heads(prefix_rows[:, :D]), plain_heads(prefix_rows[:, D:])
    inputs = tokens.astype(f32)
    norm_one = lambda field: normalize(field, ln_gain[0], ln_shift[0])
    norm_two = lambda field: normalize(field, ln_gain[1], ln_shift[1])
    normed, pull_one = jax.vjp(norm_one, inputs)
    joined = (dot(normed.astype(bf16), full_qkv) + bias_qkv.astype(f32)).astype(bf16)
    q, k, v = (plain_heads(joined[:, i * D : (i + 1) * D]) for i in range(3))
    allowed = jnp.concatenate([jnp.ones((LEN, PREFIX), bool), plain_visible(lengths[0], buckets[0])], 1)

    def one_head(parts):
        q, k, v, pk, pv, grad = parts
        run = lambda q, k, v: plain_attend(q, k, v, allowed)
        mixed, pull = jax.vjp(run, q.astype(f32), *(jnp.concatenate(t).astype(f32) for t in ((pk, k), (pv, v))))
        return mixed, pull(grad.astype(f32))

    heads = (q, k, v, pk, pv)
    mixed = lax.map(lambda parts: one_head((*parts, parts[0]))[0], heads)
    back = lambda t: t.transpose(1, 0, 2).reshape(-1, D)
    attended = back(mixed).astype(bf16)
    middle = inputs + (dot(attended, full_out) + bias_out.astype(f32))
    second, pull_two = jax.vjp(norm_two, middle)
    before = dot(second.astype(bf16), full_fc) + bias_fc.astype(f32)
    activated, pull_gelu = jax.vjp(lambda field: jax.nn.gelu(field, approximate=True), before)
    result = middle + (dot(activated.astype(bf16), full_proj) + bias_proj.astype(f32))
    grad_before = pull_gelu(dot(cotangent, full_proj, NT))[0].astype(bf16)
    grad_middle = cotangent.astype(f32) + pull_two(dot(grad_before, full_fc, NT))[0]
    grad_attended = dot(grad_middle.astype(bf16), full_out, NT).astype(bf16)
    dq, dk, dv = lax.map(lambda parts: one_head(parts)[1], (*heads, plain_heads(grad_attended)))
    grads = [back(t).astype(bf16) for t in (dq, dk[:, PREFIX:], dv[:, PREFIX:])]
    grad_prefix = jnp.concatenate([back(t[:, :PREFIX]) for t in (dk, dv)], 1)
    grad_prefix = lax.psum(grad_prefix, ("dp", "fsdp"))
    grad_normed = dot(jnp.concatenate(grads, 1), full_qkv, NT)
    grad_tokens = (grad_middle + pull_one(grad_normed)[0]).astype(bf16)
    grad_pre = precise(grad_prefix, reparam_out, NT) * (1.0 - hidden * hidden)
    return (
        result.astype(bf16), grad_tokens, precise(grad_pre, reparam_in, NT), precise(prefix_embed.T, grad_pre),
        jnp.sum(grad_pre, axis=0), precise(hidden.T, grad_prefix), jnp.sum(grad_prefix, axis=0),
    )


def on_device(dims, *args):
    if dims is None:
        return plain_layer(*args)
    _, _, _, out, gtok, small = layer(dims, *args)
    return tuple(finish(out.reshape(gtok.shape), gtok, small))


def chip_dims(mesh):
    if dict(mesh.shape) == {"dp": 8, "fsdp": 4}:
        return (4, 2, 2, 2)
    return None


def solution(mesh):
    split, lone = P(("dp", "fsdp"), None), P()
    return jax.shard_map(
        functools.partial(on_device, chip_dims(mesh)),
        mesh=mesh,
        in_specs=(split,) * 6 + (lone,) * 11 + (split, P(("dp", "fsdp"))),
        out_specs=(split, split) + (lone,) * 5,
        check_vma=False,
    )
```

```python
import functools, math
import jax, jax.numpy as jnp
from jax import lax
from jax.experimental import pallas as pl
from jax.experimental.pallas import tpu as pltpu
from jax.sharding import PartitionSpec as P

f32, bf16 = jnp.float32, jnp.bfloat16
MESH = pl.DeviceIdType.MESH
A = slice(None)
D = 1024
LEN = 1024
PREFIX = 10
BQ = 256
NQ = LEN // BQ
NEG = -1e30
ROOT = math.sqrt(2.0 / math.pi)
HIGHEST = lax.Precision.HIGHEST
NT = (((1,), (1,)), ((), ()))
NN = (((1,), (0,)), ((), ()))
OUT = 4
FC = (5, 7, 9, 12)
PROJ = (6, 8, 10, 11)
SIDE = 12
N = 12
AHEAD = ((2,), (3, 4), (5, 6), (7, 8), (9, 10), (11,), (SIDE,))
HID, PRE, GPRE, EMB, GEMB = slice(0, 512), slice(512, D), slice(D, 3 * D), slice(3 * D, 4 * D), slice(4 * D, 5 * D)


def dot(a, b, dims=NN):
    return lax.dot_general(a, b, dims, preferred_element_type=f32)


def precise(a, b, dims=NN):
    return lax.dot_general(a, b, dims, precision=HIGHEST, preferred_element_type=f32)


def close(a, b):
    high = a.astype(bf16)
    low = (a - high.astype(f32)).astype(bf16)
    t = dot(jnp.concatenate([high, low], axis=0), b.astype(bf16), NT)
    return t[: a.shape[0]] + t[a.shape[0] :]


def lanes(rows):
    return lax.broadcasted_iota(jnp.int32, (rows, 128), 1)


def split_three(value):
    high = value.astype(bf16)
    rest = value - high.astype(f32)
    mid = rest.astype(bf16)
    return high.astype(f32), mid.astype(f32), rest - mid.astype(f32)


def extra(base, value):
    b = lanes(value.shape[0]) % 64
    high, mid, low = split_three(value)
    return jnp.where(b == 1, high, jnp.where(b == 2, mid, jnp.where(b == 3, low, base))).astype(bf16)


def query_flags(i, rows):
    b = lanes(rows) % 64
    return jnp.where((b == 0) | ((b >= 4) & (b < 8) & (b != 4 + i)), 1.0, 0.0)


def half(a, h):
    return jnp.where((lanes(a.shape[0]) < 64) == (h == 0), a, jnp.zeros_like(a))


def causal():
    shape = (BQ, BQ)
    return lax.broadcasted_iota(jnp.int32, shape, 1) <= lax.broadcasted_iota(jnp.int32, shape, 0)


def forward_pair(q, k, v, pk, pv, kx, pkx, o_ref, qx_ref, kext, vext, pkext, pvext, keep):
    ln, lp = lanes(LEN), lanes(128)
    for h in (0, 1):
        rows = slice(h * 128, (h + 1) * 128)
        kext[h, :, :128] = half(k[...], h)
        kext[h, :, 128:] = half(kx[...], h)
        vext[h, :, :128] = half(v[...], h)
        vext[h, :, 128:] = jnp.where((ln < 64) == (h == 0), 1.0, 0.0).astype(bf16)
        pkext[rows, :128] = half(pk[...], h)
        pkext[rows, 128:] = half(pkx[...], h)
        pvext[rows, :128] = half(pv[...], h)
        pvext[rows, 128:] = jnp.where((lp < 64) == (h == 0), 1.0, 0.0).astype(bf16)
    for i in range(NQ):
        rows, n = pl.ds(i * BQ, BQ), (i + 1) * BQ
        flags = query_flags(i, BQ)
        qe = jnp.concatenate([q[rows, :], flags.astype(bf16)], axis=1)
        before = dot(qe, pkext[...], NT)
        acc, tops, parts = None, [], []
        for h in (0, 1):
            s = dot(qe, kext[h, :n, :], NT)
            near = jnp.where(causal(), s[:, n - BQ :], NEG)
            first = before[:, h * 128 : (h + 1) * 128]
            m = jnp.maximum(
                jnp.max(near, axis=1, keepdims=True), jnp.max(first, axis=1, keepdims=True)
            )
            if i:
                m = jnp.maximum(m, jnp.max(s[:, : n - BQ], axis=1, keepdims=True))
            near = jnp.exp(near - m).astype(bf16)
            keep(h, i, slice(n - BQ, n), near)
            a = dot(near, vext[h, n - BQ : n, :])
            if i:
                far = jnp.exp(s[:, : n - BQ] - m).astype(bf16)
                keep(h, i, slice(0, n - BQ), far)
                a = a + dot(far, vext[h, : n - BQ, :])
            parts.append(jnp.exp(first - m).astype(bf16))
            tops.append(m)
            acc = a if acc is None else acc + a
        acc = acc + dot(jnp.concatenate(parts, axis=1), pvext[...])
        inverse = 1.0 / acc[:, 128:]
        o_ref[rows, :] = (acc[:, :128] * inverse).astype(bf16)
        b, high = lanes(BQ) % 64, inverse.astype(bf16).astype(f32)
        flags = jnp.where(b == 8, high, jnp.where(b == 9, inverse - high, flags))
        qx_ref[rows, :] = extra(flags, -jnp.where(lanes(BQ) < 64, tops[0], tops[1]))


def backward_pair(q, k, v, do, dx, dsp, pkd, dq_ref, dk_ref, dv_ref, kext, vext, qt, dot_t, dkt, dvt, kept):
    b = lanes(LEN) % 64
    ones = jnp.where((b >= 1) & (b < 4), 1.0, 0.0).astype(bf16)
    for h in (0, 1):
        kext[h, :, :128] = half(k[...], h)
        vext[h, :, :128] = half(v[...], h)
        vext[h, :, 128:] = half(ones, h)
    qt[...] = q[...].T
    dot_t[...] = do[...].T

    def grad_probs(i, h):
        rows = pl.ds(i * BQ, BQ)
        return dot(jnp.concatenate([do[rows, :], dx[rows, :]], axis=1), vext[h, : (i + 1) * BQ, :], NT)

    steps = [(i, h) for i in reversed(range(NQ)) for h in (0, 1)]
    ahead = grad_probs(*steps[0])
    for (i, h), after in zip(steps, steps[1:] + [None]):
        rows, n = pl.ds(i * BQ, BQ), (i + 1) * BQ
        g = ahead
        if after is not None:
            ahead = grad_probs(*after)
        if h == 0:
            dq = dot(dsp[rows, :], pkd[...])
        hr = slice(h * 64, (h + 1) * 64)
        qth, dth = qt[hr, i * BQ : (i + 1) * BQ], dot_t[hr, i * BQ : (i + 1) * BQ]
        p = kept(h, i, n)
        ds = (p.astype(f32) * g).astype(bf16)
        dq = dq + dot(ds, kext[h, :n, :128])
        if i == NQ - 1:
            dkt[hr, :n] = dot(qth, ds)
            dvt[hr, :n] = dot(dth, p)
        else:
            dkt[hr, :n] += dot(qth, ds)
            dvt[hr, :n] += dot(dth, p)
        if h == 1:
            dq_ref[rows, :] = (dq * 0.125).astype(bf16)
    dk_ref[...] = dkt[...].T.astype(bf16)
    dv_ref[...] = dvt[...].T.astype(bf16)


def block(index, size=256):
    return pl.ds(pl.multiple_of(index * size, size), size)


def loop(body, count=4):
    lax.fori_loop(0, count, lambda r, _: (body(r), 0)[1], 0)


def unrolled(body, count=4):
    for r in range(count):
        body(r)


def center(field):
    mean = jnp.mean(field, axis=-1, keepdims=True)
    centred = field - mean
    return centred, lax.rsqrt(jnp.mean(centred * centred, axis=-1, keepdims=True) + 1e-05)


def norm_back(grad, normed, inv):
    down = grad - jnp.mean(grad, axis=-1, keepdims=True)
    return inv * (down - normed * jnp.mean(grad * normed, axis=-1, keepdims=True))


def key_columns(kx, lengths, buckets):
    full = buckets[0] == LEN
    b = lanes(256) % 64
    for r in range(4):
        place = lax.broadcasted_iota(jnp.int32, (256, 128), 0)
        within = jnp.where(full, place + r * 256, place)
        extent = jnp.where(full, lengths[0, 0], lengths[0, r])
        e = jnp.where((b == 0) & (within >= extent), NEG, 0.0)
        e = jnp.where((b >= 1) & (b < 4), 1.0, e)
        e = jnp.where((b == 4 + r) & jnp.logical_not(full), NEG, e)
        kx[r * 256 : (r + 1) * 256, :] = e.astype(bf16)


def prefix_columns():
    r, b = lax.broadcasted_iota(jnp.int32, (128, 128), 0), lanes(128) % 64
    return jnp.where((b == 0) & (r >= PREFIX), NEG, jnp.where((b >= 1) & (b < 4), 1.0, 0.0)).astype(bf16)


def head_rows(shape, per_head):
    r = lax.broadcasted_iota(jnp.int32, shape, 0) // 16
    return r == lax.broadcasted_iota(jnp.int32, shape, 1) // per_head


def layer_kernel(
    dims, x_hbm, cot_hbm, wq, wo, wf, wp, b_qkv, b_out, b_fc, b_proj, gain, shift, embed, r_in, r_in_b,
    r_out, r_out_b, lengths, buckets,
    ga, gp, stash, out_hbm, gtok_hbm, small,
    shq, sh, shp, bias, xb, nb, ob, qkv, qx, dob, gs, middle, acc, big, WQ, W, kx, pkx, pk, pv, kext, vext, pkext, pvext,
    qt, dot_t, dkt, dvt, dsp, pkd, total, came,
    zs, zr, zps, zpr, as_, ar, bs, br, cs, cr, ls, loc, ts, tr, keeps,
):
    Z, Y, X, C = dims
    dp, fs = lax.axis_index("dp"), lax.axis_index("fsdp")
    z, y, x, c = dp // Y, dp % Y, fs // C, fs % C
    zid = lambda dz: (lax.rem(z + dz, Z) * Y + y, fs)
    yid, xid, cid = (z * Y + (1 - y), fs), (dp, (1 - x) * C + c), (dp, x * C + (1 - c))

    def remote(s, d, ss, rs, dev):
        return pltpu.make_async_remote_copy(
            src_ref=s, dst_ref=d, send_sem=ss, recv_sem=rs, device_id=dev, device_id_type=MESH
        )

    def place(k, *ix):
        if k < OUT:
            return WQ.at[(k, *ix)]
        if k in PROJ:
            return gp.at[(PROJ.index(k), ix[1] * X + ix[2], *ix[3:])]
        return ga.at[(0 if k == OUT else 1 + FC.index(k), *ix)]

    def own(k):
        if k < OUT:
            return shq.at[k], place(k, z, y, x, c)
        if k in PROJ:
            return shp, place(k, z, y, x, c)
        return sh.at[0 if k == OUT else 1 + FC.index(k)], place(k, z, y, x, c)

    def z_copy(k, dz):
        if k in PROJ:
            return remote(*own(k), zps.at[dz - 1], zpr.at[PROJ.index(k)], zid(dz))
        s, d = own(k)
        if k == SIDE:
            s = d = place(k, z, A, A, c)
        return remote(s, d, zs.at[k, dz - 1], zr.at[k, dz - 1], zid(dz))

    def a_copy(k, h):
        first = (h == 0) != (k == SIDE)
        s = place(k, z if k == SIDE else A, y, x, c, h)
        return remote(s, s, as_.at[k, h], ar.at[k, h], yid if first else xid)

    def b_copy(k, h):
        first = (h != 1) != (k == SIDE)
        if k in PROJ:
            plane = gp.at[PROJ.index(k)]
            s = plane.at[pl.ds(y * X, X), c, 1] if h == 1 else plane.at[(h // 2) * X + x, c, 0]
        else:
            ix = (A, x) if first else (y, A)
            s = place(k, z if k == SIDE else A, *ix, c, h)
        return remote(s, s, bs.at[k, h], br.at[k, h], xid if first else yid)

    def halves(k):
        return (0, 1, 2) if k in PROJ else (0, 1)

    def c_copy(k):
        s = gp.at[PROJ.index(k), :, c] if k in PROJ else place(k, A, A, A, c)
        return remote(s, s, cs.at[k], cr.at[k], cid)

    def own_copy(k):
        return pltpu.make_async_copy(*own(k), ls.at[k])

    def stage_z(k):
        def go():
            if k != SIDE:
                own_copy(k).start()
            for dz in (2, 1, 3):
                z_copy(k, dz).start()

        if k == SIDE:
            for h in (0, 1):
                b_copy(k, h).wait_recv()
        if k in PROJ:
            pl.when(z == PROJ.index(k))(go)
        else:
            go()

    def stage_a(k):
        if k in PROJ:
            j = PROJ.index(k)
            pl.when(z == j)(lambda: own_copy(k).wait())
            pl.when(z != j)(lambda: z_copy(k, 1).wait_recv())
        else:
            own_copy(k).wait()
            for dz in (1, 2, 3) if k != SIDE else ():
                z_copy(k, dz).wait_recv()
        for h in (0, 1):
            a_copy(k, h).start()

    def stage_b(k):
        for h in (0, 1):
            a_copy(k, h).wait_recv()
        for h in halves(k):
            b_copy(k, h).start()

    def stage_c(k):
        if k == SIDE:
            for dz in (1, 2, 3):
                z_copy(k, dz).wait_recv()
        else:
            for h in halves(k):
                b_copy(k, h).wait_recv()
        c_copy(k).start()

    def pump(t):
        for k in AHEAD[t] if t < len(AHEAD) else ():
            stage_z(k)
        for k in (t,) if t < 2 else (2, 3) if t == 2 else (t + 1,):
            if k < N:
                stage_a(k)
        if 0 <= t - 1 < N:
            stage_b(t - 1)
        if 0 <= t - 2 < N:
            stage_c(t - 2)
        if 0 <= t - 3 < N:
            c_copy(t - 3).wait_recv()

    def local(s, d, i):
        return pltpu.make_async_copy(s, d, loc.at[i])

    slots = {OUT: 0, FC[0]: 1, FC[1]: 0, FC[2]: 1, FC[3]: 0, PROJ[0]: 2, PROJ[1]: 3, PROJ[2]: 2, PROJ[3]: 3}

    def load(k, slot=None):
        s = gp.at[PROJ.index(k)] if k in PROJ else ga.at[0 if k == OUT else 1 + FC.index(k)]
        return local(s, W.at[slots[k] if slot is None else slot], 20 + k)

    def probs(p, out):
        def piece(h, i):
            n = slice(0, (i + 1) * BQ)
            here = W.at[2 * (p % 2) + h, i, :, :, :, :, :, n]
            there = stash.at[2 * p + h, i, :, :, :, :, :, n]
            sem = keeps.at[p % 2, h, i]
            return pltpu.make_async_copy(here, there, sem) if out else pltpu.make_async_copy(there, here, sem)

        return [piece(h, i) for h in (0, 1) for i in range(NQ)]

    def start_all(copies):
        for d in copies:
            d.start()

    def wait_all(copies):
        for d in copies:
            d.wait()

    shards = [
        local(wq.at[:, :, pl.ds(j * D + g * 256, 256)], shq.at[g, :, :, pl.ds(j * 256, 256)], 33 + 3 * g + j)
        for g in range(4) for j in range(3)
    ]
    shards += [local(wf.at[:, :, pl.ds(3 * D, D)], sh.at[4], 4), local(wo, sh.at[0], 0)]
    shards += [local(wf.at[:, :, pl.ds(j * D, D)], sh.at[1 + j], 1 + j) for j in range(3)]
    shards += [local(wp, shp, 15)]
    for d in shards:
        d.start()
    rin = local(r_in, middle.at[:, pl.ds(0, 512)], 8)
    rout = [local(r_out.at[:, pl.ds(j * D, D)], acc.at[pl.ds(j * 512, 512), :], 9 + j) for j in (0, 1)]
    xload = local(x_hbm, xb, 11)
    xload.start()
    barrier = pltpu.get_barrier_semaphore()
    for d in [zid(dz) for dz in range(1, Z)] + [yid, xid, cid]:
        pl.semaphore_signal(barrier, inc=1, device_id=d, device_id_type=MESH)
    pl.semaphore_wait(barrier, Z + 2)
    for d in shards:
        d.wait()
    own_copy(SIDE).start()
    stage_z(0)
    stage_a(SIDE)
    stage_z(1)
    for d in [rin] + rout:
        d.start()
    xload.wait()

    def norm_one(r):
        rows = block(r)
        centred, inv = center(xb[rows, :].astype(f32))
        nb[rows, :] = (centred * inv * gain[0:1, :] + shift[0:1, :]).astype(bf16)

    loop(norm_one)
    pump(0)
    stage_b(SIDE)
    for j in range(3):
        bias[j : j + 1, :] = b_qkv[pl.ds(j * D, D)].reshape(1, D).astype(f32)
    small[...] = jnp.zeros_like(small)
    small[0:PREFIX, EMB] = embed[...]
    rin.wait()
    hid = jnp.tanh(precise(small[:, EMB], middle[:, 0:512]) + r_in_b[...].reshape(1, 512))
    small[:, HID] = hid
    pump(1)
    live = lax.broadcasted_iota(jnp.int32, (16, D), 0) < PREFIX
    for j, dest in ((0, pk), (1, pv)):
        rout[j].wait()
        t = precise(hid, acc[j * 512 : (j + 1) * 512, :])
        t = jnp.where(live, t + r_out_b[pl.ds(j * D, D)].reshape(1, D), 0.0)
        dest[...] = jnp.zeros_like(dest)
        dest[0:16, :] = t.astype(bf16)
    key_columns(kx, lengths, buckets)
    pkx[...] = prefix_columns()
    pump(2)
    pump(3)

    def project(g):
        cols = block(g)
        for j in range(3):
            t = dot(nb[...], WQ[g, ..., j * 256 : (j + 1) * 256].reshape(D, 256))
            t = (t + bias[j : j + 1, cols]).astype(bf16)
            qkv[j, :, cols] = t * jnp.asarray(0.125, bf16) if j == 0 else t

    def attend(p):
        cols = block(p, 128)
        pl.when(p % 2 == 0)(lambda: project(p // 2))
        pl.when(p >= 2)(lambda: wait_all(probs(p - 2, True)))

        def keep(h, i, cols, value):
            W[2 * (p % 2) + h, i, :, :, :, :, :, cols] = value.reshape(Y, X, C, 2, 16, value.shape[1])

        forward_pair(
            *(qkv.at[k, :, cols] for k in range(3)), pk.at[:, cols], pv.at[:, cols], kx, pkx,
            ob.at[:, cols], qx.at[:, cols], kext, vext, pkext, pvext, keep,
        )
        start_all(probs(p, True))
        for at, t in ((0, 4), (2, 5), (4, 6), (6, 7)):
            pl.when(p == at)(functools.partial(pump, t))

    loop(attend, 8)
    wait_all(probs(6, True))
    load(OUT).start()
    wait_all(probs(7, True))
    load(OUT).wait()
    for cb in range(4):
        cols = slice(cb * 256, (cb + 1) * 256)
        t = dot(ob[...], W[0, ..., cols].reshape(D, 256))
        middle[:, cols] = xb[:, cols].astype(f32) + (t + b_out[pl.ds(cb * 256, 256)].reshape(1, 256).astype(f32))
    cotload = local(cot_hbm, xb, 12)
    cotload.start()
    pump(8)
    load(FC[0]).start()

    def norm_two(r):
        rows = block(r)
        m = middle[rows, :]
        centred, inv = center(m)
        nb[rows, :] = (centred * inv * gain[1:2, :] + shift[1:2, :]).astype(bf16)
        acc[rows, :] = m + b_proj[...].reshape(1, D).astype(f32)
        gs[rows, :] = jnp.zeros_like(m)

    loop(norm_two)
    def hidden_part(f):
        k, r = FC[f], f % 2
        load(k).wait()
        for cb in range(4):
            cols = slice(cb * 256, (cb + 1) * 256)
            u = dot(nb[...], W[slots[k], ..., cols].reshape(D, 256))
            u = u + b_fc[pl.ds(f * D + cb * 256, 256)].reshape(1, 256).astype(f32)
            sq = u * u
            t = jnp.tanh(u * (ROOT + (ROOT * 0.044715) * sq))
            plus = 0.5 + 0.5 * t
            big[r, :, cols] = (u * plus).astype(bf16)
            slope = plus + (0.5 * u) * (1.0 - t * t) * (ROOT + (3 * ROOT * 0.044715) * sq)
            big[2 + r, :, cols] = slope.astype(bf16)

    def out_part(f):
        r = f % 2
        load(PROJ[f]).wait()
        for cb in range(4):
            cols = slice(cb * 256, (cb + 1) * 256)
            acc[:, cols] += dot(big[r], W[2 + r, ..., cols].reshape(D, 256))
            g = dot(xb[...], W[2 + r, cb].reshape(256, D), NT)
            big[2 + r, :, cols] = (g * big[2 + r, :, cols].astype(f32)).astype(bf16)

    def second_part(f):
        for cb in range(4):
            cols = slice(cb * 256, (cb + 1) * 256)
            gs[:, cols] += dot(big[2 + f % 2], W[slots[FC[f]], cb].reshape(256, D), NT)

    hidden_part(0)
    pump(9)
    load(PROJ[0]).start()
    cotload.wait()
    out_part(0)
    pump(10)
    load(FC[1]).start()
    second_part(0)
    hidden_part(1)
    pump(11)
    load(PROJ[1]).start()
    out_part(1)
    pump(12)
    load(FC[2]).start()
    second_part(1)
    stage_c(SIDE)
    hidden_part(2)
    c_copy(SIDE).wait_recv()
    load(FC[3]).start()
    pump(13)
    load(PROJ[2]).start()
    hidden_part(3)
    out_part(2)
    pump(14)
    load(PROJ[3]).start()
    second_part(2)
    load(OUT, 1).start()
    out_part(3)
    second_part(3)

    def norm_two_back(r):
        rows = block(r)
        centred, inv = center(middle[rows, :])
        t = norm_back(gs[rows, :] * gain[1:2, :], centred * inv, inv)
        t = xb[rows, :].astype(f32) + t
        gs[rows, :] = t
        nb[rows, :] = t.astype(bf16)
        W[2, r] = acc[rows, :].astype(bf16).reshape(Y, X, C, 2, 16, D)

    loop(norm_two_back)
    out_save = local(W.at[2], out_hbm, 13)
    out_save.start()
    xload = local(x_hbm, xb, 11)
    xload.start()
    for d in [rin] + rout:
        d.start()
    load(OUT, 1).wait()
    for cb in range(4):
        dob[:, cb * 256 : (cb + 1) * 256] = dot(nb[...], W[1, cb].reshape(256, D), NT).astype(bf16)

    start_all(probs(0, False))
    gi = lax.broadcasted_iota(jnp.int32, (128, 128), 0) // 64
    group = jnp.where(gi == lanes(128) // 64, 1.0, 0.0).astype(bf16)
    row = lax.broadcasted_iota(jnp.int32, (128, 128), 0) % 64
    pick = jnp.where((row == 8) | (row == 9), group, jnp.zeros_like(group))
    group = jnp.concatenate([group, group], axis=0)

    def delta(p):
        cols = block(p, 128)
        inverse = dot(qx[:, cols], pick)
        scaled = (dob[:, cols].astype(f32) * inverse).astype(bf16)
        dob[:, cols] = scaled
        prod = scaled.astype(f32) * ob[:, cols].astype(f32)
        high = prod.astype(bf16)
        low = (prod - high.astype(f32)).astype(bf16)
        sums = -dot(jnp.concatenate([high, low], axis=1), group)
        high = sums.astype(bf16)
        low = (sums - high.astype(f32)).astype(bf16)
        b = lanes(LEN) % 64
        off = pl.multiple_of(768 + (p % 2) * 128, 128)
        big[p // 2, :, pl.ds(off, 128)] = jnp.where(b == 1, high, jnp.where(b == 2, low, jnp.zeros_like(low)))

    loop(delta, 8)
    same = head_rows((256, D), 64)
    spread = [jnp.concatenate([t[0:16, :]] * 16, axis=0) for t in (pk, pv)]
    spread = [jnp.where(same, t, jnp.zeros_like(t)) for t in spread]
    pkd[...] = spread[0]
    lane = lax.broadcasted_iota(jnp.int32, (256, D), 1) % 64
    unit = jnp.where(same & (lane >= 1) & (lane < 4), 1.0, 0.0)
    dead = lax.broadcasted_iota(jnp.int32, (256, D), 0) % 16 >= PREFIX
    mask = jnp.where(same & (lane == 0) & dead, NEG, unit).astype(bf16)
    unit = unit.astype(bf16)
    prob = jnp.exp(dot(qkv[0], spread[0], NT) + dot(qx[...], mask, NT))
    deltas = jnp.concatenate([big[g, :, 768:] for g in range(4)], axis=1)
    grad = dot(dob[...], spread[1], NT) + dot(deltas, unit, NT)
    dsp[...] = (prob * grad).astype(bf16)
    for j, (left, right) in enumerate(((dsp[...], qkv[0]), (prob.astype(bf16), dob[...]))):
        t = jnp.where(same, dot(left.T, right), 0.0)
        total[0, :, j * D : (j + 1) * D] = jnp.sum(t.reshape(16, 16, D), axis=0)

    partners = [cid, xid, yid, ((z + 1 - 2 * (z % 2)) * Y + y, fs), zid(2)]

    def exchange(s):
        return remote(total.at[s], came.at[s], ts.at[s], tr.at[s], partners[s])

    def step(s):
        if s > 0:
            exchange(s - 1).wait_recv()
            total[s] = total[s - 1] + came[s - 1]
        if s < 5:
            exchange(s).start()

    out_save.wait()
    start_all(probs(1, False))

    def attend_back(p):
        for s in range(6):
            pl.when(p == s)(functools.partial(step, s))
        cols = block(p, 128)
        part = lambda j: big.at[p // 2, :, pl.ds(pl.multiple_of(j * 256 + (p % 2) * 128, 128), 128)]
        wait_all(probs(p, False))
        kept = lambda h, i, n: W[2 * (p % 2) + h, i, :, :, :, :, :, :n].reshape(BQ, n)
        backward_pair(
            *(qkv.at[k, :, cols] for k in range(3)), dob.at[:, cols], part(3), dsp, pkd.at[:, cols],
            part(0), part(1), part(2), kext, vext, qt, dot_t, dkt, dvt, kept,
        )
        pl.when(p < 6)(lambda: start_all(probs(p + 2, False)))

    loop(attend_back, 8)
    for d in rout:
        d.wait()
    rin.wait()
    small[:, GPRE] = total[5]
    hid = small[:, HID]
    t = sum(close(total[5, :, j * D : (j + 1) * D], acc[j * 512 : (j + 1) * 512, :]) for j in (0, 1))
    t = t * (1.0 - hid * hid)
    small[:, PRE] = t
    small[:, GEMB] = close(t, middle[:, 0:512])
    for cb in range(4):
        cols = slice(cb * 256, (cb + 1) * 256)
        acc[:, cols] = sum(dot(big[g, :, :768], WQ[g, cb].reshape(256, 768), NT) for g in range(4))
    xload.wait()

    def norm_one_back(r):
        rows = block(r)
        centred, inv = center(xb[rows, :].astype(f32))
        t = norm_back(acc[rows, :] * gain[0:1, :], centred * inv, inv)
        nb[rows, :] = (gs[rows, :] + t).astype(bf16)
        save(r).start()

    def save(r):
        return local(nb.at[block(r), :], gtok_hbm.at[block(r), :], 45 + r)

    loop(norm_one_back)
    for k in range(N + 1):
        if k not in PROJ:
            for dz in (1, 2, 3):
                z_copy(k, dz).wait_send()
        for h in (0, 1):
            a_copy(k, h).wait_send()
        for h in halves(k):
            b_copy(k, h).wait_send()
        c_copy(k).wait_send()
    for dz in (1, 2, 3):
        z_copy(PROJ[0], dz).wait_send()
    for s in range(5):
        exchange(s).wait_send()
    for r in range(4):
        save(r).wait()


def layer(
    dims, x, cot, wq, wo, wf, wp, b_qkv, b_out, b_fc, b_proj, gain, shift, embed, r_in, r_in_b, r_out,
    r_out_b, lengths, buckets,
):
    Z, Y, X, C = dims
    S, V, sds = pltpu.SemaphoreType.DMA, pltpu.VMEM, jax.ShapeDtypeStruct
    anys, vm, sm = (pl.BlockSpec(memory_space=s) for s in (pl.ANY, pltpu.VMEM, pltpu.SMEM))
    wide, wide32 = V((LEN, D), bf16), V((LEN, D), f32)
    return pl.pallas_call(
        functools.partial(layer_kernel, dims),
        out_shape=[
            sds((5, Z, Y, X, C, 2, 16, D), bf16), sds((4, Z, Y, X, C, 2, 16, D), bf16),
            sds((16, Z, Y, X, C, 2, 16, LEN), bf16), sds((Z, Y, X, C, 2, 16, D), bf16), sds((LEN, D), bf16),
            sds((16, 5 * D), f32),
        ],
        in_specs=[anys] * 6 + [vm] * 7 + [anys, vm, anys, vm, sm, sm],
        out_specs=[anys] * 5 + [vm],
        scratch_shapes=[
            V((4, 2, 16, 768), bf16), V((5, 2, 16, D), bf16), V((2, 2, 2, 16, D), bf16), V((8, D), f32), wide, wide, wide, V((3, LEN, D), bf16), wide, wide,
            wide32, wide32, wide32, V((4, LEN, D), bf16),
            V((4, Z, Y, X, C, 2, 16, 768), bf16), V((4, Z, Y, X, C, 2, 16, D), bf16),
            V((LEN, 128), bf16), V((128, 128), bf16), V((128, D), bf16), V((128, D), bf16),
            V((2, LEN, 256), bf16), V((2, LEN, 256), bf16), V((256, 256), bf16), V((256, 256), bf16),
            V((128, LEN), bf16), V((128, LEN), bf16), V((128, LEN), f32), V((128, LEN), f32),
            V((LEN, 256), bf16), V((256, D), bf16), V((6, 16, 2 * D), f32), V((5, 16, 2 * D), f32),
            S((N + 1, 3)), S((N + 1, 3)), S((3,)), S((4,)), *[S((N + 1, 2))] * 2, *[S((N + 1, 3))] * 2, *[S((N + 1,))] * 3, S((49,)),
            S((5,)), S((5,)), S((2, 2, NQ)),
        ],
        compiler_params=pltpu.CompilerParams(
            collective_id=0, has_side_effects=True, vmem_limit_bytes=62 << 20
        ),
    )(
        x, cot, *(w.reshape(2, 16, w.shape[1]) for w in (wq, wo, wf)), wp.reshape(2, 2, 2, 16, D),
        b_qkv, b_out, b_fc, b_proj, gain, shift, embed, r_in, r_in_b, r_out, r_out_b, lengths, buckets,
    )


def outer(left, right):
    a, b, c = (t.astype(bf16) for t in split_three(left))
    p, q, r = (t.astype(bf16) for t in split_three(right))
    left = jnp.concatenate([a, a, b, a, c, b], axis=0)
    right = jnp.concatenate([p, q, p, r, p, q], axis=0)
    return dot(left.T, right)


def finish_kernel(out_in, gtok_in, small, out, gtok, g_embed, g_in, g_in_b, g_out, g_out_b):
    g_out[...] = outer(small[:, HID], small[:, GPRE])
    g_in[...] = outer(small[:, EMB], small[:, PRE])
    out[...] = out_in[...]
    gtok[...] = gtok_in[...]
    g_out_b[...] = jnp.sum(small[:, GPRE], axis=0)
    g_in_b[...] = jnp.sum(small[:, PRE], axis=0)
    g_embed[...] = small[0:PREFIX, GEMB]


def finish(out, gtok, small):
    vm, sds = pl.BlockSpec(memory_space=pltpu.VMEM), jax.ShapeDtypeStruct
    return pl.pallas_call(
        finish_kernel,
        out_shape=[
            sds(out.shape, bf16), sds(gtok.shape, bf16), sds((PREFIX, D), f32), sds((D, 512), f32),
            sds((512,), f32), sds((512, 2 * D), f32), sds((2 * D,), f32),
        ],
        in_specs=[vm] * 3,
        out_specs=[vm] * 7,
        compiler_params=pltpu.CompilerParams(vmem_limit_bytes=62 << 20),
    )(out, gtok, small)


def normalize(field, gain, shift):
    centred, inv = center(field)
    return centred * inv * gain + shift


def plain_heads(matrix):
    return matrix.reshape(matrix.shape[0], 16, 64).transpose(1, 0, 2)


def plain_visible(seg_lengths, bucket):
    places = jnp.arange(LEN, dtype=jnp.int32)
    segment = places // bucket
    within = places - segment * bucket
    extent = sum(jnp.where(segment == which, seg_lengths[which], 0) for which in range(4))
    same = segment[:, None] == segment[None, :]
    return same & (places[None, :] <= places[:, None]) & (within < extent)[None, :]


def plain_attend(q, k, v, allowed):
    mix = lambda spec, a, b: jnp.einsum(spec, a.astype(bf16), b.astype(bf16), preferred_element_type=f32)
    scores = jnp.where(allowed, mix("qd,kd->qk", q, k) * 0.125, NEG)
    return mix("qk,kd->qd", jax.nn.softmax(scores, axis=-1), v)


def plain_layer(
    tokens, cotangent, w_qkv, w_out, w_fc, w_proj, bias_qkv, bias_out, bias_fc, bias_proj,
    ln_gain, ln_shift, prefix_embed, reparam_in, reparam_in_bias, reparam_out, reparam_out_bias,
    lengths, buckets,
):
    full_qkv, full_out, full_fc, full_proj = (
        lax.all_gather(t, ("dp", "fsdp"), axis=0, tiled=True) for t in (w_qkv, w_out, w_fc, w_proj)
    )
    hidden = jnp.tanh(precise(prefix_embed, reparam_in) + reparam_in_bias)
    prefix_rows = (precise(hidden, reparam_out) + reparam_out_bias).astype(bf16)
    pk, pv = plain_heads(prefix_rows[:, :D]), plain_heads(prefix_rows[:, D:])
    inputs = tokens.astype(f32)
    norm_one = lambda field: normalize(field, ln_gain[0], ln_shift[0])
    norm_two = lambda field: normalize(field, ln_gain[1], ln_shift[1])
    normed, pull_one = jax.vjp(norm_one, inputs)
    joined = (dot(normed.astype(bf16), full_qkv) + bias_qkv.astype(f32)).astype(bf16)
    q, k, v = (plain_heads(joined[:, i * D : (i + 1) * D]) for i in range(3))
    allowed = jnp.concatenate([jnp.ones((LEN, PREFIX), bool), plain_visible(lengths[0], buckets[0])], 1)

    def one_head(parts):
        q, k, v, pk, pv, grad = parts
        run = lambda q, k, v: plain_attend(q, k, v, allowed)
        mixed, pull = jax.vjp(run, q.astype(f32), *(jnp.concatenate(t).astype(f32) for t in ((pk, k), (pv, v))))
        return mixed, pull(grad.astype(f32))

    heads = (q, k, v, pk, pv)
    mixed = lax.map(lambda parts: one_head((*parts, parts[0]))[0], heads)
    back = lambda t: t.transpose(1, 0, 2).reshape(-1, D)
    attended = back(mixed).astype(bf16)
    middle = inputs + (dot(attended, full_out) + bias_out.astype(f32))
    second, pull_two = jax.vjp(norm_two, middle)
    before = dot(second.astype(bf16), full_fc) + bias_fc.astype(f32)
    activated, pull_gelu = jax.vjp(lambda field: jax.nn.gelu(field, approximate=True), before)
    result = middle + (dot(activated.astype(bf16), full_proj) + bias_proj.astype(f32))
    grad_before = pull_gelu(dot(cotangent, full_proj, NT))[0].astype(bf16)
    grad_middle = cotangent.astype(f32) + pull_two(dot(grad_before, full_fc, NT))[0]
    grad_attended = dot(grad_middle.astype(bf16), full_out, NT).astype(bf16)
    dq, dk, dv = lax.map(lambda parts: one_head(parts)[1], (*heads, plain_heads(grad_attended)))
    grads = [back(t).astype(bf16) for t in (dq, dk[:, PREFIX:], dv[:, PREFIX:])]
    grad_prefix = jnp.concatenate([back(t[:, :PREFIX]) for t in (dk, dv)], 1)
    grad_prefix = lax.psum(grad_prefix, ("dp", "fsdp"))
    grad_normed = dot(jnp.concatenate(grads, 1), full_qkv, NT)
    grad_tokens = (grad_middle + pull_one(grad_normed)[0]).astype(bf16)
    grad_pre = precise(grad_prefix, reparam_out, NT) * (1.0 - hidden * hidden)
    return (
        result.astype(bf16), grad_tokens, precise(grad_pre, reparam_in, NT), precise(prefix_embed.T, grad_pre),
        jnp.sum(grad_pre, axis=0), precise(hidden.T, grad_prefix), jnp.sum(grad_prefix, axis=0),
    )


def on_device(dims, *args):
    if dims is None:
        return plain_layer(*args)
    _, _, _, out, gtok, small = layer(dims, *args)
    return tuple(finish(out.reshape(gtok.shape), gtok, small))


def chip_dims(mesh):
    if dict(mesh.shape) == {"dp": 8, "fsdp": 4}:
        return (4, 2, 2, 2)
    return None


def solution(mesh):
    split, lone = P(("dp", "fsdp"), None), P()
    return jax.shard_map(
        functools.partial(on_device, chip_dims(mesh)),
        mesh=mesh,
        in_specs=(split,) * 6 + (lone,) * 11 + (split, P(("dp", "fsdp"))),
        out_specs=(split, split) + (lone,) * 5,
        check_vma=False,
    )
```
